32 devices in a mesh: dp: 8 (over z, x), mp: 4 (over y, core).
Axes of the slice: x: 2, y: 2, z: 4, core: 2. Of those that a mesh axis runs over, the one named last changes fastest.
Arguments:
- tokens: bfloat16 [13824, 768], P('dp', 'mp'), may hold values from -6 to 6
- w_qkv: bfloat16 [768, 3, 768], P(None, None, 'mp'), may hold values from -0.21875 to 0.21875
- b_qkv: bfloat16 [3, 768], P(None, 'mp'), may hold values from -3 to 3
- freqs: float32 [2, 12, 32], P(None, 'mp'), may hold values from -0.8 to 0.8
- w_out: bfloat16 [768, 768], P('mp'), may hold values from -0.875 to 0.875
- b_out: bfloat16 [768], P('mp'), may hold values from -2 to 2
- norm1_gain: bfloat16 [768], P('mp'), may hold values from 0.5 to 1.5
- norm1_bias: bfloat16 [768], P('mp'), may hold values from -2 to 2
- norm2_gain: bfloat16 [768], P('mp'), may hold values from 0.5 to 1.5
- norm2_bias: bfloat16 [768], P('mp'), may hold values from -2 to 2
- w_up: bfloat16 [768, 3072], P(None, 'mp'), may hold values from -0.21875 to 0.21875
- b_up: bfloat16 [3072], P('mp'), may hold values from -3 to 3
- w_down: bfloat16 [3072, 768], P('mp'), may hold values from -0.109375 to 0.109375
- b_down: bfloat16 [768], P('mp'), may hold values from -2 to 2
- cotangent: bfloat16 [13824, 768], P('dp', 'mp'), may hold values from -6 to 6
- keep_mask: int32 [13824], P('dp'), may hold values from 0 to 1, as said below
- coords: int32 [2, 13824], P(None, 'dp'), may hold values from 0 to 23, as said below
- block_group: int32 [8], P('dp'), may hold values from 0 to 1, as said below
Outputs:
- block_out: bfloat16 [13824, 768], P('dp', 'mp')
- input_grad: float32 [13824, 768], P('dp', 'mp')
- grad_w_qkv: float32 [768, 3, 768], P(None, None, 'mp')
- grad_b_qkv: float32 [3, 768], P(None, 'mp')
- grad_freqs: float32 [2, 12, 32], P(None, 'mp')
- grad_w_out: float32 [768, 768], P('mp')
- grad_b_out: float32 [768], P('mp')
- grad_norm1_gain: float32 [768], P('mp')
- grad_norm1_bias: float32 [768], P('mp')
- grad_norm2_gain: float32 [768], P('mp')
- grad_norm2_bias: float32 [768], P('mp')
- grad_w_up: float32 [768, 3072], P(None, 'mp')
- grad_b_up: float32 [3072], P('mp')
- grad_w_down: float32 [3072, 768], P('mp')
- grad_b_down: float32 [768], P('mp')
The draws below stay inside these ranges and needn't reach their ends.
Inputs may be any that keep to these rules, and one draw needn't show every extreme that they name: `keep_mask`: A block of group 0 holds 8 images of 196 slots one after another and then padding; a block of group 1 holds 3 images of 576 slots. Within each image the kept slots are its first ones, a quarter or more of its patches; padding is never kept; the first image of the first block of each group keeps all. `coords`: A kept slot holds the row and column of a patch of its image's grid (14 or 24 patches a side), each patch at most once per image; slots not kept hold 0. `block_group`: the group never falls from one block to the next, and both groups occur.
All inputs are finite; a program needn't handle non-finite values.
Results may differ from the reference program's by a relative error of at most 0.015.
The reference program's roundings to bfloat16 on the way count: a program that leaves them out, or rounds other values in their place, can miss the bound.
Values may be sent and summed in bfloat16 or wider, within the bound.
A program may use at most 128 MiB of HBM per device.

```python
import jax
import jax.numpy as jnp
from jax import lax

D = 768
HEADS = 12
HEAD_DIM = 64
FF = 3072
GRID_LO = 14
GRID_HI = 24
SLOTS = 576
ROWS_DEV = 1728
LOW_IMGS = 8
PAIRS = 32
BLOCKS = 8
TOKENS = 13824


def draw_layout(key):
    split_key, drop_key, order_key = jax.random.split(key, 3)
    boundary = jax.random.randint(split_key, (), 1, BLOCKS)
    block_index = jnp.arange(BLOCKS, dtype=jnp.int32)
    groups = (block_index >= boundary).astype(jnp.int32)
    grid_side = jnp.where(groups == 0, GRID_LO, GRID_HI).astype(jnp.int32)
    patches = grid_side * grid_side
    images_here = ROWS_DEV // patches
    image_slot = jnp.arange(LOW_IMGS, dtype=jnp.int32)
    drop_cap = jnp.broadcast_to((3 * patches // 4 + 1)[:, None], (BLOCKS, LOW_IMGS))
    drop_keys = jax.random.split(drop_key, 3)
    drop_first = jax.random.randint(drop_keys[0], (BLOCKS, LOW_IMGS), 0, drop_cap)
    drop_second = jax.random.randint(drop_keys[1], (BLOCKS, LOW_IMGS), 0, drop_cap)
    drop_third = jax.random.randint(drop_keys[2], (BLOCKS, LOW_IMGS), 0, drop_cap)
    dropped = jnp.minimum(jnp.minimum(drop_first, drop_second), drop_third)
    first_image = ((block_index == 0) | (block_index == boundary))[:, None] & (image_slot[None, :] == 0)
    kept_count = jnp.where(first_image, patches[:, None], patches[:, None] - dropped)
    row_index = jnp.arange(ROWS_DEV, dtype=jnp.int32)
    segment = row_index[None, :] // patches[:, None]
    position = row_index[None, :] % patches[:, None]
    segment_clip = jnp.minimum(segment, LOW_IMGS - 1)
    kept_row = jnp.take_along_axis(kept_count, segment_clip, axis=1)
    live = (segment < images_here[:, None]) & (position < kept_row)
    keep_table = live.astype(jnp.int32)
    slot_index = jnp.arange(SLOTS, dtype=jnp.int32)
    random_part = jax.random.randint(order_key, (BLOCKS, LOW_IMGS, SLOTS), 0, 1 << 20)
    sort_keys = jnp.where(slot_index[None, None, :] < patches[:, None, None], random_part * SLOTS + slot_index[None, None, :], (1 << 20) * SLOTS + slot_index[None, None, :])
    ordering = jnp.argsort(sort_keys, axis=2, stable=True).astype(jnp.int32).reshape(BLOCKS, LOW_IMGS * SLOTS)
    patch = jnp.take_along_axis(ordering, segment_clip * SLOTS + position, axis=1)
    grid_row = jnp.where(live, patch // grid_side[:, None], 0)
    grid_col = jnp.where(live, patch % grid_side[:, None], 0)
    coord_table = jnp.stack([grid_row.reshape(-1), grid_col.reshape(-1)]).astype(jnp.int32)
    return (keep_table.reshape(-1), coord_table, groups)


def draw_keep_mask(key, part):
    layout = draw_layout(key)
    return layout[0]


def draw_coords(key, part):
    layout = draw_layout(key)
    return layout[1]


def draw_block_group(key, part):
    layout = draw_layout(key)
    return layout[2]


def block_scale(rng, extent, shards, least, largest):
    def one(dim, blocks):
        steps = jax.random.uniform(jax.random.fold_in(jax.random.fold_in(rng, 6), dim), (blocks,), jnp.float32, least / len(shards), largest / len(shards))
        return jnp.repeat(jnp.exp(steps), extent[dim] // blocks).reshape((-1,) + (1,) * (len(extent) - dim - 1))

    loudness = one(*shards[0])
    for cut in shards[1:]:
        loudness = loudness * one(*cut)
    return loudness


def noise(rng, extent, spread, bound, cuts=(), kind=jnp.bfloat16):
    factor_of = block_scale(rng, extent, cuts, -0.22, 0.18) if cuts else 1.0
    array = jax.random.normal(rng, extent, jnp.float32) * spread * factor_of
    return jnp.minimum(jnp.maximum(array, -bound), bound).astype(kind)


def setup_inputs(seed: int = 0) -> dict:
    keys = jax.random.split(jax.random.key(seed), 19)
    tokens = noise(keys[0], (TOKENS, D), 1.0, 6.0, ((0, 8), (1, 4)))
    w_qkv = noise(keys[1], (D, 3, D), D ** -0.5, 0.21875, ((2, 4),))
    b_qkv = noise(keys[2], (3, D), 0.5, 3.0, ((1, 4),))
    freqs = jnp.clip(jax.random.uniform(keys[3], (2, HEADS, PAIRS), jnp.float32, -0.8, 0.8) * block_scale(keys[3], (2, HEADS, PAIRS), ((1, 4),), -0.4, 0.0), -0.8, 0.8)
    w_out = noise(keys[4], (D, D), (D // 16) ** -0.5, 0.875, ((0, 4),))
    b_out = noise(keys[5], (D,), 0.3, 2.0, ((0, 4),))
    norm1_gain = jnp.clip(1.0 + 0.1 * jax.random.normal(keys[6], (D,), jnp.float32), 0.5, 1.5).astype(jnp.bfloat16)
    norm1_bias = noise(keys[7], (D,), 0.3, 2.0, ((0, 4),))
    norm2_gain = jnp.clip(1.0 + 0.1 * jax.random.normal(keys[8], (D,), jnp.float32), 0.5, 1.5).astype(jnp.bfloat16)
    norm2_bias = noise(keys[9], (D,), 0.3, 2.0, ((0, 4),))
    w_up = noise(keys[10], (D, FF), D ** -0.5, 0.21875, ((1, 4),))
    b_up = noise(keys[11], (FF,), 0.5, 3.0, ((0, 4),))
    w_down = noise(keys[12], (FF, D), FF ** -0.5, 0.109375, ((0, 4),))
    b_down = noise(keys[13], (D,), 0.3, 2.0, ((0, 4),))
    cotangent = noise(keys[14], (TOKENS, D), 1.0, 6.0, ((0, 8), (1, 4)))
    keep_mask = draw_keep_mask(jax.random.fold_in(keys[18], 71), 0)
    coords = draw_coords(jax.random.fold_in(keys[18], 71), 0)
    block_group = draw_block_group(jax.random.fold_in(keys[18], 71), 0)
    return {"tokens": tokens, "w_qkv": w_qkv, "b_qkv": b_qkv, "freqs": freqs, "w_out": w_out, "b_out": b_out, "norm1_gain": norm1_gain, "norm1_bias": norm1_bias, "norm2_gain": norm2_gain, "norm2_bias": norm2_bias, "w_up": w_up, "b_up": b_up, "w_down": w_down, "b_down": b_down, "cotangent": cotangent, "keep_mask": keep_mask, "coords": coords, "block_group": block_group}


highest = lax.Precision.HIGHEST
norm_eps = 1e-06

@jax.custom_vjp
def low(v):
    return lax.optimization_barrier(v.astype(jnp.bfloat16)).astype(jnp.float32)

@jax.custom_vjp
def low_back(v):
    return v

def low_keep(v):
    return (low(v), None)

def low_pass(kept, grad):
    return (grad,)

def back_keep(v):
    return (v, None)

def back_low(kept, grad):
    return (low(grad),)
low.defvjp(low_keep, low_pass)
low_back.defvjp(back_keep, back_low)

def matmul(left_side, right_side):
    return jnp.dot(left_side, right_side, precision=highest, preferred_element_type=jnp.float32)

def layer_norm(values, gain, shift_bias):
    row_mean = lax.optimization_barrier(jnp.mean(values, axis=-1, keepdims=True))
    row_square = lax.optimization_barrier(jnp.mean(values * values, axis=-1, keepdims=True))
    inverse = lax.rsqrt(row_square - row_mean * row_mean + norm_eps)
    return (values - row_mean) * inverse * gain + shift_bias

def rotate_pairs(vectors, cosine_table, sine_table):
    split_at = vectors.shape[-1] // 2
    front_part = vectors[..., :split_at]
    back_part = vectors[..., split_at:]
    return jnp.concatenate([front_part * cosine_table - back_part * sine_table, front_part * sine_table + back_part * cosine_table], axis=-1)

def attend_rows(queries, keys_rot, values, segment_ids, key_keep):
    row_count = queries.shape[0]
    block_count = row_count // SLOTS

    def one_block(inputs):
        query_blk, segment_blk = inputs
        scores = low_back(HEAD_DIM ** (-0.5) * jnp.einsum('qhd,khd->hqk', query_blk, keys_rot, precision=highest, preferred_element_type=jnp.float32))
        allowed = (segment_blk[:, None] == segment_ids[None, :]) & key_keep[None, :]
        scores = jnp.where(allowed[None], scores, -1e+30)
        row_max = lax.optimization_barrier(jnp.max(scores, axis=-1, keepdims=True))
        exponent = jnp.exp(scores - row_max)
        attn_probs = low(exponent / lax.optimization_barrier(jnp.sum(exponent, axis=-1, keepdims=True)))
        return jnp.einsum('hqk,khd->qhd', attn_probs, values, precision=highest, preferred_element_type=jnp.float32)
    attended = lax.map(jax.checkpoint(one_block), (queries.reshape(block_count, SLOTS, HEADS, HEAD_DIM), segment_ids.reshape(block_count, SLOTS)))
    return attended.reshape(row_count, D)

def block_forward(stream, params, keep_rows, coord_rows, segment_ids):
    w_qkv, b_qkv, freqs, w_out, b_out, gain_one, bias_one, gain_two, bias_two, w_up, b_up, w_down, b_down = params
    row_count = stream.shape[0]
    normed_one = low(layer_norm(stream, gain_one, bias_one))
    projected = low_back(jnp.einsum('rd,dce->rce', normed_one, w_qkv, precision=highest, preferred_element_type=jnp.float32) + b_qkv)
    angles = coord_rows[0][:, None, None] * freqs[0][None] + coord_rows[1][:, None, None] * freqs[1][None]
    cosine_table = jnp.cos(angles)
    sine_table = jnp.sin(angles)
    queries = low_back(low(rotate_pairs(projected[:, 0].reshape(row_count, HEADS, HEAD_DIM), cosine_table, sine_table)))
    keys_rot = low_back(low(rotate_pairs(projected[:, 1].reshape(row_count, HEADS, HEAD_DIM), cosine_table, sine_table)))
    values = low_back(low(projected[:, 2].reshape(row_count, HEADS, HEAD_DIM)))
    key_keep = keep_rows > 0.5
    attended = low_back(low(attend_rows(queries, keys_rot, values, segment_ids, key_keep)))
    mid = stream + low_back(matmul(attended, w_out) + b_out)
    normed_two = low(layer_norm(mid, gain_two, bias_two))
    hidden_pre = low_back(matmul(normed_two, w_up) + b_up)
    activated = low(jax.nn.gelu(hidden_pre, approximate=False))
    return keep_rows[:, None] * (mid + (matmul(activated, w_down) + b_down))

def reference(tokens, w_qkv, b_qkv, freqs, w_out, b_out, norm1_gain, norm1_bias, norm2_gain, norm2_bias, w_up, b_up, w_down, b_down, cotangent, keep_mask, coords, block_group):
    params = tuple((weight_arg.astype(jnp.float32) for weight_arg in (w_qkv, b_qkv, freqs, w_out, b_out, norm1_gain, norm1_bias, norm2_gain, norm2_bias, w_up, b_up, w_down, b_down)))
    keep_float = keep_mask.astype(jnp.float32)
    keep_all = keep_float.reshape(BLOCKS, ROWS_DEV)
    block_kept = lax.optimization_barrier(jnp.sum(keep_all, axis=1))
    count_low = jnp.sum(block_kept * (block_group == 0))
    count_high = jnp.sum(block_kept * (block_group == 1))
    stream_all = tokens.astype(jnp.float32).reshape(BLOCKS, ROWS_DEV, D)
    cot_all = cotangent.astype(jnp.float32).reshape(BLOCKS, ROWS_DEV, D)
    coord_all = coords.astype(jnp.float32).reshape(2, BLOCKS, ROWS_DEV).transpose(1, 0, 2)
    row_index = jnp.arange(ROWS_DEV, dtype=jnp.int32)

    def per_device(running, inputs):
        stream, cot_rows, keep_rows, coord_rows, group_now = inputs
        segment_size = jnp.where(group_now == 0, GRID_LO * GRID_LO, SLOTS).astype(jnp.int32)
        segment_ids = (row_index // segment_size).astype(jnp.int32)

        def inner(stream_in, param_in):
            return block_forward(stream_in, param_in, keep_rows, coord_rows, segment_ids)
        outputs, pullback = jax.vjp(inner, stream, params)
        grad_stream, grad_params = pullback(cot_rows)
        factor = jnp.where(group_now == 0, count_low, count_high) / (count_low + count_high)
        running = jax.tree.map(lambda summed, addend: summed + factor * addend, running, grad_params)
        return (running, (outputs.astype(jnp.bfloat16), grad_stream))
    start_sums = jax.tree.map(jnp.zeros_like, params)
    grads, (out_blocks, grad_blocks) = lax.scan(per_device, start_sums, (stream_all, cot_all, keep_all, coord_all, block_group))
    block_out = out_blocks.reshape(TOKENS, D)
    input_grad = grad_blocks.reshape(TOKENS, D)
    return (block_out, input_grad, grads[0], grads[1], grads[2], grads[3], grads[4], grads[5], grads[6], grads[7], grads[8], grads[9], grads[10], grads[11], grads[12])
```

```python
import functools

import jax
import jax.numpy as jnp
from jax import lax
from jax.experimental import pallas as pl
from jax.experimental.pallas import tpu as pltpu
from jax.sharding import PartitionSpec as P

HEAD_DIM = 64
GRID_LO = 14
SLOTS = 576

MESH = pl.DeviceIdType.MESH
MIB = 1024 * 1024
F32 = jnp.float32
BF16 = jnp.bfloat16
NT = (((1,), (1,)), ((), ()))
TN = (((0,), (0,)), ((), ()))
NN = (((1,), (0,)), ((), ()))

ROWS = 1728
TILE = 192
TILES = ROWS // TILE
NARROW = 608
WIDE = 768
GATHER_ROWS = 288
GATHERS = ROWS // GATHER_ROWS


class Refs:
    pass


def dot(left, right, dims=NN):
    return lax.dot_general(left, right, dims, preferred_element_type=F32)


def remote(src, dst, send, recv, device):
    return pltpu.make_async_remote_copy(
        src_ref=src, dst_ref=dst, send_sem=send, recv_sem=recv, device_id=device, device_id_type=MESH
    )


def place():
    spot = Refs()
    spot.dp = lax.axis_index("dp")
    spot.mp = lax.axis_index("mp")
    spot.y = spot.mp // 2
    spot.c = spot.mp % 2
    spot.sib_mp = 2 * spot.y + 1 - spot.c
    spot.yp_mp = 2 * (1 - spot.y) + spot.c
    spot.diag_mp = 2 * (1 - spot.y) + 1 - spot.c
    spot.sib = (spot.dp, spot.sib_mp)
    spot.yp = (spot.dp, spot.yp_mp)
    return spot


def greet(devices):
    barrier = pltpu.get_barrier_semaphore()
    for device in devices:
        pl.semaphore_signal(barrier, inc=1, device_id=device, device_id_type=MESH)
    pl.semaphore_wait(barrier, len(devices))


def sin_cos(angle):
    turns = jnp.floor(angle * 0.6366197723675814 + 0.5)
    rest = angle - turns * 1.5703125
    rest = rest - turns * 4.837512969970703e-4
    rest = rest - turns * 7.549789948768648e-8
    square = rest * rest
    sine = rest + rest * square * (
        -1.6666654611e-1 + square * (8.3321608736e-3 + square * -1.9515295891e-4)
    )
    cosine = (
        1.0
        - 0.5 * square
        + square
        * square
        * (4.166664568298827e-2 + square * (-1.388731625493765e-3 + square * 2.443315711809948e-5))
    )
    quarter = turns - 4.0 * jnp.floor(turns * 0.25)
    odd = (quarter == 1.0) | (quarter == 3.0)
    sine_sign = jnp.where(quarter >= 2.0, -1.0, 1.0)
    cosine_sign = jnp.where((quarter == 1.0) | (quarter == 2.0), -1.0, 1.0)
    return (
        jnp.where(odd, cosine, sine) * sine_sign,
        jnp.where(odd, sine, cosine) * cosine_sign,
    )


def front_lanes(shape):
    return lax.broadcasted_iota(jnp.int32, shape, 1) % HEAD_DIM < HEAD_DIM // 2


def swap_halves(values):
    width = values.shape[1]
    half = HEAD_DIM // 2
    return jnp.where(
        front_lanes(values.shape),
        pltpu.roll(values, width - half, 1),
        pltpu.roll(values, half, 1),
    )


def start_gather(r, spot):
    own = pltpu.make_async_copy(r.tok, r.tokp.at[spot.mp], r.own_sem)
    own.start()
    for i in range(GATHERS):
        rows = pl.ds(i * GATHER_ROWS, GATHER_ROWS)
        remote(
            r.tok.at[rows], r.tokp.at[spot.mp, rows], r.ty_send.at[i], r.ty_recv.at[i], spot.yp
        ).start()
    remote(r.tok, r.tokp.at[spot.mp], r.tc_send, r.tc_recv, spot.sib).start()
    remote(r.small, r.smallp.at[spot.mp], r.sm_send.at[0], r.sm_recv.at[0], spot.yp).start()
    remote(r.small, r.smallp.at[spot.mp], r.sm_send.at[1], r.sm_recv.at[1], spot.sib).start()


def angle_tables(r):
    step = 144

    def block(i, carry):
        rows = pl.ds(pl.multiple_of(i * step, 16), step)
        angle = r.info[rows, 0:1] * r.freq[0:1, :] + r.info[rows, 1:2] * r.freq[1:2, :]
        sine, cosine = sin_cos(angle)
        r.cos[rows, :] = cosine
        r.sin[rows, :] = jnp.where(front_lanes(sine.shape), -sine, sine)
        return carry

    lax.fori_loop(0, ROWS // step, block, 0)


def project(r, i):
    rows = pl.ds(pl.multiple_of(i * GATHER_ROWS, 16), GATHER_ROWS)
    values = jnp.concatenate([r.tokp[j, rows, :].astype(F32) for j in range(4)], axis=1)
    r.tokf[rows, :] = values.astype(BF16)
    mean = jnp.mean(values, axis=1, keepdims=True)
    square = jnp.mean(values * values, axis=1, keepdims=True)
    inverse = lax.rsqrt(square - mean * mean + norm_eps)
    h1 = ((values - mean) * inverse * r.smallf[0:1, :] + r.smallf[1:2, :]).astype(BF16)
    r.h1[rows, :] = h1
    projected = dot(h1, r.wqkv[...]) + r.bqkv[0:1, :]
    front = projected[:, :384]
    turned = (front * r.cos[rows, :] + swap_halves(front) * r.sin[rows, :]).astype(BF16)
    r.qk[rows, :] = turned
    value = projected[:, 384:].astype(BF16)
    for h in range(3):
        r.q3[h, rows, :] = turned[:, 64 * h : 64 * h + 64]
        r.k3[h, rows, :] = turned[:, 192 + 64 * h : 256 + 64 * h]
        r.v3[h, rows, :] = value[:, 64 * h : 64 * h + 64]


def gather_and_project(r, spot):
    angle_tables(r)
    pltpu.make_async_copy(r.tok, r.tokp.at[spot.mp], r.own_sem).wait()
    from_sib = remote(r.tok, r.tokp.at[spot.mp], r.tc_send, r.tc_recv, spot.sib)
    from_sib.wait()
    small_y = remote(r.small, r.smallp.at[spot.mp], r.sm_send.at[0], r.sm_recv.at[0], spot.yp)
    small_c = remote(r.small, r.smallp.at[spot.mp], r.sm_send.at[1], r.sm_recv.at[1], spot.sib)
    small_y.wait()
    small_c.wait()
    on = r.smallp.at[spot.yp_mp]
    small_f = remote(on, on, r.sm_send.at[2], r.sm_recv.at[2], spot.sib)
    small_f.start()
    small_f.wait()
    r.smallp[spot.mp] = r.small[...]
    r.smallf[...] = jnp.concatenate([r.smallp[j] for j in range(4)], axis=1)

    def y_copy(i):
        rows = pl.ds(pl.multiple_of(i * GATHER_ROWS, 16), GATHER_ROWS)
        return remote(
            r.tok.at[rows], r.tokp.at[spot.mp, rows], r.ty_send.at[i], r.ty_recv.at[i], spot.yp
        )

    def forward(i):
        rows = pl.ds(pl.multiple_of(i * GATHER_ROWS, 16), GATHER_ROWS)
        piece = r.tokp.at[spot.yp_mp, rows]
        return remote(piece, piece, r.tf_send.at[i], r.tf_recv.at[i], spot.sib)

    y_copy(0).wait()
    forward(0).start()

    def chunk(i, carry):
        @pl.when(i + 1 < GATHERS)
        def _():
            y_copy(i + 1).wait()
            forward(i + 1).start()

        forward(i).wait()
        project(r, i)
        return carry

    lax.fori_loop(0, GATHERS, chunk, 0)


def tile_of(n):
    return n


def narrow_tile(n):
    tile = n + (n + 5) // 8 + (n + 3) // 8
    third = tile // 3
    return (tile, third * 576 - 32 * (third // 2))


def wide_tile(n):
    return (3 + 3 * n, 384 + 576 * n)


def attend_tile(r, tile, start, width):
    rows = pl.ds(pl.multiple_of(tile * TILE, 16), TILE)
    window = pl.ds(pl.multiple_of(start, 16), width)
    allowed = r.info[rows, 4:5] == r.kseg[tile, 0:1, :width]
    mask = jnp.where(allowed, 0.0, -1e30)
    outs = []
    logs = []
    for h in range(3):
        query = r.q3[h, rows, :] * BF16(0.125)
        scores = dot(query, r.k3[h, window, :], NT) + mask
        top = jnp.max(scores, axis=1, keepdims=True)
        exponent = jnp.exp(scores - top)
        total = jnp.sum(exponent, axis=1, keepdims=True)
        probs = (exponent * (1.0 / total)).astype(BF16)
        outs.append(dot(probs, r.v3[h, window, :]))
        logs.append(top + jnp.log(total))
    r.att[r.spot.mp, rows, :] = jnp.concatenate(outs, axis=1).astype(BF16)
    lane = lax.broadcasted_iota(jnp.int32, (TILE, 128), 1)
    r.lse[rows, :] = jnp.where(lane == 0, logs[0], jnp.where(lane == 1, logs[1], logs[2]))


def attend(r, spot):
    def copies(tile):
        rows = pl.ds(pl.multiple_of(tile * TILE, 16), TILE)
        piece = r.att.at[spot.mp, rows]
        other = r.att.at[spot.yp_mp, rows]
        return (
            remote(piece, piece, r.ac_send.at[tile], r.ac_recv.at[tile], spot.sib),
            remote(piece, piece, r.ay_send.at[tile], r.ay_recv.at[tile], spot.yp),
            remote(other, other, r.af_send.at[tile], r.af_recv.at[tile], spot.sib),
        )

    def send(tile):
        to_sib, to_y, _ = copies(tile)
        to_y.start()
        to_sib.start()

    def pass_on(tile):
        _, to_y, onward = copies(tile)
        to_y.wait()
        onward.start()

    def narrow(n, carry):
        @pl.when(n >= 2)
        def _():
            pass_on(narrow_tile(n - 2)[0])

        tile, start = narrow_tile(n)
        attend_tile(r, tile, start, NARROW)
        send(tile)
        return carry

    lax.fori_loop(0, 7, narrow, 0)

    def wide(n, carry):
        pass_on(narrow_tile(n + 5)[0])
        tile, start = wide_tile(n)
        attend_tile(r, tile, start, WIDE)
        send(tile)
        return carry

    lax.fori_loop(0, 2, wide, 0)
    for n in range(2):
        pass_on(wide_tile(n)[0])
    for tile in range(TILES):
        to_sib, _, onward = copies(tile)
        to_sib.wait()
        onward.wait()


def call_kernel(kernel, ins, outs, scratch, collective_id, limit):
    names = list(ins) + list(outs) + list(scratch)

    def body(*refs):
        r = Refs()
        for name, ref in zip(names, refs, strict=True):
            setattr(r, name, ref)
        r.spot = place()
        kernel(r, r.spot)

    spaces = {"vmem": pltpu.VMEM, "any": pl.ANY, "smem": pltpu.SMEM}
    results = pl.pallas_call(
        body,
        out_shape=[jax.ShapeDtypeStruct(shape, dtype) for shape, dtype, _ in outs.values()],
        in_specs=[pl.BlockSpec(memory_space=spaces[space]) for _, space in ins.values()],
        out_specs=[pl.BlockSpec(memory_space=spaces[space]) for _, _, space in outs.values()],
        scratch_shapes=list(scratch.values()),
        compiler_params=pltpu.CompilerParams(
            collective_id=collective_id, has_side_effects=True, vmem_limit_bytes=limit * MIB
        ),
    )(*[array for array, _ in ins.values()])
    return dict(zip(outs, results, strict=True))


def dma(*shape):
    return pltpu.SemaphoreType.DMA(shape) if shape else pltpu.SemaphoreType.DMA


def kernel_a(r, spot):
    greet([spot.sib, spot.yp])
    start_gather(r, spot)
    gather_and_project(r, spot)
    attend(r, spot)


def run_a(tokens, small, wqkv, bqkv, freq, info, kseg):
    ins = {
        "tok": (tokens, "vmem"),
        "small": (small, "vmem"),
        "wqkv": (wqkv, "vmem"),
        "bqkv": (bqkv, "vmem"),
        "freq": (freq, "vmem"),
        "info": (info, "vmem"),
        "kseg": (kseg, "vmem"),
    }
    outs = {
        "tokf": ((ROWS, 768), BF16, "vmem"),
        "h1": ((ROWS, 768), BF16, "vmem"),
        "qk": ((ROWS, 384), BF16, "vmem"),
        "q3": ((3, ROWS, 64), BF16, "vmem"),
        "k3": ((3, ROWS, 64), BF16, "vmem"),
        "v3": ((3, ROWS, 64), BF16, "vmem"),
        "cos": ((ROWS, 384), F32, "vmem"),
        "sin": ((ROWS, 384), F32, "vmem"),
        "smallf": ((8, 768), F32, "vmem"),
        "att": ((4, ROWS, 192), BF16, "vmem"),
        "lse": ((ROWS, 128), F32, "vmem"),
    }
    scratch = {
        "tokp": pltpu.VMEM((4, ROWS, 192), BF16),
        "smallp": pltpu.VMEM((4, 8, 192), F32),
        "own_sem": dma(),
        "ty_send": dma(GATHERS),
        "ty_recv": dma(GATHERS),
        "tf_send": dma(GATHERS),
        "tf_recv": dma(GATHERS),
        "tc_send": dma(),
        "tc_recv": dma(),
        "sm_send": dma(3),
        "sm_recv": dma(3),
        "ac_send": dma(TILES),
        "ac_recv": dma(TILES),
        "ay_send": dma(TILES),
        "ay_recv": dma(TILES),
        "af_send": dma(TILES),
        "af_recv": dma(TILES),
    }
    return call_kernel(kernel_a, ins, outs, scratch, 1, 56)


def key_windows(key_segment):
    starts = []
    for tile in range(TILES):
        if tile % 3 == 0 and tile:
            starts.append(384 + 576 * (tile // 3 - 1))
        else:
            starts.append(576 * (tile // 3) - 32 * (tile // 6))
    padded = jnp.pad(key_segment, (0, WIDE), constant_values=-3.0)
    return jnp.broadcast_to(
        jnp.stack([padded[s : s + WIDE] for s in starts])[:, None, :], (TILES, 8, WIDE)
    )


norm_eps = 1e-06
root_half = 0.7071067811865476
inv_root_two_pi = 0.3989422804014327


def norm_forward(values, gain, shift_bias):
    row_mean = jnp.mean(values, axis=-1, keepdims=True)
    row_square = jnp.mean(values * values, axis=-1, keepdims=True)
    inverse = lax.rsqrt(row_square - row_mean * row_mean + norm_eps)
    normed = (values - row_mean) * inverse
    return (normed * gain + shift_bias, normed, inverse)


def norm_backward(grad_normed, normed, inverse, gain):
    scaled = grad_normed * gain
    return inverse * (
        scaled
        - jnp.mean(scaled, axis=-1, keepdims=True)
        - normed * jnp.mean(scaled * normed, axis=-1, keepdims=True)
    )


def rotate_pairs(vectors, cosine_table, sine_table):
    split_at = vectors.shape[-1] // 2
    front_part = vectors[..., :split_at]
    back_part = vectors[..., split_at:]
    return jnp.concatenate(
        [
            front_part * cosine_table - back_part * sine_table,
            front_part * sine_table + back_part * cosine_table,
        ],
        axis=-1,
    )


def rotate_back(grads, rotated, cosine_table, sine_table):
    split_at = grads.shape[-1] // 2
    grad_front = grads[..., :split_at]
    grad_rear = grads[..., split_at:]
    rot_front = rotated[..., :split_at]
    rot_rear = rotated[..., split_at:]
    unrotated = jnp.concatenate(
        [
            grad_front * cosine_table + grad_rear * sine_table,
            grad_rear * cosine_table - grad_front * sine_table,
        ],
        axis=-1,
    )
    return (unrotated, grad_rear * rot_front - grad_front * rot_rear)


def masked_scores(query_blk, key_all, segment_blk, segment_ids, key_keep):
    scale_factor = query_blk.shape[-1] ** (-0.5)
    scores = scale_factor * jnp.einsum(
        "qhd,khd->hqk", query_blk, key_all, preferred_element_type=jnp.float32
    )
    allowed = (segment_blk[:, None] == segment_ids[None, :]) & key_keep[None, :]
    return jnp.where(allowed[None], scores, -1e30)


def contract_rows(left_side, right_side):
    return lax.dot_general(
        left_side, right_side, (((0,), (0,)), ((), ())), preferred_element_type=jnp.float32
    )


def contract_cols(left_side, right_side):
    return lax.dot_general(
        left_side, right_side, (((1,), (1,)), ((), ())), preferred_element_type=jnp.float32
    )


def local(
    tokens,
    w_qkv,
    b_qkv,
    freqs,
    w_out,
    b_out,
    norm1_gain,
    norm1_bias,
    norm2_gain,
    norm2_bias,
    w_up,
    b_up,
    w_down,
    b_down,
    cotangent,
    keep_mask,
    coords,
    block_group,
):
    row_count, width_loc = tokens.shape
    heads_loc = freqs.shape[1]
    block_count = row_count // SLOTS
    column = lax.axis_index("mp") * width_loc
    keep_float = keep_mask.astype(jnp.float32)
    keep_col = keep_float[:, None]
    group_now = block_group[0]
    kept_total = jnp.sum(keep_float)
    low_flag = (group_now == 0).astype(jnp.float32)
    counts = lax.psum(jnp.stack([kept_total * low_flag, kept_total * (1.0 - low_flag)]), "dp")
    own_weight = jnp.where(group_now == 0, counts[0], counts[1]) / (counts[0] + counts[1])
    row_index = jnp.arange(row_count, dtype=jnp.int32)
    segment_size = jnp.where(group_now == 0, GRID_LO * GRID_LO, SLOTS).astype(jnp.int32)
    segment_ids = row_index // segment_size
    key_keep = keep_mask > 0
    segment_float = segment_ids.astype(jnp.float32)
    key_segment = jnp.where(key_keep, segment_float, -1.0)
    info = jnp.stack(
        [coords[0].astype(F32), coords[1].astype(F32), keep_float, key_segment, segment_float]
        + [keep_float] * 3,
        axis=1,
    )
    small = jnp.stack(
        [
            part.astype(F32)
            for part in (norm1_gain, norm1_bias, norm2_gain, norm2_bias, b_out, b_down, b_out, b_out)
        ]
    )
    wqkv_flat = w_qkv.reshape(w_qkv.shape[0], 3 * width_loc)
    bqkv_flat = jnp.broadcast_to(b_qkv.reshape(1, 3 * width_loc).astype(F32), (8, 3 * width_loc))
    half_freqs = jnp.concatenate([freqs, freqs], axis=2).reshape(2, width_loc)
    freq = jnp.pad(jnp.concatenate([half_freqs, half_freqs], axis=1), ((0, 6), (0, 0)))
    a = run_a(tokens, small, wqkv_flat, bqkv_flat, freq, info, key_windows(key_segment))
    whole_tokens = a["tokf"]
    gain_one, bias_one, gain_two, bias_two, out_bias = (a["smallf"][n] for n in range(5))
    whole_cot = lax.all_gather(cotangent, "mp", axis=1, tiled=True)
    stream = whole_tokens.astype(jnp.float32)
    normed_one_low = a["h1"]
    _, normed_one, inverse_one = norm_forward(stream, gain_one, bias_one)
    coord_rows = coords[0].astype(jnp.float32)
    coord_cols = coords[1].astype(jnp.float32)
    angles = coord_rows[:, None, None] * freqs[0][None] + coord_cols[:, None, None] * freqs[1][None]
    cosine_table = jnp.cos(angles)
    sine_table = jnp.sin(angles)
    head_shape = (row_count, heads_loc, HEAD_DIM)
    query_low = a["qk"][:, :width_loc].reshape(head_shape)
    key_low = a["qk"][:, width_loc:].reshape(head_shape)
    query_rot, key_rot = query_low.astype(F32), key_low.astype(F32)
    value_low = a["v3"].transpose(1, 0, 2)
    block_shape = (block_count, SLOTS, heads_loc, HEAD_DIM)
    segment_blocks = segment_ids.reshape(block_count, SLOTS)
    attended = lax.dynamic_index_in_dim(a["att"], lax.axis_index("mp"), 0, False)
    log_total = (
        a["lse"][:, :heads_loc].reshape(block_count, SLOTS, heads_loc).transpose(0, 2, 1)
    )
    head_terms = jnp.dot(attended, w_out, preferred_element_type=jnp.float32)
    mid = stream + (lax.psum(head_terms, "mp") + out_bias.astype(jnp.float32))
    normed_two_out, normed_two, inverse_two = norm_forward(
        mid, gain_two.astype(jnp.float32), bias_two.astype(jnp.float32)
    )
    normed_two_low = normed_two_out.astype(jnp.bfloat16)
    mid_own = lax.dynamic_slice_in_dim(mid, column, width_loc, 1)
    hidden_pre = jnp.dot(normed_two_low, w_up, preferred_element_type=jnp.float32) + b_up.astype(
        jnp.float32
    )
    activated = jax.nn.gelu(hidden_pre, approximate=False).astype(jnp.bfloat16)
    mlp_terms = jnp.dot(activated, w_down, preferred_element_type=jnp.float32)
    mlp_own = lax.psum_scatter(
        mlp_terms.astype(jnp.bfloat16), "mp", scatter_dimension=1, tiled=True
    ).astype(jnp.float32)
    block_out = (keep_col * (mid_own + (mlp_own + b_down.astype(jnp.float32)))).astype(jnp.bfloat16)
    grad_out_full = keep_col * whole_cot.astype(jnp.float32)
    grad_out_own = keep_col * cotangent.astype(jnp.float32)
    grad_out_low = grad_out_full.astype(jnp.bfloat16)
    grad_b_down = jnp.sum(grad_out_own, axis=0)
    grad_w_down = contract_rows(activated, grad_out_low)
    grad_act = contract_cols(grad_out_low, w_down)
    derivative = 0.5 * (
        1.0 + lax.erf(hidden_pre * root_half)
    ) + hidden_pre * inv_root_two_pi * jnp.exp(-0.5 * hidden_pre * hidden_pre)
    grad_pre = (grad_act * derivative).astype(jnp.bfloat16)
    grad_b_up = jnp.sum(grad_pre.astype(jnp.float32), axis=0)
    grad_w_up = contract_rows(normed_two_low, grad_pre)
    norm_two_terms = contract_cols(grad_pre, w_up)
    grad_normed_two = lax.psum(norm_two_terms, "mp")
    grad_gain_two = lax.dynamic_slice_in_dim(
        jnp.sum(grad_normed_two * normed_two, axis=0), column, width_loc, 0
    )
    grad_bias_two = lax.dynamic_slice_in_dim(jnp.sum(grad_normed_two, axis=0), column, width_loc, 0)
    grad_mid = grad_out_full + norm_backward(
        grad_normed_two, normed_two, inverse_two, gain_two.astype(jnp.float32)
    )
    grad_mid_low = grad_mid.astype(jnp.bfloat16)
    grad_mid_own = lax.dynamic_slice_in_dim(grad_mid, column, width_loc, 1)
    grad_b_out = lax.dynamic_slice_in_dim(
        jnp.sum(grad_mid_low.astype(jnp.float32), axis=0), column, width_loc, 0
    )
    grad_w_out = contract_rows(attended, grad_mid_low)
    grad_attended = contract_cols(grad_mid_low, w_out).astype(jnp.bfloat16).reshape(block_shape)
    scale_factor = HEAD_DIM ** (-0.5)

    def back_block(carry, inputs):
        key_sum, value_sum = carry
        query_blk, segment_blk, grad_blk, log_blk = inputs
        scores = masked_scores(query_blk, key_low, segment_blk, segment_ids, key_keep)
        attn_probs = jnp.exp(scores - log_blk[..., None])
        grad_probs = jnp.einsum(
            "qhd,khd->hqk", grad_blk, value_low, preferred_element_type=jnp.float32
        )
        grad_scores = (
            attn_probs * (grad_probs - jnp.sum(attn_probs * grad_probs, axis=-1, keepdims=True))
        ).astype(jnp.bfloat16)
        grad_query = scale_factor * jnp.einsum(
            "hqk,khd->qhd", grad_scores, key_low, preferred_element_type=jnp.float32
        )
        key_sum = key_sum + scale_factor * jnp.einsum(
            "hqk,qhd->khd", grad_scores, query_blk, preferred_element_type=jnp.float32
        )
        value_sum = value_sum + jnp.einsum(
            "hqk,qhd->khd",
            attn_probs.astype(jnp.bfloat16),
            grad_blk,
            preferred_element_type=jnp.float32,
        )
        return ((key_sum, value_sum), grad_query.astype(jnp.bfloat16))

    empty_sum = jnp.zeros(head_shape, jnp.float32)
    (key_total, value_total), grad_query = lax.scan(
        back_block,
        (empty_sum, empty_sum),
        (query_low.reshape(block_shape), segment_blocks, grad_attended, log_total),
    )
    grad_key = key_total.astype(jnp.bfloat16)
    grad_value = value_total.astype(jnp.bfloat16)
    grad_query_raw, angle_query = rotate_back(
        grad_query.reshape(head_shape).astype(jnp.float32), query_rot, cosine_table, sine_table
    )
    grad_key_raw, angle_key = rotate_back(
        grad_key.astype(jnp.float32), key_rot, cosine_table, sine_table
    )
    grad_angle = angle_query + angle_key
    grad_freqs = jnp.stack(
        [
            jnp.sum(coord_rows[:, None, None] * grad_angle, axis=0),
            jnp.sum(coord_cols[:, None, None] * grad_angle, axis=0),
        ]
    )
    grad_projected = jnp.stack(
        [
            grad_query_raw.reshape(row_count, width_loc),
            grad_key_raw.reshape(row_count, width_loc),
            grad_value.reshape(row_count, width_loc).astype(jnp.float32),
        ],
        axis=1,
    ).astype(jnp.bfloat16)
    grad_b_qkv = jnp.sum(grad_projected.astype(jnp.float32), axis=0)
    grad_w_qkv = jnp.einsum(
        "rd,rce->dce", normed_one_low, grad_projected, preferred_element_type=jnp.float32
    )
    norm_one_terms = jnp.einsum(
        "rce,dce->rd", grad_projected, w_qkv, preferred_element_type=jnp.float32
    )
    grad_normed_one = lax.psum(norm_one_terms, "mp")
    grad_gain_one = lax.dynamic_slice_in_dim(
        jnp.sum(grad_normed_one * normed_one, axis=0), column, width_loc, 0
    )
    grad_bias_one = lax.dynamic_slice_in_dim(jnp.sum(grad_normed_one, axis=0), column, width_loc, 0)
    grad_stream = norm_backward(
        grad_normed_one, normed_one, inverse_one, gain_one.astype(jnp.float32)
    )
    input_grad = grad_mid_own + lax.dynamic_slice_in_dim(grad_stream, column, width_loc, 1)
    all_sums = lax.psum(
        (
            own_weight * grad_w_qkv,
            own_weight * grad_b_qkv,
            own_weight * grad_freqs,
            own_weight * grad_w_out,
            own_weight * grad_b_out,
            own_weight * grad_gain_one,
            own_weight * grad_bias_one,
            own_weight * grad_gain_two,
            own_weight * grad_bias_two,
            own_weight * grad_w_up,
            own_weight * grad_b_up,
            own_weight * grad_w_down,
            own_weight * grad_b_down,
        ),
        "dp",
    )
    return (
        block_out,
        input_grad,
        all_sums[0],
        all_sums[1],
        all_sums[2],
        all_sums[3],
        all_sums[4],
        all_sums[5],
        all_sums[6],
        all_sums[7],
        all_sums[8],
        all_sums[9],
        all_sums[10],
        all_sums[11],
        all_sums[12],
    )


def solution(mesh):
    return jax.shard_map(
        local,
        mesh=mesh,
        in_specs=(
            P("dp", "mp"),
            P(None, None, "mp"),
            P(None, "mp"),
            P(None, "mp", None),
            P("mp", None),
            P("mp"),
            P("mp"),
            P("mp"),
            P("mp"),
            P("mp"),
            P(None, "mp"),
            P("mp"),
            P("mp", None),
            P("mp"),
            P("dp", "mp"),
            P("dp"),
            P(None, "dp"),
            P("dp"),
        ),
        out_specs=(
            P("dp", "mp"),
            P("dp", "mp"),
            P(None, None, "mp"),
            P(None, "mp"),
            P(None, "mp", None),
            P("mp", None),
            P("mp"),
            P("mp"),
            P("mp"),
            P("mp"),
            P("mp"),
            P(None, "mp"),
            P("mp"),
            P("mp", None),
            P("mp"),
        ),
        check_vma=False,
    )
```

```python
import functools

import jax
import jax.numpy as jnp
from jax import lax
from jax.experimental import pallas as pl
from jax.experimental.pallas import tpu as pltpu
from jax.sharding import PartitionSpec as P

HEAD_DIM = 64
GRID_LO = 14
SLOTS = 576

MESH = pl.DeviceIdType.MESH
MIB = 1024 * 1024
VM = pltpu.VMEM
F32 = jnp.float32
BF16 = jnp.bfloat16
NT = (((1,), (1,)), ((), ()))
TN = (((0,), (0,)), ((), ()))
NN = (((1,), (0,)), ((), ()))

ROWS = 1728
TILE = 192
TILES = ROWS // TILE
NARROW = 608
WIDE = 768
GATHER_ROWS = 288
GATHERS = ROWS // GATHER_ROWS


class Refs:
    pass


def dot(left, right, dims=NN):
    return lax.dot_general(left, right, dims, preferred_element_type=F32)


def remote(src, dst, send, recv, device):
    return pltpu.make_async_remote_copy(
        src_ref=src, dst_ref=dst, send_sem=send, recv_sem=recv, device_id=device, device_id_type=MESH
    )


def place():
    spot = Refs()
    spot.dp = lax.axis_index("dp")
    spot.mp = lax.axis_index("mp")
    spot.y = spot.mp // 2
    spot.c = spot.mp % 2
    spot.sib_mp = 2 * spot.y + 1 - spot.c
    spot.yp_mp = 2 * (1 - spot.y) + spot.c
    spot.diag_mp = 2 * (1 - spot.y) + 1 - spot.c
    spot.sib = (spot.dp, spot.sib_mp)
    spot.yp = (spot.dp, spot.yp_mp)
    return spot


def greet(devices):
    barrier = pltpu.get_barrier_semaphore()
    for device in devices:
        pl.semaphore_signal(barrier, inc=1, device_id=device, device_id_type=MESH)
    pl.semaphore_wait(barrier, len(devices))


def sin_cos(angle):
    turns = jnp.floor(angle * 0.6366197723675814 + 0.5)
    rest = angle - turns * 1.5703125
    rest = rest - turns * 4.837512969970703e-4
    rest = rest - turns * 7.549789948768648e-8
    square = rest * rest
    sine = rest + rest * square * (
        -1.6666654611e-1 + square * (8.3321608736e-3 + square * -1.9515295891e-4)
    )
    cosine = (
        1.0
        - 0.5 * square
        + square
        * square
        * (4.166664568298827e-2 + square * (-1.388731625493765e-3 + square * 2.443315711809948e-5))
    )
    quarter = turns - 4.0 * jnp.floor(turns * 0.25)
    odd = (quarter == 1.0) | (quarter == 3.0)
    sine_sign = jnp.where(quarter >= 2.0, -1.0, 1.0)
    cosine_sign = jnp.where((quarter == 1.0) | (quarter == 2.0), -1.0, 1.0)
    return (
        jnp.where(odd, cosine, sine) * sine_sign,
        jnp.where(odd, sine, cosine) * cosine_sign,
    )


def front_lanes(shape):
    return lax.broadcasted_iota(jnp.int32, shape, 1) % HEAD_DIM < HEAD_DIM // 2


def swap_halves(values):
    width = values.shape[1]
    half = HEAD_DIM // 2
    return jnp.where(
        front_lanes(values.shape),
        pltpu.roll(values, width - half, 1),
        pltpu.roll(values, half, 1),
    )


def start_gather(r, spot):
    own = pltpu.make_async_copy(r.tok, r.tokp.at[spot.mp], r.own_sem)
    own.start()
    for i in range(GATHERS):
        rows = pl.ds(i * GATHER_ROWS, GATHER_ROWS)
        remote(
            r.tok.at[rows], r.tokp.at[spot.mp, rows], r.ty_send.at[i], r.ty_recv.at[i], spot.yp
        ).start()
    remote(r.tok, r.tokp.at[spot.mp], r.tc_send, r.tc_recv, spot.sib).start()
    remote(r.small, r.smallp.at[spot.mp], r.sm_send.at[0], r.sm_recv.at[0], spot.yp).start()
    remote(r.small, r.smallp.at[spot.mp], r.sm_send.at[1], r.sm_recv.at[1], spot.sib).start()


def angle_tables(r):
    step = 144

    def block(i, carry):
        rows = pl.ds(pl.multiple_of(i * step, 16), step)
        angle = r.info[rows, 0:1] * r.freq[0:1, :] + r.info[rows, 1:2] * r.freq[1:2, :]
        sine, cosine = sin_cos(angle)
        r.cos[rows, :] = cosine
        r.sin[rows, :] = jnp.where(front_lanes(sine.shape), -sine, sine)
        return carry

    lax.fori_loop(0, ROWS // step, block, 0)


def project(r, i):
    rows = pl.ds(pl.multiple_of(i * GATHER_ROWS, 16), GATHER_ROWS)
    values = jnp.concatenate([r.tokp[j, rows, :].astype(F32) for j in range(4)], axis=1)
    r.tokf[rows, :] = values.astype(BF16)
    mean = jnp.mean(values, axis=1, keepdims=True)
    square = jnp.mean(values * values, axis=1, keepdims=True)
    inverse = lax.rsqrt(square - mean * mean + norm_eps)
    h1 = ((values - mean) * inverse * r.smallf[0:1, :] + r.smallf[1:2, :]).astype(BF16)
    r.h1[rows, :] = h1
    projected = dot(h1, r.wqkv[...]) + r.bqkv[0:1, :]
    front = projected[:, :384]
    turned = (front * r.cos[rows, :] + swap_halves(front) * r.sin[rows, :]).astype(BF16)
    r.qk[rows, :] = turned
    value = projected[:, 384:].astype(BF16)
    for h in range(3):
        r.q3[h, rows, :] = turned[:, 64 * h : 64 * h + 64]
        r.k3[h, rows, :] = turned[:, 192 + 64 * h : 256 + 64 * h]
        r.v3[h, rows, :] = value[:, 64 * h : 64 * h + 64]


def gather_and_project(r, spot):
    angle_tables(r)
    pltpu.make_async_copy(r.tok, r.tokp.at[spot.mp], r.own_sem).wait()
    from_sib = remote(r.tok, r.tokp.at[spot.mp], r.tc_send, r.tc_recv, spot.sib)
    from_sib.wait()
    small_y = remote(r.small, r.smallp.at[spot.mp], r.sm_send.at[0], r.sm_recv.at[0], spot.yp)
    small_c = remote(r.small, r.smallp.at[spot.mp], r.sm_send.at[1], r.sm_recv.at[1], spot.sib)
    small_y.wait()
    small_c.wait()
    on = r.smallp.at[spot.yp_mp]
    small_f = remote(on, on, r.sm_send.at[2], r.sm_recv.at[2], spot.sib)
    small_f.start()
    small_f.wait()
    r.smallp[spot.mp] = r.small[...]
    r.smallf[...] = jnp.concatenate([r.smallp[j] for j in range(4)], axis=1)

    def y_copy(i):
        rows = pl.ds(pl.multiple_of(i * GATHER_ROWS, 16), GATHER_ROWS)
        return remote(
            r.tok.at[rows], r.tokp.at[spot.mp, rows], r.ty_send.at[i], r.ty_recv.at[i], spot.yp
        )

    def forward(i):
        rows = pl.ds(pl.multiple_of(i * GATHER_ROWS, 16), GATHER_ROWS)
        piece = r.tokp.at[spot.yp_mp, rows]
        return remote(piece, piece, r.tf_send.at[i], r.tf_recv.at[i], spot.sib)

    y_copy(0).wait()
    forward(0).start()

    def chunk(i, carry):
        @pl.when(i + 1 < GATHERS)
        def _():
            y_copy(i + 1).wait()
            forward(i + 1).start()

        forward(i).wait()
        project(r, i)
        return carry

    lax.fori_loop(0, GATHERS, chunk, 0)


def narrow_tile(n):
    tile = n + (n + 5) // 8 + (n + 3) // 8
    third = tile // 3
    return (tile, third * 576 - 32 * (third // 2))


def wide_tile(n):
    return (3 + 3 * n, 384 + 576 * n)


def attend_tile(r, tile, start, width):
    rows = pl.ds(pl.multiple_of(tile * TILE, 16), TILE)
    window = pl.ds(pl.multiple_of(start, 16), width)
    allowed = r.info[rows, 4:5] == r.kseg[tile, 0:1, :width]
    mask = jnp.where(allowed, 0.0, -1e30)
    outs = []
    logs = []
    for h in range(3):
        query = r.q3[h, rows, :] * BF16(0.125)
        scores = dot(query, r.k3[h, window, :], NT) + mask
        top = jnp.max(scores, axis=1, keepdims=True)
        exponent = jnp.exp(scores - top)
        total = jnp.sum(exponent, axis=1, keepdims=True)
        probs = (exponent * (1.0 / total)).astype(BF16)
        outs.append(dot(probs, r.v3[h, window, :]))
        logs.append(top + jnp.log(total))
    r.att[r.spot.mp, rows, :] = jnp.concatenate(outs, axis=1).astype(BF16)
    lane = lax.broadcasted_iota(jnp.int32, (TILE, 128), 1)
    r.lse[rows, :] = jnp.where(lane == 0, logs[0], jnp.where(lane == 1, logs[1], logs[2]))


def attend(r, spot):
    def copies(tile):
        rows = pl.ds(pl.multiple_of(tile * TILE, 16), TILE)
        piece = r.att.at[spot.mp, rows]
        other = r.att.at[spot.yp_mp, rows]
        return (
            remote(piece, piece, r.ac_send.at[tile], r.ac_recv.at[tile], spot.sib),
            remote(piece, piece, r.ay_send.at[tile], r.ay_recv.at[tile], spot.yp),
            remote(other, other, r.af_send.at[tile], r.af_recv.at[tile], spot.sib),
        )

    def send(tile):
        to_sib, to_y, _ = copies(tile)
        to_y.start()
        to_sib.start()

    def pass_on(tile):
        _, to_y, onward = copies(tile)
        to_y.wait()
        onward.start()

    def narrow(n, carry):
        @pl.when(n >= 2)
        def _():
            pass_on(narrow_tile(n - 2)[0])

        tile, start = narrow_tile(n)
        attend_tile(r, tile, start, NARROW)
        send(tile)
        return carry

    lax.fori_loop(0, 7, narrow, 0)

    def wide(n, carry):
        pass_on(narrow_tile(n + 5)[0])
        tile, start = wide_tile(n)
        attend_tile(r, tile, start, WIDE)
        send(tile)
        return carry

    lax.fori_loop(0, 2, wide, 0)
    for n in range(2):
        pass_on(wide_tile(n)[0])
    for tile in range(TILES):
        to_sib, _, onward = copies(tile)
        to_sib.wait()
        onward.wait()


def call_kernel(kernel, ins, outs, scratch, collective_id, limit, dp_bits):
    names = list(ins) + list(outs) + list(scratch)

    def body(*refs):
        r = Refs()
        for name, ref in zip(names, refs, strict=True):
            setattr(r, name, ref)
        r.spot = place()
        r.dp_bits = dp_bits
        kernel(r, r.spot)

    results = pl.pallas_call(
        body,
        out_shape=[jax.ShapeDtypeStruct(shape, dtype) for shape, dtype, _ in outs.values()],
        in_specs=[pl.BlockSpec(memory_space=space) for _, space in ins.values()],
        out_specs=[pl.BlockSpec(memory_space=space) for _, _, space in outs.values()],
        scratch_shapes=list(scratch.values()),
        compiler_params=pltpu.CompilerParams(
            collective_id=collective_id, has_side_effects=True, vmem_limit_bytes=limit * MIB
        ),
    )(*[array for array, _ in ins.values()])
    named = Refs()
    for name, result in zip(outs, results, strict=True):
        setattr(named, name, result)
    return named


def dma(*shape):
    return pltpu.SemaphoreType.DMA(shape) if shape else pltpu.SemaphoreType.DMA


def dp_partner(spot, bit):
    mine = (spot.dp // (1 << bit)) % 2
    return spot.dp + (1 - 2 * mine) * (1 << bit)


def sum_counts(r, spot):
    total = r.cnt[...]
    for bit in range(r.dp_bits):
        r.cnts[bit] = total
        copy = remote(
            r.cnts.at[bit],
            r.cntr.at[bit],
            r.cn_send.at[bit],
            r.cn_recv.at[bit],
            (dp_partner(spot, bit), spot.mp),
        )
        copy.start()
        copy.wait()
        total = total + r.cntr[bit]
    low = total[:, 0:1]
    high = total[:, 1:2]
    own = jnp.where(r.cnt[:, 2:3] > 0.5, low, high) / (low + high)
    r.share[...] = jnp.broadcast_to(own, (8, 128))


def kernel_a(r, spot):
    greet([spot.sib, spot.yp] + [(dp_partner(spot, bit), spot.mp) for bit in range(r.dp_bits)])
    start_gather(r, spot)
    sum_counts(r, spot)
    gather_and_project(r, spot)
    attend(r, spot)


def run_a(tokens, small, wqkv, bqkv, freq, info, kseg, cnt, dp_bits):
    ins = dict(
        tok=(tokens, VM),
        small=(small, VM),
        wqkv=(wqkv, VM),
        bqkv=(bqkv, VM),
        freq=(freq, VM),
        info=(info, VM),
        kseg=(kseg, VM),
        cnt=(cnt, VM),
    )
    outs = dict(
        tokf=((ROWS, 768), BF16, VM),
        h1=((ROWS, 768), BF16, VM),
        qk=((ROWS, 384), BF16, VM),
        q3=((3, ROWS, 64), BF16, VM),
        k3=((3, ROWS, 64), BF16, VM),
        v3=((3, ROWS, 64), BF16, VM),
        cos=((ROWS, 384), F32, VM),
        sin=((ROWS, 384), F32, VM),
        smallf=((8, 768), F32, VM),
        att=((4, ROWS, 192), BF16, VM),
        lse=((ROWS, 128), F32, VM),
        share=((8, 128), F32, VM),
    )
    scratch = dict(
        cnts=pltpu.VMEM((dp_bits, 8, 128), F32),
        cntr=pltpu.VMEM((dp_bits, 8, 128), F32),
        cn_send=dma(dp_bits),
        cn_recv=dma(dp_bits),
        tokp=pltpu.VMEM((4, ROWS, 192), BF16),
        smallp=pltpu.VMEM((4, 8, 192), F32),
        own_sem=dma(),
        ty_send=dma(GATHERS),
        ty_recv=dma(GATHERS),
        tf_send=dma(GATHERS),
        tf_recv=dma(GATHERS),
        tc_send=dma(),
        tc_recv=dma(),
        sm_send=dma(3),
        sm_recv=dma(3),
        ac_send=dma(TILES),
        ac_recv=dma(TILES),
        ay_send=dma(TILES),
        ay_recv=dma(TILES),
        af_send=dma(TILES),
        af_recv=dma(TILES),
    )
    return call_kernel(kernel_a, ins, outs, scratch, 1, 56, dp_bits)


PART = ROWS // 4
SUB = 144
SUBS = PART // SUB


def part_order(spot, n):
    y = spot.y + (1 - n // 2) * (1 - 2 * spot.y)
    c = spot.c + (1 - n % 2) * (1 - 2 * spot.c)
    return 2 * y + c


def phi_parts(value):
    scaled = jnp.clip(value * root_half, -3.832506856900711, 3.832506856900711)
    square = scaled * scaled
    top = 0.00022905065861350646
    for factor in (
        0.0034082910107109506,
        0.050955695062380861,
        0.18520832239976145,
        1.128379143519084,
    ):
        top = top * square + factor
    low = -1.1791602954361697e-7
    for factor in (
        0.000023547966471313185,
        0.0010179625278914885,
        0.014070470171167667,
        0.11098505178285362,
        0.49746925110067538,
        1.0,
    ):
        low = low * square + factor
    error = scaled * top / low
    return (0.5 + 0.5 * error, inv_root_two_pi * jnp.exp(-0.5 * value * value))


def own_columns(spot, values):
    return pltpu.roll(values, (768 - 192 * spot.mp) % 768, 1)[:, :192]


def core_columns(spot, values):
    cut = [values[:, 192 * j : 192 * j + 192] for j in range(4)]
    mine = [jnp.where(spot.c == 0, cut[2 * y], cut[2 * y + 1]) for y in range(2)]
    other = [jnp.where(spot.c == 0, cut[2 * y + 1], cut[2 * y]) for y in range(2)]
    return (mine, other)


def part_rows(k, length=PART, offset=0):
    return pl.ds(pl.multiple_of(k * PART + offset, 16), length)


def b_gathers(r, spot):
    own = r.wof.at[pl.ds(pl.multiple_of(192 * spot.mp, 16), 192)]
    other = r.wof.at[pl.ds(pl.multiple_of(192 * spot.yp_mp, 16), 192)]
    moves = Refs()
    moves.cot_own = pltpu.make_async_copy(r.cot, r.cotp.at[spot.mp], r.own_sem.at[0])
    moves.wo_own = pltpu.make_async_copy(r.wout, own, r.own_sem.at[1])
    moves.wo_y = remote(r.wout, own, r.wo_send.at[0], r.wo_recv.at[0], spot.yp)
    moves.wo_c = remote(r.wout, own, r.wo_send.at[1], r.wo_recv.at[1], spot.sib)
    moves.wo_f = remote(other, other, r.wo_send.at[2], r.wo_recv.at[2], spot.sib)
    moves.cot_c = remote(r.cot, r.cotp.at[spot.mp], r.ct_send.at[0], r.ct_recv.at[0], spot.sib)
    moves.cot_y = remote(r.cot, r.cotp.at[spot.mp], r.ct_send.at[1], r.ct_recv.at[1], spot.yp)
    piece = r.cotp.at[spot.yp_mp]
    moves.cot_f = remote(piece, piece, r.ct_send.at[2], r.ct_recv.at[2], spot.sib)
    return moves


def mlp_forward(r, spot, k):
    rows = part_rows(k)
    terms = r.smallf[4:5, :]
    for j in range(4):
        terms = terms + dot(r.att[j, rows, :], r.wof[192 * j : 192 * j + 192, :])
    r.work[...] = r.tokf[rows, :].astype(F32) + terms

    def norm(i, carry):
        local = pl.ds(pl.multiple_of(i * 48, 16), 48)
        rows_now = pl.ds(pl.multiple_of(k * PART + i * 48, 16), 48)
        mid = r.work[local, :]
        r.midc[rows_now, :] = own_columns(spot, mid)
        mean = jnp.mean(mid, axis=1, keepdims=True)
        square = jnp.mean(mid * mid, axis=1, keepdims=True)
        inverse = lax.rsqrt(square - mean * mean + norm_eps)
        normed = (mid - mean) * inverse
        r.n2[local, :] = normed
        r.inv2[local, :] = jnp.broadcast_to(inverse, (48, 128))
        r.h2[rows_now, :] = (normed * r.smallf[2:3, :] + r.smallf[3:4, :]).astype(BF16)
        return carry

    lax.fori_loop(0, PART // 48, norm, 0)
    r.work[...] = dot(r.h2[rows, :], r.wup[...]) + r.bup[0:1, :]

    def gelu(i, carry):
        local = pl.ds(pl.multiple_of(i * 48, 16), 48)
        rows_now = pl.ds(pl.multiple_of(k * PART + i * 48, 16), 48)
        value = r.work[local, :]
        lower, density = phi_parts(value)
        r.act[rows_now, :] = (value * lower).astype(BF16)
        r.work[local, :] = lower + value * density
        return carry

    lax.fori_loop(0, PART // 48, gelu, 0)


def mlp_output(r, spot, k):
    rows = part_rows(k)
    mine, other = core_columns(spot, dot(r.act[rows, :], r.wdown[...]))
    for y in range(2):
        r.mown[y, rows, :] = mine[y]
        r.msend[y, rows, :] = other[y].astype(BF16)


def mlp_backward(r, spot, k):
    rows = part_rows(k)

    def cotangents(i, carry):
        rows_now = pl.ds(pl.multiple_of(k * PART + i * SUB, 16), SUB)
        values = jnp.concatenate([r.cotp[j, rows_now, :].astype(F32) for j in range(4)], axis=1)
        r.gout[rows_now, :] = (values * r.info[rows_now, 2:3]).astype(BF16)
        return carry

    lax.fori_loop(0, SUBS, cotangents, 0)
    g_pre = (dot(r.gout[rows, :], r.wdown[...], NT) * r.work[...]).astype(BF16)
    r.gpre[rows, :] = g_pre
    r.sums[0:1, :] += jnp.sum(g_pre.astype(F32), axis=0, keepdims=True)
    r.work[...] = dot(r.gpre[rows, :], r.wup[...], NT)


def kernel_b(r, spot):
    greet([spot.sib, spot.yp])
    moves = b_gathers(r, spot)
    for move in (moves.wo_own, moves.cot_own, moves.wo_y, moves.wo_c, moves.cot_y, moves.cot_c):
        move.start()
    r.sums[...] = jnp.zeros_like(r.sums)
    moves.wo_own.wait()
    moves.wo_y.wait()
    moves.wo_f.start()
    moves.wo_c.wait()
    moves.wo_f.wait()

    def reduce_copies():
        return (
            remote(r.ps.at[0], r.rb.at[0], r.rs_send.at[0], r.rs_recv.at[0], spot.sib),
            remote(r.ps.at[1], r.rb.at[1], r.rs_send.at[1], r.rs_recv.at[1], spot.yp),
            remote(r.ps.at[2], r.rb.at[2], r.rs_send.at[2], r.rs_recv.at[2], spot.sib),
        )

    def out_copy(n, k):
        piece = r.msend.at[:, part_rows(k)]
        return remote(
            piece, r.mrecv.at[:, part_rows(k)], r.mc_send.at[n], r.mc_recv.at[n], spot.sib
        )

    def part(n, carry):
        k = part_order(spot, n)
        mlp_forward(r, spot, k)
        mlp_output(r, spot, k)
        out_copy(n, k).start()

        @pl.when(n == 0)
        def _():
            moves.cot_own.wait()
            moves.cot_c.wait()
            moves.cot_y.wait()
            moves.cot_f.start()
            moves.cot_f.wait()

        mlp_backward(r, spot, k)

        @pl.when(n == 0)
        def _():
            r.ps[0] = r.work[...].astype(BF16)
            reduce_copies()[0].start()

        @pl.when(n == 1)
        def _():
            reduce_copies()[0].wait()
            r.ps[1] = (r.work[...] + r.rb[0].astype(F32)).astype(BF16)
            reduce_copies()[1].start()

        @pl.when(n == 2)
        def _():
            r.ps[2] = r.work[...].astype(BF16)
            reduce_copies()[2].start()

        return carry

    lax.fori_loop(0, 4, part, 0)
    reduce_copies()[1].wait()
    reduce_copies()[2].wait()

    def norm_back(i, carry):
        local = pl.ds(pl.multiple_of(i * 48, 16), 48)
        rows_now = pl.ds(pl.multiple_of(spot.mp * PART + i * 48, 16), 48)
        grad = r.work[local, :] + r.rb[2, local, :].astype(F32) + r.rb[1, local, :].astype(F32)
        normed = r.n2[local, :]
        r.sums[1:2, :] += jnp.sum(grad * normed, axis=0, keepdims=True)
        r.sums[2:3, :] += jnp.sum(grad, axis=0, keepdims=True)
        scaled = grad * r.smallf[2:3, :]
        first = jnp.mean(scaled, axis=1, keepdims=True)
        second = jnp.mean(scaled * normed, axis=1, keepdims=True)
        back = r.inv2[local, 0:1] * (scaled - first - normed * second)
        r.gatt[rows_now, :] = (r.gout[rows_now, :].astype(F32) + back).astype(BF16)
        return carry

    def spread(s):
        own = r.gatt.at[part_rows(spot.mp, SUB, s * SUB)]
        other = r.gatt.at[part_rows(spot.yp_mp, SUB, s * SUB)]
        return (
            remote(own, own, r.gy_send.at[s], r.gy_recv.at[s], spot.yp),
            remote(own, own, r.gc_send.at[s], r.gc_recv.at[s], spot.sib),
            remote(other, other, r.gf_send.at[s], r.gf_recv.at[s], spot.sib),
        )

    for s in range(SUBS):
        lax.fori_loop(3 * s, 3 * s + 3, norm_back, 0)
        to_y, to_sib, _ = spread(s)
        to_y.start()
        to_sib.start()

    r.gdn[...] = (dot(r.act[...], r.gout[...], TN) * r.share[0:1, 0:1]).astype(BF16)

    for n in range(4):
        out_copy(n, part_order(spot, n)).wait()

    def chip_sum(i, carry):
        rows_now = pl.ds(pl.multiple_of(i * SUB, 16), SUB)
        r.ysend[rows_now, :] = (
            r.mown[1 - spot.y, rows_now, :] + r.mrecv[1 - spot.y, rows_now, :].astype(F32)
        ).astype(BF16)
        return carry

    lax.fori_loop(0, ROWS // SUB, chip_sum, 0)
    out_y = remote(r.ysend, r.yrecv, r.my_send, r.my_recv, spot.yp)
    out_y.start()
    for s in range(SUBS):
        to_y, _, onward = spread(s)
        to_y.wait()
        onward.start()
    r.gup[...] = (dot(r.h2[...], r.gpre[...], TN) * r.share[0:1, 0:1]).astype(BF16)
    out_y.wait()
    bias = own_columns(spot, jnp.broadcast_to(r.smallb[0:1, :], (8, 768)))[0:1, :]

    def finish(i, carry):
        rows_now = pl.ds(pl.multiple_of(i * SUB, 16), SUB)
        total = (
            r.mown[spot.y, rows_now, :]
            + r.mrecv[spot.y, rows_now, :].astype(F32)
            + r.yrecv[rows_now, :].astype(F32)
        )
        keep = r.info[rows_now, 2:3]
        r.out[rows_now, :] = (keep * (r.midc[rows_now, :] + (total + bias))).astype(BF16)
        cot = r.cot[rows_now, :].astype(F32) * keep
        r.sums[3:4, :192] += jnp.sum(cot, axis=0, keepdims=True)
        return carry

    lax.fori_loop(0, ROWS // SUB, finish, 0)
    for s in range(SUBS):
        _, to_sib, onward = spread(s)
        to_sib.wait()
        onward.wait()


def run_b(a, cot, wout, wup, bup, wdown, info, dp_bits):
    ins = dict(
        att=(a.att, VM),
        tokf=(a.tokf, VM),
        cot=(cot, VM),
        wout=(wout, VM),
        wup=(wup, VM),
        bup=(bup, VM),
        wdown=(wdown, VM),
        info=(info, VM),
        smallf=(a.smallf, VM),
        smallb=(a.smallb, VM),
        share=(a.share, VM),
    )
    outs = dict(
        gatt=((ROWS, 768), BF16, VM),
        out=((ROWS, 192), BF16, VM),
        gdn=((768, 768), BF16, VM),
        gup=((768, 768), BF16, VM),
        sums=((8, 768), F32, VM),
    )
    scratch = dict(
        wof=pltpu.VMEM((768, 768), BF16),
        cotp=pltpu.VMEM((4, ROWS, 192), BF16),
        gout=pltpu.VMEM((ROWS, 768), BF16),
        h2=pltpu.VMEM((ROWS, 768), BF16),
        act=pltpu.VMEM((ROWS, 768), BF16),
        gpre=pltpu.VMEM((ROWS, 768), BF16),
        work=pltpu.VMEM((PART, 768), F32),
        n2=pltpu.VMEM((PART, 768), F32),
        inv2=pltpu.VMEM((PART, 128), F32),
        midc=pltpu.VMEM((ROWS, 192), F32),
        ps=pltpu.VMEM((3, PART, 768), BF16),
        rb=pltpu.VMEM((3, PART, 768), BF16),
        mown=pltpu.VMEM((2, ROWS, 192), F32),
        msend=pltpu.VMEM((2, ROWS, 192), BF16),
        mrecv=pltpu.VMEM((2, ROWS, 192), BF16),
        ysend=pltpu.VMEM((ROWS, 192), BF16),
        yrecv=pltpu.VMEM((ROWS, 192), BF16),
        own_sem=dma(2),
        wo_send=dma(3),
        wo_recv=dma(3),
        ct_send=dma(3),
        ct_recv=dma(3),
        rs_send=dma(3),
        rs_recv=dma(3),
        mc_send=dma(4),
        mc_recv=dma(4),
        my_send=dma(),
        my_recv=dma(),
        gy_send=dma(SUBS),
        gy_recv=dma(SUBS),
        gc_send=dma(SUBS),
        gc_recv=dma(SUBS),
        gf_send=dma(SUBS),
        gf_recv=dma(SUBS),
    )
    return call_kernel(kernel_b, ins, outs, scratch, 2, 60, dp_bits)


class Reduce:
    def __init__(self, spot, acc, arrive, res, order, send, recv):
        self.spot, self.acc, self.arrive, self.res = spot, acc, arrive, res
        self.send, self.recv = send, recv
        self.phases = []
        self.at = 0
        offset, size, held = 0, acc.shape[0], None
        used = 0
        gathers = []
        for bit in order:
            mine = (spot.dp // (1 << bit)) % 2
            start = 0 if held is None else held
            source = acc if held is None else arrive
            if (size // 2) % 16 == 0:
                size = size // 2
                keep, away = start + mine * size, start + (1 - mine) * size
                offset = offset + mine * size
                gathers.append(("gather", bit, res, offset, offset, size, 0))
            else:
                keep, away = start, start
            self.phases.append(("sum", bit, source, away, keep, size, used))
            held = used
            used += size
        self.own = (held, offset, size)
        self.sums = len(self.phases)
        self.phases += gathers[::-1]

    def copy(self):
        kind, bit, source, away, keep, size, used = self.phases[self.at]
        piece = source.at[pl.ds(pl.multiple_of(away, 16), size)]
        target = self.arrive.at[pl.ds(used, size)] if kind == "sum" else piece
        device = (dp_partner(self.spot, bit), self.spot.mp)
        return remote(piece, target, self.send.at[self.at], self.recv.at[self.at], device)

    def start(self):
        self.copy().start()

    def add(self):
        _, _, source, _, keep, size, used = self.phases[self.at]
        last = self.at == self.sums - 1
        step = 48 if size % 48 == 0 else 16

        def block(i, carry):
            rows = pl.ds(pl.multiple_of(keep + i * step, 16), step)
            new = pl.ds(pl.multiple_of(used + i * step, 16), step)
            total = (source[rows, :].astype(F32) + self.arrive[new, :].astype(F32)).astype(BF16)
            if last:
                self.res[pl.ds(pl.multiple_of(self.own[1] + i * step, 16), step), :] = total
            else:
                self.arrive[new, :] = total
            return carry

        lax.fori_loop(0, size // step, block, 0)

    def advance(self):
        if self.at >= len(self.phases):
            return
        self.copy().wait()
        if self.phases[self.at][0] == "sum":
            self.add()
        self.at += 1
        if self.at < len(self.phases):
            self.start()


def arrive_rows(rows, dp_bits):
    total = 0
    for _ in range(dp_bits):
        rows = rows // 2 if (rows // 2) % 16 == 0 else rows
        total += rows
    return total


def back_tile(r, spot, tile, start, width):
    rows = pl.ds(pl.multiple_of(tile * TILE, 16), TILE)
    window = pl.ds(pl.multiple_of(start, 16), width)
    g_att = dot(r.gatt[rows, :], r.wout[...], NT).astype(BF16)
    allowed = r.info[window, 3:4] == r.qseg[tile, 0:1, :]
    mask = jnp.where(allowed, 0.0, -1e30)
    logs = jnp.transpose(r.lse[rows, :])
    outs = []
    for h in range(3):
        query = r.q3[h, rows, :] * BF16(0.125)
        keys = r.k3[h, window, :]
        grad = g_att[:, 64 * h : 64 * h + 64]
        probs = jnp.exp(dot(keys, query, NT) + mask - logs[h : h + 1, :])
        g_probs = dot(r.v3[h, window, :], grad, NT)
        center = jnp.sum(probs * g_probs, axis=0, keepdims=True)
        g_scores = (probs * (g_probs - center)).astype(BF16)
        r.dv[h, window, :] += dot(probs.astype(BF16), grad)
        r.dk[h, window, :] += dot(g_scores, query)
        outs.append(dot(keys, g_scores, TN) * 0.125)
    r.dq[rows, :] = jnp.transpose(jnp.concatenate(outs, axis=0)).astype(BF16)


def unrotate(r):
    step = 144

    def block(i, carry):
        rows = pl.ds(pl.multiple_of(i * step, 16), step)
        parts = [r.dq[rows, :].astype(F32)]
        parts += [r.dk[h, rows, :].astype(BF16).astype(F32) for h in range(3)]
        grads = jnp.concatenate(parts, axis=1)
        rotated = r.qk[rows, :].astype(F32)
        plain = grads * r.cos[rows, :] - swap_halves(grads) * r.sin[rows, :]
        values = jnp.concatenate([r.dv[h, rows, :] for h in range(3)], axis=1)
        packed = jnp.concatenate([plain, values], axis=1).astype(BF16)
        r.gproj[rows, :] = packed
        turn = grads * swap_halves(rotated)
        turn = jnp.where(front_lanes(turn.shape), -turn, turn)
        r.sums[0:1, :576] += jnp.sum(packed.astype(F32), axis=0, keepdims=True)
        r.sums[1:2, :384] += jnp.sum(turn * r.info[rows, 0:1], axis=0, keepdims=True)
        r.sums[2:3, :384] += jnp.sum(turn * r.info[rows, 1:2], axis=0, keepdims=True)
        r.sums[3:4, :] += jnp.sum(r.gatt[rows, :].astype(F32), axis=0, keepdims=True)
        return carry

    lax.fori_loop(0, ROWS // step, block, 0)


def first_norm_back(r, spot, n):
    rows = part_rows(n)
    r.work[...] = dot(r.gproj[rows, :], r.wqkv[...], NT)

    def block(i, carry):
        local = pl.ds(pl.multiple_of(i * 48, 16), 48)
        rows_now = pl.ds(pl.multiple_of(n * PART + i * 48, 16), 48)
        values = r.tokf[rows_now, :].astype(F32)
        mean = jnp.mean(values, axis=1, keepdims=True)
        square = jnp.mean(values * values, axis=1, keepdims=True)
        inverse = lax.rsqrt(square - mean * mean + norm_eps)
        normed = (values - mean) * inverse
        grad = r.work[local, :]
        scaled = grad * r.smallf[0:1, :]
        first = jnp.sum(scaled, axis=1, keepdims=True)
        second = jnp.sum(scaled * normed, axis=1, keepdims=True)
        lane = lax.broadcasted_iota(jnp.int32, (48, 128), 1)
        r.stat[rows_now, :] = jnp.where(lane == 0, first, jnp.where(lane == 1, second, inverse))
        r.n1[rows_now, :] = own_columns(spot, normed)
        mine, other = core_columns(spot, grad)
        for y in range(2):
            r.mown[y, rows_now, :] = mine[y]
            r.msend[y, rows_now, :] = other[y].astype(BF16)
        return carry

    lax.fori_loop(0, PART // 48, block, 0)


def kernel_c(r, spot):
    peers = [(dp_partner(spot, bit), spot.mp) for bit in range(r.dp_bits)]
    greet([spot.sib, spot.yp] + peers)
    load = pltpu.make_async_copy(r.att.at[spot.mp], r.attown, r.load_sem)
    load.start()
    order = list(range(r.dp_bits))
    turned = order[1:] + order[:1]
    down = Reduce(spot, r.gdn, r.ardn, r.resdn, order, r.dn_send, r.dn_recv)
    up = Reduce(spot, r.gup, r.arup, r.resup, turned, r.up_send, r.up_recv)
    out = Reduce(spot, r.accwo, r.arwo, r.reswo, order, r.wo_send, r.wo_recv)
    qkv = Reduce(spot, r.accqkv, r.arqkv, r.resqkv, order, r.qk_send, r.qk_recv)
    down.start()
    up.start()
    load.wait()
    r.accwo[...] = (dot(r.attown[...], r.gatt[...], TN) * r.share[0:1, 0:1]).astype(BF16)
    out.start()
    r.sums[...] = jnp.zeros_like(r.sums)
    r.sums[8:16, :] = r.sumsb[...]
    r.dk[...] = jnp.zeros_like(r.dk)
    r.dv[...] = jnp.zeros_like(r.dv)

    def narrow(n, carry):
        turn = n + spot.y * (6 - 2 * n)
        tile, start = narrow_tile(turn)
        back_tile(r, spot, tile, start, NARROW)
        return carry

    lax.fori_loop(0, 3, narrow, 0)
    down.advance()
    up.advance()
    out.advance()
    lax.fori_loop(3, 5, narrow, 0)
    down.advance()
    out.advance()
    lax.fori_loop(5, 7, narrow, 0)
    up.advance()
    down.advance()
    out.advance()

    def wide(n, carry):
        tile, start = wide_tile(n)
        back_tile(r, spot, tile, start, WIDE)
        return carry

    lax.fori_loop(0, 2, wide, 0)
    down.advance()
    up.advance()
    out.advance()
    unrotate(r)
    r.accqkv[...] = (dot(r.h1[...], r.gproj[...], TN) * r.share[0:1, 0:1]).astype(BF16)
    qkv.start()
    down.advance()
    up.advance()
    out.advance()

    def core_copy(n):
        piece = part_rows(n)
        return remote(
            r.msend.at[:, piece], r.mrecv.at[:, piece], r.mc_send.at[n], r.mc_recv.at[n], spot.sib
        )

    def y_copy(n):
        piece = part_rows(n)
        return remote(
            r.ysend.at[piece], r.yrecv.at[piece], r.my_send.at[n], r.my_recv.at[n], spot.yp
        )

    def pass_on(n):
        core_copy(n).wait()

        def chip_sum(i, carry):
            rows_now = pl.ds(pl.multiple_of(n * PART + i * SUB, 16), SUB)
            r.ysend[rows_now, :] = (
                r.mown[1 - spot.y, rows_now, :] + r.mrecv[1 - spot.y, rows_now, :].astype(F32)
            ).astype(BF16)
            return carry

        lax.fori_loop(0, SUBS, chip_sum, 0)
        y_copy(n).start()

    def part(n, carry):
        first_norm_back(r, spot, n)
        core_copy(n).start()

        @pl.when(n >= 1)
        def _():
            pass_on(n - 1)

        return carry

    lax.fori_loop(0, 2, part, 0)
    up.advance()
    qkv.advance()
    lax.fori_loop(2, 4, part, 0)
    pass_on(3)
    for t in range(13):
        r.strow[:, 128 * t : 128 * t + 128] = jnp.transpose(r.stat[128 * t : 128 * t + 128, :])[0:8, :]
    r.strow[:, 1664:1792] = jnp.transpose(
        jnp.concatenate([r.stat[1664:1728, :], jnp.zeros((64, 128), F32)], axis=0)
    )[0:8, :]
    to_sib = remote(r.strow, r.starr.at[0], r.st_send.at[0], r.st_recv.at[0], spot.sib)
    to_sib.start()
    qkv.advance()
    to_sib.wait()
    r.stsum[...] = r.strow[...] + r.starr[0]
    to_y = remote(r.stsum, r.starr.at[1], r.st_send.at[1], r.st_recv.at[1], spot.yp)
    to_y.start()
    down.advance()
    qkv.advance()
    to_y.wait()
    r.sttot[0:8, :] = r.stsum[...] + r.starr[1]
    for t in range(13):
        r.back[128 * t : 128 * t + 128, :] = jnp.transpose(r.sttot[:, 128 * t : 128 * t + 128])
    r.back[1664:1728, :] = jnp.transpose(r.sttot[:, 1664:1792])[0:64, :]
    for n in range(4):
        y_copy(n).wait()

    def finish(i, carry):
        rows = pl.ds(pl.multiple_of(i * SUB, 16), SUB)
        grad = (
            r.mown[spot.y, rows, :]
            + r.mrecv[spot.y, rows, :].astype(F32)
            + r.yrecv[rows, :].astype(F32)
        )
        normed = r.n1[rows, :]
        r.sums[4:5, :192] += jnp.sum(grad * normed, axis=0, keepdims=True)
        r.sums[5:6, :192] += jnp.sum(grad, axis=0, keepdims=True)
        first = r.back[rows, 0:1] * (1.0 / 768.0)
        second = r.back[rows, 1:2] * (1.0 / 768.0)
        scaled = grad * r.small[0:1, :]
        step_back = r.stat[rows, 2:3] * (scaled - first - normed * second)
        r.igrad[rows, :] = own_columns(spot, r.gatt[rows, :].astype(F32)) + step_back
        return carry

    lax.fori_loop(0, ROWS // SUB, finish, 0)
    r.sums[...] = r.sums[...] * r.share[0:1, 0:1]
    for step, device in enumerate([spot.sib, spot.yp] + peers):
        span = pl.ds(8, 8) if step < 2 else pl.ds(0, 16)
        r.sumx[step] = r.sums[...]
        copy = remote(
            r.sumx.at[step, span], r.sumr.at[step, span], r.su_send.at[step], r.su_recv.at[step], device
        )
        copy.start()
        qkv.advance()
        copy.wait()
        if step < 2:
            r.sums[9:11, :] = r.sumx[step, 9:11, :] + r.sumr[step, 9:11, :]
        else:
            r.sums[...] = r.sumx[step] + r.sumr[step]
    for reduce in (down, up, out, qkv):
        while reduce.at < len(reduce.phases):
            reduce.advance()


def run_c(a, b, small, wout, wqkv, info, qseg, dp_bits):
    ins = dict(
        gatt=(b.gatt, VM),
        att=(a.att, pl.ANY),
        gdn=(b.gdn, VM),
        gup=(b.gup, VM),
        sumsb=(b.sums, VM),
        tokf=(a.tokf, VM),
        h1=(a.h1, VM),
        q3=(a.q3, VM),
        k3=(a.k3, VM),
        v3=(a.v3, VM),
        lse=(a.lse, VM),
        qk=(a.qk, VM),
        cos=(a.cos, VM),
        sin=(a.sin, VM),
        info=(info, VM),
        qseg=(qseg, VM),
        wout=(wout, VM),
        wqkv=(wqkv, VM),
        smallf=(a.smallf, VM),
        small=(small, VM),
        share=(a.share, VM),
    )
    outs = dict(
        igrad=((ROWS, 192), F32, VM),
        resdn=((768, 768), BF16, VM),
        resup=((768, 768), BF16, VM),
        reswo=((192, 768), BF16, VM),
        resqkv=((768, 576), BF16, VM),
        sums=((16, 768), F32, VM),
    )
    phases = 2 * dp_bits
    scratch = dict(
        attown=pltpu.VMEM((ROWS, 192), BF16),
        accwo=pltpu.VMEM((192, 768), BF16),
        accqkv=pltpu.VMEM((768, 576), BF16),
        ardn=pltpu.VMEM((arrive_rows(768, dp_bits), 768), BF16),
        arup=pltpu.VMEM((arrive_rows(768, dp_bits), 768), BF16),
        arwo=pltpu.VMEM((arrive_rows(192, dp_bits), 768), BF16),
        arqkv=pltpu.VMEM((arrive_rows(768, dp_bits), 576), BF16),
        dk=pltpu.VMEM((3, ROWS, 64), F32),
        dv=pltpu.VMEM((3, ROWS, 64), F32),
        dq=pltpu.VMEM((ROWS, 192), BF16),
        gproj=pltpu.VMEM((ROWS, 576), BF16),
        work=pltpu.VMEM((PART, 768), F32),
        stat=pltpu.VMEM((ROWS, 128), F32),
        back=pltpu.VMEM((ROWS, 128), F32),
        strow=pltpu.VMEM((8, 1792), F32),
        stsum=pltpu.VMEM((8, 1792), F32),
        starr=pltpu.VMEM((2, 8, 1792), F32),
        sttot=pltpu.VMEM((128, 1792), F32),
        n1=pltpu.VMEM((ROWS, 192), F32),
        mown=pltpu.VMEM((2, ROWS, 192), F32),
        msend=pltpu.VMEM((2, ROWS, 192), BF16),
        mrecv=pltpu.VMEM((2, ROWS, 192), BF16),
        ysend=pltpu.VMEM((ROWS, 192), BF16),
        yrecv=pltpu.VMEM((ROWS, 192), BF16),
        sumx=pltpu.VMEM((dp_bits + 2, 16, 768), F32),
        sumr=pltpu.VMEM((dp_bits + 2, 16, 768), F32),
        load_sem=dma(),
        dn_send=dma(phases),
        dn_recv=dma(phases),
        up_send=dma(phases),
        up_recv=dma(phases),
        wo_send=dma(phases),
        wo_recv=dma(phases),
        qk_send=dma(phases),
        qk_recv=dma(phases),
        mc_send=dma(4),
        mc_recv=dma(4),
        my_send=dma(4),
        my_recv=dma(4),
        st_send=dma(2),
        st_recv=dma(2),
        su_send=dma(dp_bits + 2),
        su_recv=dma(dp_bits + 2),
    )
    return call_kernel(kernel_c, ins, outs, scratch, 3, 63, dp_bits)


def key_windows(key_segment):
    starts = []
    for tile in range(TILES):
        if tile % 3 == 0 and tile:
            starts.append(384 + 576 * (tile // 3 - 1))
        else:
            starts.append(576 * (tile // 3) - 32 * (tile // 6))
    padded = jnp.pad(key_segment, (0, WIDE), constant_values=-3.0)
    return jnp.broadcast_to(
        jnp.stack([padded[s : s + WIDE] for s in starts])[:, None, :], (TILES, 8, WIDE)
    )


norm_eps = 1e-06
root_half = 0.7071067811865476
inv_root_two_pi = 0.3989422804014327


def local(
    tokens,
    w_qkv,
    b_qkv,
    freqs,
    w_out,
    b_out,
    norm1_gain,
    norm1_bias,
    norm2_gain,
    norm2_bias,
    w_up,
    b_up,
    w_down,
    b_down,
    cotangent,
    keep_mask,
    coords,
    block_group,
):
    row_count, width_loc = tokens.shape
    heads_loc = freqs.shape[1]
    column = lax.axis_index("mp") * width_loc
    keep_float = keep_mask.astype(jnp.float32)
    group_now = block_group[0]
    kept_total = jnp.sum(keep_float)
    row_index = jnp.arange(row_count, dtype=jnp.int32)
    segment_size = jnp.where(group_now == 0, GRID_LO * GRID_LO, SLOTS).astype(jnp.int32)
    segment_ids = row_index // segment_size
    key_keep = keep_mask > 0
    segment_float = segment_ids.astype(jnp.float32)
    key_segment = jnp.where(key_keep, segment_float, -1.0)
    info = jnp.stack(
        [coords[0].astype(F32), coords[1].astype(F32), keep_float, key_segment, segment_float]
        + [keep_float] * 3,
        axis=1,
    )
    small = jnp.stack(
        [
            part.astype(F32)
            for part in (norm1_gain, norm1_bias, norm2_gain, norm2_bias, b_out, b_down, b_out, b_out)
        ]
    )
    wqkv_flat = w_qkv.reshape(w_qkv.shape[0], 3 * width_loc)
    bqkv_flat = jnp.broadcast_to(b_qkv.reshape(1, 3 * width_loc).astype(F32), (8, 3 * width_loc))
    half_freqs = jnp.concatenate([freqs, freqs], axis=2).reshape(2, width_loc)
    freq = jnp.pad(jnp.concatenate([half_freqs, half_freqs], axis=1), ((0, 6), (0, 0)))
    low = (group_now == 0).astype(F32)
    cnt = jnp.pad(
        jnp.broadcast_to(jnp.stack([kept_total * low, kept_total * (1.0 - low), low]), (8, 3)),
        ((0, 0), (0, 125)),
    )
    dp_bits = lax.axis_size("dp").bit_length() - 1
    a = run_a(tokens, small, wqkv_flat, bqkv_flat, freq, info, key_windows(key_segment), cnt, dp_bits)
    a.smallb = jnp.broadcast_to(a.smallf[5:6], (8, 768))
    bup = jnp.broadcast_to(b_up.astype(F32)[None], (8, b_up.shape[0]))
    b = run_b(a, cotangent, w_out, w_up, bup, w_down, info, dp_bits)
    qseg = jnp.broadcast_to(segment_float.reshape(TILES, 1, TILE), (TILES, 8, TILE))
    c = run_c(a, b, small, w_out, wqkv_flat, info, qseg, dp_bits)
    sums = c.sums

    def own(row):
        return lax.dynamic_slice_in_dim(row, column, width_loc, 0)

    turns = sums[1:3, :384].reshape(2, 2, heads_loc, 2, HEAD_DIM // 2)
    return (
        b.out,
        c.igrad,
        c.resqkv.astype(F32).reshape(w_qkv.shape),
        sums[0, : 3 * width_loc].reshape(3, width_loc),
        jnp.sum(turns, axis=(1, 3)),
        c.reswo.astype(F32),
        own(sums[3]),
        sums[4, :width_loc],
        sums[5, :width_loc],
        own(sums[9]),
        own(sums[10]),
        c.resup.astype(F32),
        sums[8],
        c.resdn.astype(F32),
        sums[11, :width_loc],
    )


def solution(mesh):
    return jax.shard_map(
        local,
        mesh=mesh,
        in_specs=(
            P("dp", "mp"),
            P(None, None, "mp"),
            P(None, "mp"),
            P(None, "mp", None),
            P("mp", None),
            P("mp"),
            P("mp"),
            P("mp"),
            P("mp"),
            P("mp"),
            P(None, "mp"),
            P("mp"),
            P("mp", None),
            P("mp"),
            P("dp", "mp"),
            P("dp"),
            P(None, "dp"),
            P("dp"),
        ),
        out_specs=(
            P("dp", "mp"),
            P("dp", "mp"),
            P(None, None, "mp"),
            P(None, "mp"),
            P(None, "mp", None),
            P("mp", None),
            P("mp"),
            P("mp"),
            P("mp"),
            P("mp"),
            P("mp"),
            P(None, "mp"),
            P("mp"),
            P("mp", None),
            P("mp"),
        ),
        check_vma=False,
    )
```

```python
import jax
import jax.numpy as jnp
from jax import lax
from jax.experimental import pallas as pl
from jax.experimental.pallas import tpu as pltpu
from jax.sharding import PartitionSpec as P

HEAD_DIM = 64
GRID_LO = 14
SLOTS = 576

MESH = pl.DeviceIdType.MESH
MIB = 1024 * 1024
VM = pltpu.VMEM
F32 = jnp.float32
BF16 = jnp.bfloat16
NT = (((1,), (1,)), ((), ()))
NN = (((1,), (0,)), ((), ()))

D = 768
OWN = 192
ROWS = 1728
LANES = 1792
CHUNK = 256
CHUNKS = LANES // CHUNK
TILE = 128
TILES = LANES // TILE
NARROW = 608

norm_eps = 1e-06
root_half = 0.7071067811865476
inv_root_two_pi = 0.3989422804014327


class Refs:
    pass


def dot(left, right, dims=NN):
    return lax.dot_general(left, right, dims, preferred_element_type=F32)


def remote(src, dst, send, recv, device):
    return pltpu.make_async_remote_copy(
        src_ref=src, dst_ref=dst, send_sem=send, recv_sem=recv, device_id=device, device_id_type=MESH
    )


def place():
    spot = Refs()
    spot.dp = lax.axis_index("dp")
    spot.mp = lax.axis_index("mp")
    spot.y = spot.mp // 2
    spot.c = spot.mp % 2
    spot.sib_mp = 2 * spot.y + 1 - spot.c
    spot.yp_mp = 2 * (1 - spot.y) + spot.c
    spot.sib = (spot.dp, spot.sib_mp)
    spot.yp = (spot.dp, spot.yp_mp)
    return spot


def greet(devices):
    barrier = pltpu.get_barrier_semaphore()
    for device in devices:
        pl.semaphore_signal(barrier, inc=1, device_id=device, device_id_type=MESH)
    pl.semaphore_wait(barrier, len(devices))


def dp_partner(spot, bit):
    mine = (spot.dp // (1 << bit)) % 2
    return (spot.dp + (1 - 2 * mine) * (1 << bit), spot.mp)


def feat(j):
    return pl.ds(pl.multiple_of(OWN * j, 16), OWN)


def lanes(c):
    return pl.ds(pl.multiple_of(c * CHUNK, CHUNK), CHUNK)


def tile_lanes(t):
    return pl.ds(pl.multiple_of(t * TILE, TILE), TILE)


class Reduce:
    def __init__(self, spot, acc, arrive, res, order, send, recv):
        self.spot, self.res, self.send, self.recv = spot, res, send, recv
        self.at = 0
        self.phases = []
        gathers = []
        rows, cols = acc.shape
        row, col = 0, 0
        source, own_row, own_col = acc, 0, 0
        for level, bit in enumerate(order):
            mine = (spot.dp // (1 << bit)) % 2
            keep, away, halved = (0, 0), (0, 0), True
            if (rows // 2) % 16 == 0:
                rows = rows // 2
                keep, away = (mine * rows, 0), ((1 - mine) * rows, 0)
            elif (cols // 2) % 128 == 0:
                cols = cols // 2
                keep, away = (0, mine * cols), (0, (1 - mine) * cols)
            else:
                halved = False
            own_row, own_col = own_row + keep[0], own_col + keep[1]
            shape = (rows, cols)
            self.phases.append((bit, source, away, keep, shape, arrive[level]))
            if halved:
                gathers.append((bit, res, (own_row, own_col), None, shape, res))
            source = arrive[level]
        self.own = (own_row, own_col)
        self.sums = len(self.phases)
        self.phases += gathers[::-1]

    def piece(self, ref, corner, shape):
        def span(start, size, unit, whole):
            if size == whole:
                return pl.ds(0, size)
            return pl.ds(pl.multiple_of(start, unit), size)

        return ref.at[
            span(corner[0], shape[0], 16, ref.shape[0]), span(corner[1], shape[1], 128, ref.shape[1])
        ]

    def copy(self):
        bit, source, away, keep, shape, target = self.phases[self.at]
        piece = self.piece(source, away, shape)
        goal = piece if keep is None else target
        return remote(
            piece, goal, self.send.at[self.at], self.recv.at[self.at], dp_partner(self.spot, bit)
        )

    def start(self):
        self.copy().start()

    def add(self):
        _, source, _, keep, shape, target = self.phases[self.at]
        held = self.piece(source, keep, shape)
        last = self.at == self.sums - 1
        goal = self.piece(self.res, self.own, shape) if last else target
        step = 48 if shape[0] % 48 == 0 else 16

        def block(i, carry):
            rows = pl.ds(pl.multiple_of(i * step, 16), step)
            goal[rows, :] = (held[rows, :].astype(F32) + target[rows, :].astype(F32)).astype(BF16)
            return carry

        lax.fori_loop(0, shape[0] // step, block, 0)

    def advance(self):
        if self.at >= len(self.phases):
            return
        self.copy().wait()
        if self.at < self.sums:
            self.add()
        self.at += 1
        if self.at < len(self.phases):
            self.start()


def arrive_shapes(rows, cols, dp_bits):
    shapes = []
    for _ in range(dp_bits):
        if (rows // 2) % 16 == 0:
            rows = rows // 2
        elif (cols // 2) % 128 == 0:
            cols = cols // 2
        shapes.append((rows, cols))
    return shapes


class Exchange:
    def __init__(self, r, spot, part, arrive, out, come, sems, stats=None):
        self.r, self.spot = r, spot
        self.part, self.arrive, self.out, self.come = part, arrive, out, come
        self.sems, self.stats = sems, stats

    def core(self, c):
        at = lanes(c)
        copies = [
            remote(
                self.part.at[:, 1 - self.spot.c, :, at],
                self.arrive.at[:, :, at],
                self.sems.at[0, c],
                self.sems.at[1, c],
                self.spot.sib,
            )
        ]
        if self.stats is not None:
            copies.append(
                remote(
                    self.stats.at[0, :, at],
                    self.stats.at[1, :, at],
                    self.sems.at[2, c],
                    self.sems.at[3, c],
                    self.spot.sib,
                )
            )
        return copies

    def over(self, c):
        at = lanes(c)
        copies = [
            remote(
                self.out.at[:, at],
                self.come.at[:, at],
                self.sems.at[4, c],
                self.sems.at[5, c],
                self.spot.yp,
            )
        ]
        if self.stats is not None:
            copies.append(
                remote(
                    self.stats.at[2, :, at],
                    self.stats.at[3, :, at],
                    self.sems.at[6, c],
                    self.sems.at[7, c],
                    self.spot.yp,
                )
            )
        return copies

    def give(self, c, values):
        at = lanes(c)
        for j in range(4):
            self.part[j // 2, j % 2, :, at] = values[OWN * j : OWN * j + OWN].astype(BF16)
        for copy in self.core(c):
            copy.start()

    def pass_on(self, c):
        at = lanes(c)
        for copy in self.core(c):
            copy.wait()
        away = 1 - self.spot.y
        self.out[:, at] = (
            self.part[away, self.spot.c, :, at].astype(F32) + self.arrive[away, :, at].astype(F32)
        ).astype(BF16)
        if self.stats is not None:
            self.stats[2, :, at] = self.stats[0, :, at] + self.stats[1, :, at]
        for copy in self.over(c):
            copy.start()

    def take(self, c):
        at = lanes(c)
        for copy in self.over(c):
            copy.wait()
        home = self.spot.y
        return (
            self.part[home, self.spot.c, :, at].astype(F32)
            + self.arrive[home, :, at].astype(F32)
            + self.come[:, at].astype(F32)
        )

    def take_stats(self, c):
        at = lanes(c)
        return (self.stats[2, :, at] + self.stats[3, :, at]) * (1.0 / D)


class Spread:
    def __init__(self, spot, full, sems):
        self.spot, self.full, self.sems = spot, full, sems

    def piece(self, j, c, kind, device):
        part = self.full.at[feat(j), lanes(c)]
        return remote(part, part, self.sems.at[2 * kind, c], self.sems.at[2 * kind + 1, c], device)

    def to_y(self, c):
        return self.piece(self.spot.mp, c, 0, self.spot.yp)

    def to_sib(self, c):
        return self.piece(self.spot.mp, c, 1, self.spot.sib)

    def onward(self, c):
        return self.piece(self.spot.yp_mp, c, 2, self.spot.sib)

    def send(self, c):
        self.to_y(c).start()
        self.to_sib(c).start()

    def relay(self, c):
        self.to_y(c).wait()
        self.onward(c).start()

    def arrived(self, c):
        self.to_sib(c).wait()
        self.onward(c).wait()


def sin_cos(angle):
    turns = jnp.floor(angle * 0.6366197723675814 + 0.5)
    rest = angle - turns * 1.5703125
    rest = rest - turns * 4.837512969970703e-4
    rest = rest - turns * 7.549789948768648e-8
    square = rest * rest
    sine = rest + rest * square * (
        -1.6666654611e-1 + square * (8.3321608736e-3 + square * -1.9515295891e-4)
    )
    cosine = (
        1.0
        - 0.5 * square
        + square
        * square
        * (4.166664568298827e-2 + square * (-1.388731625493765e-3 + square * 2.443315711809948e-5))
    )
    quarter = turns - 4.0 * jnp.floor(turns * 0.25)
    odd = (quarter == 1.0) | (quarter == 3.0)
    sine_sign = jnp.where(quarter >= 2.0, -1.0, 1.0)
    cosine_sign = jnp.where((quarter == 1.0) | (quarter == 2.0), -1.0, 1.0)
    return (
        jnp.where(odd, cosine, sine) * sine_sign,
        jnp.where(odd, sine, cosine) * cosine_sign,
    )


def phi_parts(value):
    scaled = jnp.clip(value * root_half, -3.832506856900711, 3.832506856900711)
    square = scaled * scaled
    top = 0.00022905065861350646
    for factor in (
        0.0034082910107109506,
        0.050955695062380861,
        0.18520832239976145,
        1.128379143519084,
    ):
        top = top * square + factor
    low = -1.1791602954361697e-7
    for factor in (
        0.000023547966471313185,
        0.0010179625278914885,
        0.014070470171167667,
        0.11098505178285362,
        0.49746925110067538,
        1.0,
    ):
        low = low * square + factor
    error = scaled * top / low
    return (0.5 + 0.5 * error, inv_root_two_pi * jnp.exp(-0.5 * value * value))


def normalize(values):
    mean = jnp.mean(values, axis=0, keepdims=True)
    square = jnp.mean(values * values, axis=0, keepdims=True)
    inverse = lax.rsqrt(square - mean * mean + norm_eps)
    return ((values - mean) * inverse, mean, inverse)


def turn_by(values, cosine, sine):
    out = []
    for h in range(3):
        front, rear = values[64 * h : 64 * h + 32], values[64 * h + 32 : 64 * h + 64]
        co, si = cosine[32 * h : 32 * h + 32], sine[32 * h : 32 * h + 32]
        out += [front * co - rear * si, front * si + rear * co]
    return jnp.concatenate(out, axis=0)


def block_diagonal(tile):
    zero = jnp.zeros((64, TILE), tile.dtype)
    parts = []
    for h in range(3):
        column = [zero, zero, zero]
        column[h] = tile[64 * h : 64 * h + 64]
        parts.append(jnp.concatenate(column, axis=0))
    return jnp.concatenate(parts, axis=1)


def from_diagonal(values, heads):
    return jnp.concatenate(
        [values[64 * h : 64 * h + 64, TILE * n : TILE * n + TILE] for n, h in enumerate(heads)], axis=0
    )


def fold(values):
    return values[:, :128] + values[:, 128:]


def angle_tables(r):
    def block(c, carry):
        at = lanes(c)
        angle = r.cols[0:96, 2:3] * r.info[0:1, at] + r.cols[0:96, 3:4] * r.info[1:2, at]
        sine, cosine = sin_cos(angle)
        r.cos[:, at] = cosine
        r.sin[:, at] = sine
        return carry

    lax.fori_loop(0, CHUNKS, block, 0)

    def column(t, carry):
        row = r.info[3:4, tile_lanes(t)]
        r.kcol[pl.ds(pl.multiple_of(t * TILE, TILE), TILE), :] = jnp.transpose(
            jnp.broadcast_to(row, (TILE, TILE))
        )
        return carry

    lax.fori_loop(0, TILES, column, 0)


def flip(source, goal):
    for i in range(source.shape[1] // 128):
        part = source[:, 128 * i : 128 * i + 128].astype(F32)
        goal[128 * i : 128 * i + 128, 0 : source.shape[0]] = jnp.transpose(part).astype(BF16)


def project(r, c):
    at = lanes(c)
    normed, _, _ = normalize(r.x[:, at].astype(F32))
    h1 = (normed * r.small[:, 4:5] + r.small[:, 5:6]).astype(BF16)
    r.h1[:, at] = h1
    projected = dot(r.wqkv[...], h1) + r.cols[0:576, 1:2]
    cosine, sine = r.cos[:, at], r.sin[:, at]
    query = turn_by(projected[0:192], cosine, sine)
    key = turn_by(projected[192:384], cosine, sine)
    value = projected[384:576]
    r.qk[0:192, at] = query.astype(BF16)
    r.qk[192:384, at] = key.astype(BF16)
    r.v[:, at] = value.astype(BF16)
    r.kn[at, :] = jnp.transpose(key).astype(BF16)
    r.vn[at, :] = jnp.transpose(value).astype(BF16)


def tile_mask(r, tile, start, width):
    window = pl.ds(pl.multiple_of(start, 16), width)
    allowed = r.kcol[window, :] == r.info[4:5, tile_lanes(tile)]
    return jnp.where(allowed, 0.0, -1e30)


def repeat(mask, values):
    return jnp.concatenate([mask] * (values.shape[1] // TILE), axis=1)


def head_groups(width):
    return [(0, 1, 2)] if width <= NARROW else [(0,), (1,), (2,)]


def attend_tile(r, spot, tile, start, width, values):
    window = pl.ds(pl.multiple_of(start, 16), width)
    at = tile_lanes(tile)
    queries = block_diagonal(r.qk[0:192, at] * BF16(0.125))
    mask = tile_mask(r, tile, start, width)
    for heads in head_groups(width):
        span = slice(TILE * heads[0], TILE * heads[-1] + TILE)
        scores = dot(r.kn[window, :], queries[:, span])
        scores = scores + repeat(mask, scores)
        top = jnp.max(scores, axis=0, keepdims=True)
        exponent = jnp.exp(scores - top)
        total = jnp.sum(exponent, axis=0, keepdims=True)
        probs = (exponent * (1.0 / total)).astype(BF16)
        out = from_diagonal(dot(values, probs), heads).astype(BF16)
        r.att[head_rows(spot, heads), at] = out
        r.lse[tile, :, span] = jnp.broadcast_to(top + jnp.log(total), (8, span.stop - span.start))


def head_rows(spot, heads):
    return pl.ds(pl.multiple_of(OWN * spot.mp + 64 * heads[0], 16), 64 * len(heads))


def back_tile(r, spot, tile, start, width, keys):
    window = pl.ds(pl.multiple_of(start, 16), width)
    at = tile_lanes(tile)
    queries = block_diagonal(r.qk[0:192, at] * BF16(0.125))
    grads = block_diagonal(dot(r.wout[...], r.gatt[:, at]).astype(BF16))
    mask = tile_mask(r, tile, start, width)
    for heads in head_groups(width):
        span = slice(TILE * heads[0], TILE * heads[-1] + TILE)
        query, grad = queries[:, span], grads[:, span]
        scores = dot(r.kn[window, :], query)
        probs = jnp.exp(scores + repeat(mask, scores) - r.lse[tile, 0:1, span])
        g_probs = dot(r.vn[window, :], grad)
        center = jnp.sum(probs * g_probs, axis=0, keepdims=True)
        g_scores = (probs * (g_probs - center)).astype(BF16)
        r.dv[window, :] += dot(probs.astype(BF16), grad, NT)
        r.dk[window, :] += dot(g_scores, query, NT)
        rows = slice(64 * heads[0], 64 * heads[-1] + 64)
        r.dq[rows, at] = (from_diagonal(dot(keys, g_scores), heads) * 0.125).astype(BF16)


def mlp_part(r, spot, c, outward, sums):
    at = lanes(c)
    mid = r.x[:, at].astype(F32) + (dot(r.wot[...], r.att[:, at]) + r.small[:, 8:9])
    normed, mean, inverse = normalize(mid)
    r.work[...] = mid
    r.mido[:, at] = r.work[feat(spot.mp), :]
    r.rows2[0:1, at] = mean
    r.rows2[1:2, at] = inverse
    h2 = (normed * r.small[:, 6:7] + r.small[:, 7:8]).astype(BF16)
    r.h2[:, at] = h2
    hidden = dot(r.wupt[...], h2) + r.cols[:, 0:1]
    lower, density = phi_parts(hidden)
    active = (hidden * lower).astype(BF16)
    r.act[:, at] = active
    slope = lower + hidden * density
    outward.give(c, dot(r.wdnt[...], active))
    g_pre = (dot(r.wdn[...], r.gout[:, at]) * slope).astype(BF16)
    r.gpre[:, at] = g_pre
    r.sbup[...] += fold(g_pre.astype(F32))
    g_h2 = dot(r.wup[...], g_pre)
    scaled = g_h2 * r.small[:, 6:7]
    r.stats[0, 0:1, at] = jnp.sum(scaled, axis=0, keepdims=True)
    r.stats[0, 1:2, at] = jnp.sum(scaled * normed, axis=0, keepdims=True)
    sums.give(c, g_h2)


def second_norm_back(r, spot, c, sums):
    at = lanes(c)
    grad = sums.take(c)
    means = sums.take_stats(c)
    normed = (r.mido[:, at] - r.rows2[0:1, at]) * r.rows2[1:2, at]
    r.sg2[...] += fold(grad * normed)
    r.sb2[...] += fold(grad)
    back = r.rows2[1:2, at] * (
        grad * r.cols[0:192, 6:7] - means[0:1, :] - normed * means[1:2, :]
    )
    g_att = (r.gout[feat(spot.mp), at].astype(F32) + back).astype(BF16)
    r.gatt[feat(spot.mp), at] = g_att
    r.sbo[...] += fold(g_att.astype(F32))


def unrotate(r, c):
    at = lanes(c)
    cosine, sine = r.cos[:, at], r.sin[:, at]
    g_query = r.dq[0:192, at].astype(F32)
    g_key = jnp.transpose(r.dk[at, :]).astype(BF16).astype(F32)
    g_value = jnp.transpose(r.dv[at, :]).astype(BF16)
    plain = [turn_by(g, cosine, -sine).astype(BF16) for g in (g_query, g_key)]
    r.gproj[0:576, at] = jnp.concatenate(plain + [g_value], axis=0)
    angle = []
    for h in range(3):
        total = 0.0
        for part, g in enumerate((g_query, g_key)):
            rotated = r.qk[192 * part : 192 * part + 192, at].astype(F32)
            a, b = slice(64 * h, 64 * h + 32), slice(64 * h + 32, 64 * h + 64)
            total = total + (g[b] * rotated[a] - g[a] * rotated[b])
        angle.append(total)
    angle = jnp.concatenate(angle, axis=0)
    r.sf0[...] += fold(angle * r.info[0:1, at])
    r.sf1[...] += fold(angle * r.info[1:2, at])


def first_part(r, spot, c, sums):
    at = lanes(c)
    g_h1 = dot(r.wqkvn[:, 0:576], r.gproj[0:576, at])
    normed, mean, inverse = normalize(r.x[:, at].astype(F32))
    r.rows2[0:1, at] = mean
    r.rows2[1:2, at] = inverse
    scaled = g_h1 * r.small[:, 4:5]
    r.stats[0, 0:1, at] = jnp.sum(scaled, axis=0, keepdims=True)
    r.stats[0, 1:2, at] = jnp.sum(scaled * normed, axis=0, keepdims=True)
    sums.give(c, g_h1)


def first_norm_back(r, spot, c, sums):
    at = lanes(c)
    grad = sums.take(c)
    means = sums.take_stats(c)
    own = feat(spot.mp)
    normed = (r.x[own, at].astype(F32) - r.rows2[0:1, at]) * r.rows2[1:2, at]
    r.sg1[...] += fold(grad * normed)
    r.sb1[...] += fold(grad)
    back = r.rows2[1:2, at] * (
        grad * r.cols[0:192, 4:5] - means[0:1, :] - normed * means[1:2, :]
    )
    r.mido[:, at] = r.gatt[own, at].astype(F32) + back


def kernel(r, spot):
    peers = [dp_partner(spot, bit) for bit in range(r.dp_bits)]
    token_load = pltpu.make_async_copy(r.tok, r.out, r.load_sem.at[4])
    token_load.start()
    loads = Refs()
    for n, (name, source) in enumerate(
        dict(wqkv=r.in_wqkv, wup=r.in_wup, wdn=r.in_wdn, wout=r.in_wout).items()
    ):
        setattr(loads, name, pltpu.make_async_copy(source, getattr(r, name), r.load_sem.at[n]))
        getattr(loads, name).start()
    greet([spot.sib, spot.yp] + peers)
    own = feat(spot.mp)
    r.x[own, ROWS - 64 : LANES] = jnp.zeros((OWN, 128), BF16)
    token_load.wait()
    r.x[own, 0:ROWS] = r.out[...]
    pltpu.make_async_copy(r.cot, r.out, r.load_sem.at[5]).start()
    tokens = Spread(spot, r.x, r.tk_sem)
    for c in range(CHUNKS):
        tokens.send(c)
    r.small[own, :] = r.cols[0:192, :]
    small_y = remote(r.cols.at[0:192], r.small.at[own], r.sm_sem.at[0], r.sm_sem.at[1], spot.yp)
    small_c = remote(r.cols.at[0:192], r.small.at[own], r.sm_sem.at[2], r.sm_sem.at[3], spot.sib)
    there = r.small.at[feat(spot.yp_mp)]
    small_f = remote(there, there, r.sm_sem.at[4], r.sm_sem.at[5], spot.sib)
    small_y.start()
    small_c.start()

    def count_copy(bit):
        return remote(r.cnts.at[bit], r.cntr.at[bit], r.cn_sem.at[0, bit], r.cn_sem.at[1, bit], peers[bit])

    r.cnts[0] = r.cnt[...]
    count_copy(0).start()
    angle_tables(r)
    small_y.wait()
    small_f.start()
    for ref in (r.sbup, r.sg1, r.sb1, r.sg2, r.sb2, r.sbo, r.sf0, r.sf1, r.dk, r.dv):
        ref[...] = jnp.zeros_like(ref)
    loads.wup.wait()
    flip(r.wup, r.wupt)
    small_c.wait()
    small_f.wait()
    loads.wdn.wait()
    flip(r.wdn, r.wdnt)
    for bit in range(r.dp_bits):
        count_copy(bit).wait()
        total = r.cnts[bit] + r.cntr[bit]
        if bit + 1 < r.dp_bits:
            r.cnts[bit + 1] = total
            count_copy(bit + 1).start()
    low, high = total[:, 0:1], total[:, 1:2]
    share = jnp.where(r.cnt[:, 2:3] > 0.5, low, high) / (low + high)
    r.share[...] = jnp.broadcast_to(share, (8, 128))
    loads.wqkv.wait()
    loads.wout.wait()

    tokens.relay(0)

    def project_chunk(c, carry):
        @pl.when(c + 1 < CHUNKS)
        def _():
            tokens.relay(c + 1)

        tokens.arrived(c)
        project(r, c)
        return carry

    lax.fori_loop(0, CHUNKS, project_chunk, 0)

    wo_here = r.wof.at[own]
    wo_there = r.wof.at[feat(spot.yp_mp)]
    wo_y = remote(r.wout, wo_here, r.wo_sem.at[0], r.wo_sem.at[1], spot.yp)
    wo_c = remote(r.wout, wo_here, r.wo_sem.at[2], r.wo_sem.at[3], spot.sib)
    wo_f = remote(wo_there, wo_there, r.wo_sem.at[4], r.wo_sem.at[5], spot.sib)
    wo_y.start()
    wo_c.start()
    r.wof[own, :] = r.wout[...]
    r.gout[own, ROWS - 64 : LANES] = jnp.zeros((OWN, 128), BF16)
    keep = r.info[2:3, 0:ROWS]
    pltpu.make_async_copy(r.cot, r.out, r.load_sem.at[5]).wait()
    r.gout[own, 0:ROWS] = (r.out[...].astype(F32) * keep).astype(BF16)
    attended = Spread(spot, r.att, r.at_sem)
    cotangents = Spread(spot, r.gout, r.ct_sem)

    def after_tile(t):
        @pl.when(t % 2 == 1)
        def _():
            attended.send(t // 2)
            cotangents.send(t // 2)

            @pl.when(t >= 5)
            def _():
                attended.relay(t // 2 - 2)
                cotangents.relay(t // 2 - 2)

    for j in range(3):
        start = 576 * j - 32 * (j // 2)
        r.win[:, 0:NARROW] = r.v[:, start : start + NARROW]

        def attend(i, carry):
            attend_tile(r, spot, 5 * j + i, start, NARROW, r.win[:, 0:NARROW])
            after_tile(5 * j + i)
            return carry

        lax.fori_loop(0, 4, attend, 0)
        if j == 0:
            attend_tile(r, spot, 4, 0, 1152, r.v[:, 0:1152])
            after_tile(4)
        if j == 1:
            attend_tile(r, spot, 9, 976, 752, r.v[:, 976:1728])
            after_tile(9)
    wo_y.wait()
    wo_f.start()
    wo_c.wait()
    wo_f.wait()
    flip(r.wof, r.wot)
    r.atto[...] = r.att[own, :]

    outward = Exchange(r, spot, r.mp, r.mr, r.ms, r.mc, r.mo_sem)
    second = Exchange(r, spot, r.gp, r.gr, r.gs, r.gc, r.g2_sem, r.stats)
    g_att = Spread(spot, r.gatt, r.ga_sem)
    order = list(range(r.dp_bits))
    turned = order[1:] + order[:1]
    down = Reduce(spot, r.accdn, r.ardn, r.resdn, order, r.dn_sem.at[0], r.dn_sem.at[1])
    up = Reduce(spot, r.accup, r.arup, r.resup, turned, r.up_sem.at[0], r.up_sem.at[1])
    out = Reduce(spot, r.accwo, r.arwo, r.reswo, order, r.wr_sem.at[0], r.wr_sem.at[1])
    share = r.share[0:1, 0:1]

    def mlp_step(n, carry):
        @pl.when(n < CHUNKS)
        def _():
            @pl.when(n >= CHUNKS - 2)
            def _():
                attended.relay(n)
                cotangents.relay(n)

            attended.arrived(n)
            cotangents.arrived(n)
            mlp_part(r, spot, n, outward, second)

        @pl.when(n == CHUNKS)
        def _():
            r.accdn[...] = (dot(r.act[...], r.gout[...], NT) * r.share[0:1, 0:1]).astype(BF16)
            down.start()

        @pl.when(n == CHUNKS + 1)
        def _():
            r.accup[...] = (dot(r.h2[...], r.gpre[...], NT) * r.share[0:1, 0:1]).astype(BF16)
            up.start()

        @pl.when((n >= 1) & (n <= CHUNKS))
        def _():
            second.pass_on(n - 1)

        @pl.when((n >= 3) & (n <= CHUNKS + 2))
        def _():
            second_norm_back(r, spot, n - 3, second)
            g_att.send(n - 3)

        @pl.when(n >= 4)
        def _():
            g_att.relay(n - 4)

        return carry

    lax.fori_loop(0, CHUNKS + 4, mlp_step, 0)

    for c in range(CHUNKS):
        outward.pass_on(c)

    def before_tile(t):
        @pl.when(t % 2 == 0)
        def _():
            g_att.arrived(t // 2)

    for j in range(3):
        start = 576 * j - 32 * (j // 2)
        r.win[:, 0:NARROW] = r.qk[192:384, start : start + NARROW]

        def back(i, carry):
            before_tile(5 * j + i)
            back_tile(r, spot, 5 * j + i, start, NARROW, r.win[:, 0:NARROW])
            return carry

        lax.fori_loop(0, 4, back, 0)
        if j == 0:
            before_tile(4)
            back_tile(r, spot, 4, 0, 1152, r.qk[192:384, 0:1152])
        if j == 1:
            back_tile(r, spot, 9, 976, 752, r.qk[192:384, 976:1728])
        down.advance()
        up.advance()
        if j == 1:
            finish_out(r, spot, outward)
            down.advance()
    r.accwo[...] = (dot(r.atto[...], r.gatt[...], NT) * r.share[0:1, 0:1]).astype(BF16)
    out.start()
    lax.fori_loop(0, CHUNKS, lambda c, carry: (unrotate(r, c), carry)[1], 0)
    down.advance()
    up.advance()
    r.accqk[...] = (dot(r.gproj[0:384, :], r.h1[...], NT) * r.share[0:1, 0:1]).astype(BF16)
    r.accv[...] = (dot(r.gproj[384:576, :], r.h1[...], NT) * r.share[0:1, 0:1]).astype(BF16)
    pair = Reduce(spot, r.accqk, r.arqk, r.resqk, order, r.qr_sem.at[0], r.qr_sem.at[1])
    value = Reduce(spot, r.accv, r.arv, r.resv, turned, r.vr_sem.at[0], r.vr_sem.at[1])
    pair.start()
    value.start()
    out.advance()
    flip(r.wqkv, r.wqkvn)
    first = Exchange(r, spot, r.gp, r.gr, r.gs, r.gc, r.g1_sem, r.stats)

    def last_step(n, carry):
        @pl.when(n < CHUNKS)
        def _():
            first_part(r, spot, n, first)

        @pl.when((n >= 1) & (n <= CHUNKS))
        def _():
            first.pass_on(n - 1)

        @pl.when(n >= 3)
        def _():
            first_norm_back(r, spot, n - 3, first)

        @pl.when(n == 3)
        def _():
            pair.advance()
            value.advance()
            out.advance()

        @pl.when(n == 5)
        def _():
            down.advance()
            up.advance()

        @pl.when(n == 7)
        def _():
            pair.advance()
            value.advance()
            out.advance()

        return carry

    lax.fori_loop(0, CHUNKS + 3, last_step, 0)

    def total(ref):
        return jnp.sum(ref[...], axis=1, keepdims=True)

    b_down = jnp.sum(r.gout[own, :].astype(F32), axis=1, keepdims=True)
    b_qkv = jnp.sum(r.gproj[0:576, :].astype(F32), axis=1, keepdims=True)
    columns = [
        total(r.sbup),
        jnp.concatenate([b_qkv, total(r.sf0), total(r.sf1)], axis=0),
        jnp.concatenate([total(r.sbo), total(r.sg1), total(r.sb1), total(r.sg2)], axis=0),
        jnp.concatenate([total(r.sb2), b_down, jnp.zeros((384, 1), F32)], axis=0),
    ]
    lane = lax.broadcasted_iota(jnp.int32, (D, 128), 1)
    table = jnp.zeros((D, 128), F32)
    for n, column in enumerate(columns):
        table = jnp.where(lane == n, column, table)
    table = jnp.transpose(table * r.share[0:1, 0:1])[0:8, :]
    for bit in range(r.dp_bits):
        r.sumx[bit] = table
        copy = remote(
            r.sumx.at[bit], r.sumr.at[bit], r.su_sem.at[0, bit], r.su_sem.at[1, bit], peers[bit]
        )
        copy.start()
        pair.advance()
        value.advance()
        out.advance()
        copy.wait()
        table = table + r.sumr[bit]
    r.sums[...] = table
    reduces = (pair, value, out, down, up)
    while any(reduce.at < len(reduce.phases) for reduce in reduces):
        for reduce in reduces:
            reduce.advance()


def finish_out(r, spot, outward):
    for c in range(CHUNKS):
        at = lanes(c)
        total = outward.take(c)
        whole = r.mido[:, at] + (total + r.cols[0:192, 9:10])
        r.gs[:, at] = (r.info[2:3, at] * whole).astype(BF16)
    r.out[...] = r.gs[:, 0:ROWS]


def dma(*shape):
    return pltpu.SemaphoreType.DMA(shape)


def run(dp_bits, **arrays):
    on_demand = ("tok", "cot", "in_wqkv", "in_wup", "in_wdn", "in_wout")
    outs = dict(
        out=((OWN, ROWS), BF16),
        igrad=((OWN, LANES), F32),
        resdn=((D, D), BF16),
        resup=((D, D), BF16),
        reswo=((OWN, D), BF16),
        resqk=((384, D), BF16),
        resv=((OWN, D), BF16),
        sums=((8, D), F32),
    )

    def levels(rows):
        return [VM(shape, BF16) for shape in arrive_shapes(rows, D, dp_bits)]

    full = VM((D, LANES), BF16)
    own = VM((OWN, LANES), BF16)
    square = VM((D, D), BF16)
    spread = dma(6, CHUNKS)
    reduce = dma(2, 2 * dp_bits)
    scratch = dict(
        x=full,
        h1=full,
        qk=VM((384, LANES), BF16),
        v=own,
        kn=VM((LANES, OWN), BF16),
        vn=VM((LANES, OWN), BF16),
        cos=VM((96, LANES), F32),
        sin=VM((96, LANES), F32),
        kcol=VM((LANES, TILE), F32),
        win=VM((OWN, 640), BF16),
        lse=VM((TILES, 8, 384), F32),
        small=VM((D, 128), F32),
        share=VM((8, 128), F32),
        att=full,
        gout=full,
        wqkv=VM((576, D), BF16),
        wup=square,
        wupt=square,
        wdn=square,
        wdnt=square,
        wout=VM((OWN, D), BF16),
        wof=square,
        wot=square,
        h2=full,
        act=full,
        gpre=full,
        work=VM((D, CHUNK), F32),
        rows2=VM((8, LANES), F32),
        stats=VM((4, 8, LANES), F32),
        mp=VM((2, 2, OWN, LANES), BF16),
        mr=VM((2, OWN, LANES), BF16),
        gp=VM((2, 2, OWN, LANES), BF16),
        gr=VM((2, OWN, LANES), BF16),
        gs=own,
        gc=own,
        dk=VM((LANES, OWN), F32),
        dv=VM((LANES, OWN), F32),
        ardn=levels(D),
        arup=levels(D),
        arwo=levels(OWN),
        arqk=levels(384),
        arv=levels(OWN),
        sbup=VM((D, 128), F32),
        sg1=VM((OWN, 128), F32),
        sb1=VM((OWN, 128), F32),
        sg2=VM((OWN, 128), F32),
        sb2=VM((OWN, 128), F32),
        sbo=VM((OWN, 128), F32),
        sf0=VM((96, 128), F32),
        sf1=VM((96, 128), F32),
        cnts=VM((dp_bits, 8, 128), F32),
        cntr=VM((dp_bits, 8, 128), F32),
        sumx=VM((dp_bits, 8, D), F32),
        sumr=VM((dp_bits, 8, D), F32),
        load_sem=dma(6),
        tk_sem=spread,
        at_sem=spread,
        ct_sem=spread,
        ga_sem=spread,
        sm_sem=dma(6),
        wo_sem=dma(6),
        cn_sem=dma(2, dp_bits),
        su_sem=dma(2, dp_bits),
        mo_sem=dma(8, CHUNKS),
        g2_sem=dma(8, CHUNKS),
        g1_sem=dma(8, CHUNKS),
        dn_sem=reduce,
        up_sem=reduce,
        wr_sem=reduce,
        qr_sem=reduce,
        vr_sem=reduce,
    )
    shapes, structure = jax.tree.flatten(scratch, is_leaf=lambda leaf: not isinstance(leaf, (dict, list)))

    def body(*refs):
        r = Refs()
        for name, ref in zip(list(arrays) + list(outs), refs):
            setattr(r, name, ref)
        named = jax.tree.unflatten(structure, refs[len(arrays) + len(outs) :])
        for name, ref in named.items():
            setattr(r, name, ref)
        r.mido, r.gatt, r.atto = r.igrad, r.att, r.v
        r.dq, r.gproj, r.ms = r.act, r.h2, r.act.at[OWN : 2 * OWN]
        r.mc = r.act.at[2 * OWN : 3 * OWN]
        r.accdn, r.accup, r.accwo = r.wof, r.wupt, r.wdn.at[0:OWN]
        r.wqkvn = r.wot
        r.accqk, r.accv = r.wdnt.at[0:384], r.wdnt.at[384:576]
        r.dp_bits = dp_bits
        kernel(r, place())

    results = pl.pallas_call(
        body,
        out_shape=[jax.ShapeDtypeStruct(shape, dtype) for shape, dtype in outs.values()],
        in_specs=[
            pl.BlockSpec(memory_space=pl.ANY if name in on_demand else VM) for name in arrays
        ],
        out_specs=[pl.BlockSpec(memory_space=VM) for _ in outs],
        scratch_shapes=shapes,
        compiler_params=pltpu.CompilerParams(
            collective_id=1, has_side_effects=True, vmem_limit_bytes=64 * MIB - 65536
        ),
    )(*arrays.values())
    named = Refs()
    for name, result in zip(outs, results, strict=True):
        setattr(named, name, result)
    return named


def local(
    tokens,
    w_qkv,
    b_qkv,
    freqs,
    w_out,
    b_out,
    norm1_gain,
    norm1_bias,
    norm2_gain,
    norm2_bias,
    w_up,
    b_up,
    w_down,
    b_down,
    cotangent,
    keep_mask,
    coords,
    block_group,
):
    row_count, width_loc = tokens.shape
    heads_loc = freqs.shape[1]
    keep = keep_mask.astype(F32)
    group_now = block_group[0]
    low = (group_now == 0).astype(F32)
    kept_total = jnp.sum(keep)
    segment_size = jnp.where(group_now == 0, GRID_LO * GRID_LO, SLOTS).astype(jnp.int32)
    segment = (jnp.arange(row_count, dtype=jnp.int32) // segment_size).astype(F32)
    key_segment = jnp.where(keep_mask > 0, segment, -1.0)
    info = jnp.stack(
        [coords[0].astype(F32), coords[1].astype(F32), keep, key_segment, segment] + [keep] * 3
    )
    info = jnp.pad(info, ((0, 0), (0, LANES - row_count)))
    small = jnp.stack(
        [part.astype(F32) for part in (norm1_gain, norm1_bias, norm2_gain, norm2_bias, b_out, b_down)],
        axis=1,
    )
    cols = jnp.concatenate(
        [
            b_up.astype(F32)[:, None],
            jnp.pad(b_qkv.reshape(-1, 1).astype(F32), ((0, D - 3 * width_loc), (0, 0))),
            jnp.pad(freqs.reshape(2, 96).T, ((0, D - 96), (0, 0))),
            jnp.pad(small, ((0, D - width_loc), (0, 0))),
        ],
        axis=1,
    )
    counts = jnp.stack([kept_total * low, kept_total * (1.0 - low), low])

    def wide(array):
        return jnp.pad(array, ((0, 0), (0, 128 - array.shape[1])))

    a = run(
        lax.axis_size("dp").bit_length() - 1,
        tok=tokens.T,
        cot=cotangent.T,
        cols=wide(cols),
        info=info,
        cnt=wide(jnp.broadcast_to(counts, (8, 3))),
        in_wqkv=w_qkv.transpose(1, 2, 0).reshape(3 * width_loc, D),
        in_wup=w_up,
        in_wdn=w_down,
        in_wout=w_out,
    )
    sums = a.sums
    grad_qkv = jnp.concatenate([a.resqk, a.resv], axis=0).astype(F32)
    half = (2, heads_loc, HEAD_DIM // 2)
    return (
        a.out.T,
        a.igrad[:, :row_count].T,
        grad_qkv.reshape(3, width_loc, D).transpose(2, 0, 1),
        sums[1, : 3 * width_loc].reshape(3, width_loc),
        sums[1, 3 * width_loc :].reshape(half),
        a.reswo.astype(F32),
        sums[2, 0:192],
        sums[2, 192:384],
        sums[2, 384:576],
        sums[2, 576:768],
        sums[3, 0:192],
        a.resup.astype(F32),
        sums[0],
        a.resdn.astype(F32),
        sums[3, 192:384],
    )


def solution(mesh):
    return jax.shard_map(
        local,
        mesh=mesh,
        in_specs=(
            P("dp", "mp"),
            P(None, None, "mp"),
            P(None, "mp"),
            P(None, "mp", None),
            P("mp", None),
            P("mp"),
            P("mp"),
            P("mp"),
            P("mp"),
            P("mp"),
            P(None, "mp"),
            P("mp"),
            P("mp", None),
            P("mp"),
            P("dp", "mp"),
            P("dp"),
            P(None, "dp"),
            P("dp"),
        ),
        out_specs=(
            P("dp", "mp"),
            P("dp", "mp"),
            P(None, None, "mp"),
            P(None, "mp"),
            P(None, "mp", None),
            P("mp", None),
            P("mp"),
            P("mp"),
            P("mp"),
            P("mp"),
            P("mp"),
            P(None, "mp"),
            P("mp"),
            P("mp", None),
            P("mp"),
        ),
        check_vma=False,
    )
```

```python
import jax
import jax.numpy as jnp
from jax import lax
from jax.experimental import pallas as pl
from jax.experimental.pallas import tpu as pltpu
from jax.sharding import PartitionSpec as P

HEAD_DIM = 64
GRID_LO = 14
SLOTS = 576

MESH = pl.DeviceIdType.MESH
MIB = 1024 * 1024
VM = pltpu.VMEM
F32 = jnp.float32
BF16 = jnp.bfloat16
NT = (((1,), (1,)), ((), ()))
NN = (((1,), (0,)), ((), ()))

D = 768
OWN = 192
ROWS = 1728
LANES = 1792
CHUNK = 256
CHUNKS = LANES // CHUNK
TILE = 128
TILES = LANES // TILE
NARROW = 608

norm_eps = 1e-06
root_half = 0.7071067811865476
inv_root_two_pi = 0.3989422804014327


class Refs:
    pass


def dot(left, right, dims=NN):
    return lax.dot_general(left, right, dims, preferred_element_type=F32)


def remote(src, dst, send, recv, device):
    return pltpu.make_async_remote_copy(
        src_ref=src, dst_ref=dst, send_sem=send, recv_sem=recv, device_id=device, device_id_type=MESH
    )


def place():
    spot = Refs()
    spot.dp = lax.axis_index("dp")
    spot.mp = lax.axis_index("mp")
    spot.y = spot.mp // 2
    spot.c = spot.mp % 2
    spot.sib_mp = 2 * spot.y + 1 - spot.c
    spot.yp_mp = 2 * (1 - spot.y) + spot.c
    spot.sib = (spot.dp, spot.sib_mp)
    spot.yp = (spot.dp, spot.yp_mp)
    return spot


def greet(devices):
    barrier = pltpu.get_barrier_semaphore()
    for device in devices:
        pl.semaphore_signal(barrier, inc=1, device_id=device, device_id_type=MESH)
    pl.semaphore_wait(barrier, len(devices))


def dp_partner(spot, bit):
    mine = (spot.dp // (1 << bit)) % 2
    return (spot.dp + (1 - 2 * mine) * (1 << bit), spot.mp)


def feat(j):
    return pl.ds(pl.multiple_of(OWN * j, 16), OWN)


def lanes(c):
    return pl.ds(pl.multiple_of(c * CHUNK, CHUNK), CHUNK)


def tile_lanes(t):
    return pl.ds(pl.multiple_of(t * TILE, TILE), TILE)


class Reduce:
    def __init__(self, spot, acc, arrive, res, order, sems):
        self.spot, self.res, self.send, self.recv = spot, res, sems.at[0], sems.at[1]
        self.at = 0
        self.phases = []
        gathers = []
        rows, cols = acc.shape
        row, col = 0, 0
        source, own_row, own_col = acc, 0, 0
        for level, bit in enumerate(order):
            mine = (spot.dp // (1 << bit)) % 2
            keep, away, halved = (0, 0), (0, 0), True
            if (rows // 2) % 16 == 0:
                rows = rows // 2
                keep, away = (mine * rows, 0), ((1 - mine) * rows, 0)
            elif (cols // 2) % 128 == 0:
                cols = cols // 2
                keep, away = (0, mine * cols), (0, (1 - mine) * cols)
            else:
                halved = False
            own_row, own_col = own_row + keep[0], own_col + keep[1]
            shape = (rows, cols)
            self.phases.append((bit, source, away, keep, shape, arrive[level]))
            if halved:
                gathers.append((bit, res, (own_row, own_col), None, shape, res))
            source = arrive[level]
        self.own = (own_row, own_col)
        self.sums = len(self.phases)
        self.phases += gathers[::-1]

    def piece(self, ref, corner, shape):
        def span(start, size, unit, whole):
            if size == whole:
                return pl.ds(0, size)
            return pl.ds(pl.multiple_of(start, unit), size)

        return ref.at[
            span(corner[0], shape[0], 16, ref.shape[0]), span(corner[1], shape[1], 128, ref.shape[1])
        ]

    def copy(self):
        bit, source, away, keep, shape, target = self.phases[self.at]
        piece = self.piece(source, away, shape)
        goal = piece if keep is None else target
        return remote(
            piece, goal, self.send.at[self.at], self.recv.at[self.at], dp_partner(self.spot, bit)
        )

    def start(self):
        self.copy().start()

    def add(self):
        _, source, _, keep, shape, target = self.phases[self.at]
        held = self.piece(source, keep, shape)
        last = self.at == self.sums - 1
        goal = self.piece(self.res, self.own, shape) if last else target
        step = 48 if shape[0] % 48 == 0 else 16

        def block(i, carry):
            rows = pl.ds(pl.multiple_of(i * step, 16), step)
            goal[rows, :] = (held[rows, :].astype(F32) + target[rows, :].astype(F32)).astype(BF16)
            return carry

        lax.fori_loop(0, shape[0] // step, block, 0)

    def advance(self):
        if self.at >= len(self.phases):
            return
        self.copy().wait()
        if self.at < self.sums:
            self.add()
        self.at += 1
        if self.at < len(self.phases):
            self.start()


def arrive_shapes(rows, cols, dp_bits):
    shapes = []
    for _ in range(dp_bits):
        if (rows // 2) % 16 == 0:
            rows = rows // 2
        elif (cols // 2) % 128 == 0:
            cols = cols // 2
        shapes.append((rows, cols))
    return shapes


class Exchange:
    def __init__(self, r, spot, part, arrive, out, come, sems, stats=None):
        self.r, self.spot = r, spot
        self.part, self.arrive, self.out, self.come = part, arrive, out, come
        self.sems, self.stats = sems, stats

    def core(self, c):
        at = lanes(c)
        copies = [
            remote(
                self.part.at[:, 1 - self.spot.c, :, at],
                self.arrive.at[:, :, at],
                self.sems.at[0, c],
                self.sems.at[1, c],
                self.spot.sib,
            )
        ]
        if self.stats is not None:
            copies.append(
                remote(
                    self.stats.at[0, :, at],
                    self.stats.at[1, :, at],
                    self.sems.at[2, c],
                    self.sems.at[3, c],
                    self.spot.sib,
                )
            )
        return copies

    def over(self, c):
        at = lanes(c)
        copies = [
            remote(
                self.out.at[:, at],
                self.come.at[:, at],
                self.sems.at[4, c],
                self.sems.at[5, c],
                self.spot.yp,
            )
        ]
        if self.stats is not None:
            copies.append(
                remote(
                    self.stats.at[2, :, at],
                    self.stats.at[3, :, at],
                    self.sems.at[6, c],
                    self.sems.at[7, c],
                    self.spot.yp,
                )
            )
        return copies

    def give(self, c, values):
        at = lanes(c)
        for j in range(4):
            self.part[j // 2, j % 2, :, at] = values[OWN * j : OWN * j + OWN].astype(BF16)
        for copy in self.core(c):
            copy.start()

    def pass_on(self, c):
        at = lanes(c)
        for copy in self.core(c):
            copy.wait()
        away = 1 - self.spot.y
        self.out[:, at] = (
            self.part[away, self.spot.c, :, at].astype(F32) + self.arrive[away, :, at].astype(F32)
        ).astype(BF16)
        if self.stats is not None:
            self.stats[2, :, at] = self.stats[0, :, at] + self.stats[1, :, at]
        for copy in self.over(c):
            copy.start()

    def take(self, c):
        at = lanes(c)
        for copy in self.over(c):
            copy.wait()
        home = self.spot.y
        return (
            self.part[home, self.spot.c, :, at].astype(F32)
            + self.arrive[home, :, at].astype(F32)
            + self.come[:, at].astype(F32)
        )

    def take_stats(self, c):
        at = lanes(c)
        return (self.stats[2, :, at] + self.stats[3, :, at]) * (1.0 / D)


class Spread:
    def __init__(self, spot, full, sems):
        self.spot, self.full, self.sems = spot, full, sems

    def piece(self, j, c, kind, device):
        part = self.full.at[feat(j), lanes(c)]
        return remote(part, part, self.sems.at[2 * kind, c], self.sems.at[2 * kind + 1, c], device)

    def to_y(self, c):
        return self.piece(self.spot.mp, c, 0, self.spot.yp)

    def to_sib(self, c):
        return self.piece(self.spot.mp, c, 1, self.spot.sib)

    def onward(self, c):
        return self.piece(self.spot.yp_mp, c, 2, self.spot.sib)

    def send(self, c):
        self.to_y(c).start()
        self.to_sib(c).start()

    def relay(self, c):
        self.to_y(c).wait()
        self.onward(c).start()

    def arrived(self, c):
        self.to_sib(c).wait()
        self.onward(c).wait()


def sin_cos(angle):
    turns = jnp.floor(angle * 0.6366197723675814 + 0.5)
    rest = angle - turns * 1.5703125
    rest = rest - turns * 4.837512969970703e-4
    rest = rest - turns * 7.549789948768648e-8
    square = rest * rest
    sine = rest + rest * square * (
        -1.6666654611e-1 + square * (8.3321608736e-3 + square * -1.9515295891e-4)
    )
    cosine = (
        1.0
        - 0.5 * square
        + square
        * square
        * (4.166664568298827e-2 + square * (-1.388731625493765e-3 + square * 2.443315711809948e-5))
    )
    quarter = turns - 4.0 * jnp.floor(turns * 0.25)
    odd = (quarter == 1.0) | (quarter == 3.0)
    sine_sign = jnp.where(quarter >= 2.0, -1.0, 1.0)
    cosine_sign = jnp.where((quarter == 1.0) | (quarter == 2.0), -1.0, 1.0)
    return (
        jnp.where(odd, cosine, sine) * sine_sign,
        jnp.where(odd, sine, cosine) * cosine_sign,
    )


def phi_parts(value):
    scaled = jnp.clip(value * root_half, -3.832506856900711, 3.832506856900711)
    square = scaled * scaled
    top = 0.00022905065861350646
    for factor in (
        0.0034082910107109506,
        0.050955695062380861,
        0.18520832239976145,
        1.128379143519084,
    ):
        top = top * square + factor
    low = -1.1791602954361697e-7
    for factor in (
        0.000023547966471313185,
        0.0010179625278914885,
        0.014070470171167667,
        0.11098505178285362,
        0.49746925110067538,
        1.0,
    ):
        low = low * square + factor
    error = scaled * top / low
    return (0.5 + 0.5 * error, inv_root_two_pi * jnp.exp(-0.5 * value * value))


def normalize(values):
    mean = jnp.mean(values, axis=0, keepdims=True)
    square = jnp.mean(values * values, axis=0, keepdims=True)
    inverse = lax.rsqrt(square - mean * mean + norm_eps)
    return ((values - mean) * inverse, mean, inverse)


def turn_by(values, cosine, sine):
    out = []
    for h in range(3):
        front, rear = values[64 * h : 64 * h + 32], values[64 * h + 32 : 64 * h + 64]
        co, si = cosine[32 * h : 32 * h + 32], sine[32 * h : 32 * h + 32]
        out += [front * co - rear * si, front * si + rear * co]
    return jnp.concatenate(out, axis=0)


def block_diagonal(tile):
    zero = jnp.zeros((64, TILE), tile.dtype)
    parts = []
    for h in range(3):
        column = [zero, zero, zero]
        column[h] = tile[64 * h : 64 * h + 64]
        parts.append(jnp.concatenate(column, axis=0))
    return jnp.concatenate(parts, axis=1)


def from_diagonal(values, heads):
    return jnp.concatenate(
        [values[64 * h : 64 * h + 64, TILE * n : TILE * n + TILE] for n, h in enumerate(heads)], axis=0
    )


def fold(values):
    return values[:, :128] + values[:, 128:]


def row_tables(r):
    pad = jnp.zeros((1, D - 3 * OWN), F32)
    qkv = jnp.concatenate([r.bqkv[n : n + 1, :].astype(F32) for n in range(3)] + [pad], axis=1)
    pad = jnp.zeros((2, D - 96), F32)
    freqs = jnp.concatenate([r.freqs[h] for h in range(3)] + [pad], axis=1)
    table = jnp.concatenate(
        [r.pack[0:1, :], qkv, freqs, r.pack[1:8, :], jnp.zeros((117, D), F32)], axis=0
    )
    for i in range(D // 128):
        r.cols[128 * i : 128 * i + 128, :] = jnp.transpose(table[:, 128 * i : 128 * i + 128])
    low = 1.0 - r.group[0].astype(F32)
    keep = r.keep[...].astype(F32)
    middle = lax.broadcasted_iota(jnp.int32, (1, ROWS), 1).astype(F32) + 0.5
    segment = low * jnp.floor(middle * (1.0 / (GRID_LO * GRID_LO))) + (1.0 - low) * jnp.floor(
        middle * (1.0 / SLOTS)
    )
    r.info[...] = jnp.zeros_like(r.info)
    r.info[0:2, 0:ROWS] = r.coords[...].astype(F32)
    r.info[2:3, 0:ROWS] = keep
    r.info[3:4, 0:ROWS] = keep * (segment + 1.0) - 1.0
    r.info[4:5, 0:ROWS] = segment
    kept = jnp.sum(keep, axis=1, keepdims=True)
    lane = lax.broadcasted_iota(jnp.int32, (8, 128), 1)
    r.cnt[...] = kept * jnp.where(lane == 0, low, jnp.where(lane == 1, 1.0 - low, 0.0))


def angle_tables(r):
    def block(c, carry):
        at = lanes(c)
        angle = r.cols[0:96, 2:3] * r.info[0:1, at] + r.cols[0:96, 3:4] * r.info[1:2, at]
        sine, cosine = sin_cos(angle)
        r.cos[:, at] = cosine
        r.sin[:, at] = sine
        return carry

    lax.fori_loop(0, CHUNKS, block, 0)

    def column(t, carry):
        row = r.info[3:4, tile_lanes(t)]
        r.kcol[pl.ds(pl.multiple_of(t * TILE, TILE), TILE), :] = jnp.transpose(
            jnp.broadcast_to(row, (TILE, TILE))
        )
        return carry

    lax.fori_loop(0, TILES, column, 0)


def flip(source, goal):
    for i in range(source.shape[1] // 128):
        part = source[:, 128 * i : 128 * i + 128].astype(F32)
        goal[128 * i : 128 * i + 128, 0 : source.shape[0]] = jnp.transpose(part).astype(BF16)


def project(r, c):
    at = lanes(c)
    normed, mean, inverse = normalize(r.x[:, at].astype(F32))
    r.rows1[0:1, at] = mean
    r.rows1[1:2, at] = inverse
    h1 = (normed * r.small[:, 4:5] + r.small[:, 5:6]).astype(BF16)
    r.h1[:, at] = h1
    projected = dot(r.wqkv[...], h1) + r.cols[0:576, 1:2]
    cosine, sine = r.cos[:, at], r.sin[:, at]
    query = turn_by(projected[0:192], cosine, sine)
    key = turn_by(projected[192:384], cosine, sine)
    value = projected[384:576]
    r.qk[0:192, at] = query.astype(BF16)
    r.qk[192:384, at] = key.astype(BF16)
    r.v[:, at] = value.astype(BF16)
    r.kn[at, :] = jnp.transpose(key).astype(BF16)
    r.vn[at, :] = jnp.transpose(value).astype(BF16)


def tile_mask(r, tile, start, width):
    window = pl.ds(pl.multiple_of(start, 16), width)
    allowed = r.kcol[window, :] == r.info[4:5, tile_lanes(tile)]
    return jnp.where(allowed, 0.0, -1e30)


def repeat(mask, values):
    return jnp.concatenate([mask] * (values.shape[1] // TILE), axis=1)


def head_groups(width):
    return [(0, 1, 2)] if width <= NARROW else [(0,), (1,), (2,)]


def attend_tile(r, spot, tile, start, width, values):
    window = pl.ds(pl.multiple_of(start, 16), width)
    at = tile_lanes(tile)
    queries = block_diagonal(r.qk[0:192, at] * BF16(0.125))
    mask = tile_mask(r, tile, start, width)
    for heads in head_groups(width):
        span = slice(TILE * heads[0], TILE * heads[-1] + TILE)
        scores = dot(r.kn[window, :], queries[:, span])
        scores = scores + repeat(mask, scores)
        top = jnp.max(scores, axis=0, keepdims=True)
        exponent = jnp.exp(scores - top)
        total = jnp.sum(exponent, axis=0, keepdims=True)
        probs = (exponent * (1.0 / total)).astype(BF16)
        out = from_diagonal(dot(values, probs), heads).astype(BF16)
        r.att[head_rows(spot, heads), at] = out
        r.lse[tile, :, span] = jnp.broadcast_to(top + jnp.log(total), (8, span.stop - span.start))


def head_rows(spot, heads):
    return pl.ds(pl.multiple_of(OWN * spot.mp + 64 * heads[0], 16), 64 * len(heads))


def back_tile(r, spot, tile, start, width, keys):
    window = pl.ds(pl.multiple_of(start, 16), width)
    at = tile_lanes(tile)
    queries = block_diagonal(r.qk[0:192, at] * BF16(0.125))
    grads = block_diagonal(dot(r.wout[...], r.gatt[:, at]).astype(BF16))
    mask = tile_mask(r, tile, start, width)
    for heads in head_groups(width):
        span = slice(TILE * heads[0], TILE * heads[-1] + TILE)
        query, grad = queries[:, span], grads[:, span]
        scores = dot(r.kn[window, :], query)
        probs = jnp.exp(scores + repeat(mask, scores) - r.lse[tile, 0:1, span])
        g_probs = dot(r.vn[window, :], grad)
        center = jnp.sum(probs * g_probs, axis=0, keepdims=True)
        g_scores = (probs * (g_probs - center)).astype(BF16)
        r.dv[window, :] += dot(probs.astype(BF16), grad, NT)
        r.dk[window, :] += dot(g_scores, query, NT)
        rows = slice(64 * heads[0], 64 * heads[-1] + 64)
        r.dq[rows, at] = (from_diagonal(dot(keys, g_scores), heads) * 0.125).astype(BF16)


def mlp_forward(r, spot, c, outward):
    at = lanes(c)
    mid = r.x[:, at].astype(F32) + (dot(r.wot[...], r.att[:, at]) + r.small[:, 8:9])
    normed, mean, inverse = normalize(mid)
    r.work[...] = mid
    r.mido[:, at] = r.work[feat(spot.mp), :]
    r.rows2[0:1, at] = mean
    r.rows2[1:2, at] = inverse
    h2 = (normed * r.small[:, 6:7] + r.small[:, 7:8]).astype(BF16)
    r.h2[:, at] = h2
    hidden = dot(r.wupt[...], h2) + r.cols[:, 0:1]
    lower, density = phi_parts(hidden)
    active = (hidden * lower).astype(BF16)
    r.act[:, at] = active
    r.gpre[:, at] = (lower + hidden * density).astype(BF16)
    outward.give(c, dot(r.wdnt[...], active))


def give_gradient(r, c, sums, grad, gain, bias, low):
    at = lanes(c)
    r.stats[0, 0:1, at] = jnp.sum(grad * gain, axis=0, keepdims=True)
    r.stats[0, 1:2, at] = jnp.sum(grad * (low[:, at].astype(F32) - bias), axis=0, keepdims=True)
    sums.give(c, grad)


def mlp_backward(r, c, sums):
    at = lanes(c)
    g_act = dot(r.wdn[...], r.gout[:, at])
    g_pre = (g_act * r.gpre[:, at].astype(F32)).astype(BF16)
    r.gpre[:, at] = g_pre
    r.sbup[...] += fold(g_pre.astype(F32))
    give_gradient(r, c, sums, dot(r.wup[...], g_pre), r.small[:, 6:7], r.small[:, 7:8], r.h2)


def second_norm_back(r, spot, c, sums):
    at = lanes(c)
    grad = sums.take(c)
    means = sums.take_stats(c)
    normed = (r.mido[:, at] - r.rows2[0:1, at]) * r.rows2[1:2, at]
    r.sg2[...] += fold(grad * normed)
    r.sb2[...] += fold(grad)
    back = r.rows2[1:2, at] * (
        grad * r.cols[0:192, 6:7] - means[0:1, :] - normed * means[1:2, :]
    )
    g_att = (r.gout[feat(spot.mp), at].astype(F32) + back).astype(BF16)
    r.gatt[feat(spot.mp), at] = g_att
    r.sbo[...] += fold(g_att.astype(F32))


def unrotate(r, c):
    at = lanes(c)
    cosine, sine = r.cos[:, at], r.sin[:, at]
    g_query = r.dq[0:192, at].astype(F32)
    g_key = jnp.transpose(r.dk[at, :]).astype(BF16).astype(F32)
    g_value = jnp.transpose(r.dv[at, :]).astype(BF16)
    plain = [turn_by(g, cosine, -sine).astype(BF16) for g in (g_query, g_key)]
    r.gproj[0:576, at] = jnp.concatenate(plain + [g_value], axis=0)
    angle = []
    for h in range(3):
        total = 0.0
        for part, g in enumerate((g_query, g_key)):
            rotated = r.qk[192 * part : 192 * part + 192, at].astype(F32)
            a, b = slice(64 * h, 64 * h + 32), slice(64 * h + 32, 64 * h + 64)
            total = total + (g[b] * rotated[a] - g[a] * rotated[b])
        angle.append(total)
    angle = jnp.concatenate(angle, axis=0)
    r.sf0[...] += fold(angle * r.info[0:1, at])
    r.sf1[...] += fold(angle * r.info[1:2, at])


def first_part(r, c, sums):
    grad = dot(r.wqkvn[:, 0:576], r.gproj[0:576, lanes(c)])
    give_gradient(r, c, sums, grad, r.small[:, 4:5], r.small[:, 5:6], r.h1)


def first_norm_back(r, spot, c, sums):
    at = lanes(c)
    grad = sums.take(c)
    means = sums.take_stats(c)
    own = feat(spot.mp)
    normed = (r.x[own, at].astype(F32) - r.rows1[0:1, at]) * r.rows1[1:2, at]
    r.sg1[...] += fold(grad * normed)
    r.sb1[...] += fold(grad)
    back = r.rows1[1:2, at] * (
        grad * r.cols[0:192, 4:5] - means[0:1, :] - normed * means[1:2, :]
    )
    r.igrad[:, at] = r.gatt[own, at].astype(F32) + back


def kernel(r, spot):
    peers = [dp_partner(spot, bit) for bit in range(r.dp_bits)]
    token_load = pltpu.make_async_copy(r.tok, r.out, r.load_sem.at[4])
    token_load.start()
    cot_load = pltpu.make_async_copy(r.cot, r.out, r.load_sem.at[5])
    loads = Refs()
    for n, (name, source) in enumerate(
        dict(wqkv=r.in_wqkv, wup=r.in_wup, wdn=r.in_wdn, wout=r.in_wout).items()
    ):
        setattr(loads, name, pltpu.make_async_copy(source, getattr(r, name), r.load_sem.at[n]))
        getattr(loads, name).start()
    greet([spot.sib, spot.yp] + peers)
    own = feat(spot.mp)
    r.x[own, ROWS - 64 : LANES] = jnp.zeros((OWN, 128), BF16)
    token_load.wait()
    r.x[own, 0:ROWS] = r.out[...]
    cot_load.start()
    tokens = Spread(spot, r.x, r.tk_sem)
    for c in range(CHUNKS):
        tokens.send(c)
    row_tables(r)
    r.small[own, :] = r.cols[0:192, :]
    here, there = r.small.at[own], r.small.at[feat(spot.yp_mp)]
    small_y = remote(r.cols.at[0:192], here, r.sm_sem.at[0], r.sm_sem.at[1], spot.yp)
    small_c = remote(r.cols.at[0:192], here, r.sm_sem.at[2], r.sm_sem.at[3], spot.sib)
    small_f = remote(there, there, r.sm_sem.at[4], r.sm_sem.at[5], spot.sib)
    small_y.start()
    small_c.start()

    def count_copy(bit):
        return remote(
            r.cnts.at[bit], r.cntr.at[bit], r.cn_sem.at[0, bit], r.cn_sem.at[1, bit], peers[bit]
        )

    r.cnts[0] = r.cnt[...]
    count_copy(0).start()
    angle_tables(r)
    cot_load.wait()
    r.gout[own, ROWS - 64 : LANES] = jnp.zeros((OWN, 128), BF16)
    r.gout[own, 0:ROWS] = (r.out[...].astype(F32) * r.info[2:3, 0:ROWS]).astype(BF16)
    small_y.wait()
    small_f.start()
    for ref in (r.sbup, r.sg1, r.sb1, r.sg2, r.sb2, r.sbo, r.sf0, r.sf1, r.dk, r.dv):
        ref[...] = jnp.zeros_like(ref)
    loads.wup.wait()
    flip(r.wup, r.wupt)
    small_c.wait()
    small_f.wait()
    loads.wdn.wait()
    flip(r.wdn, r.wdnt)
    total = r.cnt[...]
    for bit in range(r.dp_bits):
        count_copy(bit).wait()
        total = r.cnts[bit] + r.cntr[bit]
        if bit + 1 < r.dp_bits:
            r.cnts[bit + 1] = total
            count_copy(bit + 1).start()
    low, high = total[:, 0:1], total[:, 1:2]
    own_low = 1.0 - r.group[0].astype(F32)
    share = (own_low * low + (1.0 - own_low) * high) / (low + high)
    r.share[...] = jnp.broadcast_to(share, (8, 128))
    loads.wqkv.wait()
    loads.wout.wait()
    wo_here = r.wof.at[own]
    wo_there = r.wof.at[feat(spot.yp_mp)]
    wo_y = remote(r.wout, wo_here, r.wo_sem.at[0], r.wo_sem.at[1], spot.yp)
    wo_c = remote(r.wout, wo_here, r.wo_sem.at[2], r.wo_sem.at[3], spot.sib)
    wo_f = remote(wo_there, wo_there, r.wo_sem.at[4], r.wo_sem.at[5], spot.sib)
    wo_c.start()
    r.wof[own, :] = r.wout[...]
    attended = Spread(spot, r.att, r.at_sem)
    cotangents = Spread(spot, r.gout, r.ct_sem)

    tokens.relay(0)

    def project_chunk(c, carry):
        @pl.when(c + 1 < CHUNKS)
        def _():
            tokens.relay(c + 1)

        tokens.arrived(c)

        @pl.when(c == 2)
        def _():
            wo_y.start()

        @pl.when(c >= 4)
        def _():
            cotangents.send(c - 4)

        project(r, c)
        return carry

    lax.fori_loop(0, CHUNKS, project_chunk, 0)

    def windows(source):
        for j in range(3):
            start = 576 * j - 32 * (j // 2)
            r.win[j, :, 0:NARROW] = source[:, start : start + NARROW]

    def both_tiles(c, tile, source):
        for half in range(2):
            t = 2 * c + half
            j = t // 5

            @pl.when((t != 4) & (t != 9))
            def _():
                tile(r, spot, t, 576 * j - 32 * (j // 2), NARROW, r.win[j, :, 0:NARROW])

            if half == 0:

                @pl.when(t == 4)
                def _():
                    tile(r, spot, 4, 0, 1152, source[:, 0:1152])

            else:

                @pl.when(t == 9)
                def _():
                    tile(r, spot, 9, 976, 752, source[:, 976:1728])

    windows(r.v)

    def attend(c, carry):
        both_tiles(c, attend_tile, r.v)
        attended.send(c)

        @pl.when(c + 3 < CHUNKS)
        def _():
            cotangents.send(c + 3)

        @pl.when((c >= 3) & (c <= 5))
        def _():
            cotangents.relay(c - 3)

        return carry

    lax.fori_loop(0, CHUNKS, attend, 0)
    wo_y.wait()
    wo_f.start()
    r.atto[...] = r.att[own, :]
    attended.relay(0)
    wo_c.wait()
    wo_f.wait()
    flip(r.wof, r.wot)

    outward = Exchange(r, spot, r.mp, r.mr, r.ms, r.mc, r.mo_sem)
    second = Exchange(r, spot, r.gp, r.gr, r.gs, r.gc, r.g2_sem, r.stats)
    g_att = Spread(spot, r.gatt, r.ga_sem)
    order = list(range(r.dp_bits))
    turned = order[1:] + order[:1]

    def halves(acc, arrive, res, sems):
        rows = acc.shape[0] // 2
        return [
            Reduce(
                spot,
                acc.at[rows * n : rows * n + rows],
                arrive[n],
                res.at[rows * n : rows * n + rows],
                order,
                sems.at[n],
            )
            for n in range(2)
        ]

    down = halves(r.accdn, r.ardn, r.resdn, r.dn_sem)
    up = halves(r.accup, r.arup, r.resup, r.up_sem)

    def advance(*reduces):
        for reduce in reduces:
            reduce.advance()

    def forward(n, carry):
        @pl.when(n + 1 < CHUNKS)
        def _():
            attended.relay(n + 1)

            @pl.when(n + 1 >= 3)
            def _():
                cotangents.relay(n + 1)

        attended.arrived(n)
        mlp_forward(r, spot, n, outward)
        return carry

    lax.fori_loop(0, CHUNKS, forward, 0)
    for c in range(CHUNKS):
        cotangents.arrived(c)
    r.accdn[...] = (dot(r.act[...], r.gout[...], NT) * r.share[0:1, 0:1]).astype(BF16)
    down[0].start()
    down[1].start()

    def norm_step(c):
        second_norm_back(r, spot, c, second)
        g_att.send(c)

    def backward(n, carry):
        mlp_backward(r, n, second)

        @pl.when(n >= 1)
        def _():
            second.pass_on(n - 1)

        @pl.when(n >= 3)
        def _():
            norm_step(n - 3)

        @pl.when(n == 3)
        def _():
            advance(down[0])

        @pl.when(n == 6)
        def _():
            advance(down[1], down[0])

        return carry

    lax.fori_loop(0, CHUNKS, backward, 0)
    second.pass_on(CHUNKS - 1)
    r.accup[...] = (dot(r.h2[...], r.gpre[...], NT) * r.share[0:1, 0:1]).astype(BF16)
    up[0].start()
    up[1].start()
    flip(r.wqkv, r.wqkvn)
    windows(r.qk.at[192:384])
    first = Exchange(r, spot, r.gp, r.gr, r.gs, r.gc, r.g1_sem, r.stats)
    g_att.relay(0)

    def first_chunks(chunks):
        def one(c, carry):
            unrotate(r, c)
            first_part(r, c, first)
            return carry

        lax.fori_loop(chunks[0], chunks[-1] + 1, one, 0)

    def back(c, carry):
        @pl.when(c + 4 < CHUNKS)
        def _():
            norm_step(c + 4)

        @pl.when(c + 1 < CHUNKS)
        def _():
            g_att.relay(c + 1)

        g_att.arrived(c)
        both_tiles(c, back_tile, r.qk.at[192:384])

        @pl.when(c == 0)
        def _():
            advance(down[1], down[0])

        @pl.when(c == 2)
        def _():
            first_chunks((0, 1))
            advance(up[0], down[1], down[0], up[1])

        @pl.when(c == 3)
        def _():
            first.pass_on(0)
            first.pass_on(1)
            outward.pass_on(0)
            outward.pass_on(1)

        @pl.when(c == 4)
        def _():
            first_chunks((2, 3))
            advance(up[0], down[1], down[0])

        @pl.when(c == 5)
        def _():
            first.pass_on(2)
            first.pass_on(3)
            outward.pass_on(2)
            outward.pass_on(3)
            advance(up[1])

        return carry

    lax.fori_loop(0, CHUNKS, back, 0)
    first_chunks((4, 5, 6))
    advance(down[1], up[0], down[0], up[1])
    r.accqkv[...] = (dot(r.gproj[0:576, :], r.h1[...], NT) * r.share[0:1, 0:1]).astype(BF16)
    qkv = [
        Reduce(
            spot,
            r.accqkv.at[OWN * n : OWN * n + OWN],
            r.arqkv[n],
            r.resqkv.at[OWN * n : OWN * n + OWN],
            order if n < 2 else turned,
            r.qr_sem.at[n],
        )
        for n in range(3)
    ]
    for reduce in qkv:
        reduce.start()
    for c in range(4, CHUNKS):
        first.pass_on(c)
    r.accwo[...] = (dot(r.atto[...], r.gatt[...], NT) * r.share[0:1, 0:1]).astype(BF16)
    out = Reduce(spot, r.accwo, r.arwo, r.reswo, turned, r.wr_sem)
    out.start()
    for c in range(4, CHUNKS):
        outward.pass_on(c)
    advance(up[0])

    def norm_one(c, carry):
        first_norm_back(r, spot, c, first)
        return carry

    lax.fori_loop(0, 5, norm_one, 0)
    advance(down[1], qkv[2], up[1])
    lax.fori_loop(5, CHUNKS, norm_one, 0)
    advance(qkv[0], out)

    def lane_sum(ref):
        return jnp.sum(ref[...], axis=1, keepdims=True)

    b_down = jnp.sum(r.gout[own, :].astype(F32), axis=1, keepdims=True)
    b_qkv = jnp.sum(r.gproj[0:576, :].astype(F32), axis=1, keepdims=True)
    columns = [
        lane_sum(r.sbup),
        jnp.concatenate([b_qkv, lane_sum(r.sf0), lane_sum(r.sf1)], axis=0),
        jnp.concatenate([lane_sum(r.sbo), lane_sum(r.sg1), lane_sum(r.sb1), lane_sum(r.sg2)], axis=0),
        jnp.concatenate([lane_sum(r.sb2), b_down, jnp.zeros((384, 1), F32)], axis=0),
    ]
    lane = lax.broadcasted_iota(jnp.int32, (D, 128), 1)
    table = jnp.zeros((D, 128), F32)
    for n, column in enumerate(columns):
        table = jnp.where(lane == n, column, table)
    table = jnp.transpose(table * r.share[0:1, 0:1])[0:8, :]
    between = [
        (qkv[1], up[0], qkv[2], up[1], out, qkv[0], qkv[1]),
        (up[0], qkv[0], qkv[2], qkv[1]),
        (qkv[0], qkv[1], up[1], out, qkv[2], qkv[0], qkv[1], out),
    ]
    for bit in range(r.dp_bits):
        r.sumx[bit] = table
        copy = remote(
            r.sumx.at[bit], r.sumr.at[bit], r.su_sem.at[0, bit], r.su_sem.at[1, bit], peers[bit]
        )
        copy.start()
        if bit < len(between):
            advance(*between[bit])
        copy.wait()
        table = table + r.sumr[bit]
    r.sums[...] = table
    finish_out(r, spot, outward)
    reduces = [qkv[2], qkv[0], out, qkv[1]] + up + down
    while any(reduce.at < len(reduce.phases) for reduce in reduces):
        advance(*reduces)


def finish_out(r, spot, outward):
    for c in range(CHUNKS):
        at = lanes(c)
        total = outward.take(c)
        whole = r.mido[:, at] + (total + r.cols[0:192, 9:10])
        r.gs[:, at] = (r.info[2:3, at] * whole).astype(BF16)
    r.out[...] = r.gs[:, 0:ROWS]


def dma(*shape):
    return pltpu.SemaphoreType.DMA(shape)


def run(dp_bits, **arrays):
    scalars = ("group",)
    on_demand = ("tok", "cot", "in_wqkv", "in_wup", "in_wdn", "in_wout")
    outs = dict(
        out=((OWN, ROWS), BF16),
        igrad=((OWN, LANES), F32),
        resdn=((D, D), BF16),
        resup=((D, D), BF16),
        reswo=((OWN, D), BF16),
        resqkv=((576, D), BF16),
        sums=((8, D), F32),
    )

    def levels(rows):
        return [VM(shape, BF16) for shape in arrive_shapes(rows, D, dp_bits)]

    full = VM((D, LANES), BF16)
    own = VM((OWN, LANES), BF16)
    square = VM((D, D), BF16)
    spread = dma(6, CHUNKS)
    scratch = dict(
        x=full,
        h1=full,
        qk=VM((384, LANES), BF16),
        v=own,
        kn=VM((LANES, OWN), BF16),
        vn=VM((LANES, OWN), BF16),
        cos=VM((96, LANES), F32),
        sin=VM((96, LANES), F32),
        kcol=VM((LANES, TILE), F32),
        win=VM((3, OWN, 640), BF16),
        lse=VM((TILES, 8, 384), F32),
        small=VM((D, 128), F32),
        share=VM((8, 128), F32),
        att=full,
        gout=full,
        wqkv=VM((576, D), BF16),
        wup=square,
        wupt=square,
        wdn=square,
        wdnt=square,
        wout=VM((OWN, D), BF16),
        wof=square,
        wot=square,
        h2=full,
        act=full,
        gpre=full,
        work=VM((D, CHUNK), F32),
        mido=VM((OWN, LANES), F32),
        rows1=VM((8, LANES), F32),
        rows2=VM((8, LANES), F32),
        info=VM((8, LANES), F32),
        cols=VM((D, 128), F32),
        cnt=VM((8, 128), F32),
        stats=VM((4, 8, LANES), F32),
        mp=VM((2, 2, OWN, LANES), BF16),
        mr=VM((2, OWN, LANES), BF16),
        gp=VM((2, 2, OWN, LANES), BF16),
        gr=VM((2, OWN, LANES), BF16),
        gs=own,
        gc=own,
        dk=VM((LANES, OWN), F32),
        dv=VM((LANES, OWN), F32),
        ardn=[levels(384), levels(384)],
        arup=[levels(384), levels(384)],
        arwo=levels(OWN),
        arqkv=[levels(OWN), levels(OWN), levels(OWN)],
        sbup=VM((D, 128), F32),
        sg1=VM((OWN, 128), F32),
        sb1=VM((OWN, 128), F32),
        sg2=VM((OWN, 128), F32),
        sb2=VM((OWN, 128), F32),
        sbo=VM((OWN, 128), F32),
        sf0=VM((96, 128), F32),
        sf1=VM((96, 128), F32),
        cnts=VM((dp_bits, 8, 128), F32),
        cntr=VM((dp_bits, 8, 128), F32),
        sumx=VM((dp_bits, 8, D), F32),
        sumr=VM((dp_bits, 8, D), F32),
        load_sem=dma(6),
        tk_sem=spread,
        at_sem=spread,
        ct_sem=spread,
        ga_sem=spread,
        sm_sem=dma(6),
        wo_sem=dma(6),
        cn_sem=dma(2, dp_bits),
        su_sem=dma(2, dp_bits),
        mo_sem=dma(8, CHUNKS),
        g2_sem=dma(8, CHUNKS),
        g1_sem=dma(8, CHUNKS),
        dn_sem=dma(2, 2, 2 * dp_bits),
        up_sem=dma(2, 2, 2 * dp_bits),
        wr_sem=dma(2, 2 * dp_bits),
        qr_sem=dma(3, 2, 2 * dp_bits),
    )
    shapes, structure = jax.tree.flatten(scratch, is_leaf=lambda leaf: not isinstance(leaf, (dict, list)))

    def body(*refs):
        r = Refs()
        for name, ref in zip(list(arrays) + list(outs), refs):
            setattr(r, name, ref)
        named = jax.tree.unflatten(structure, refs[len(arrays) + len(outs) :])
        for name, ref in named.items():
            setattr(r, name, ref)
        r.gatt, r.atto = r.att, r.v
        r.dq, r.gproj, r.ms = r.act, r.h2, r.act.at[OWN : 2 * OWN]
        r.mc = r.act.at[2 * OWN : 3 * OWN]
        r.accdn, r.accup, r.accwo = r.wof, r.wupt, r.wdn.at[0:OWN]
        r.wqkvn = r.wot
        r.accqkv = r.wdnt.at[0:576]
        r.dp_bits = dp_bits
        kernel(r, place())

    results = pl.pallas_call(
        body,
        out_shape=[jax.ShapeDtypeStruct(shape, dtype) for shape, dtype in outs.values()],
        in_specs=[
            pl.BlockSpec(
                memory_space=pl.ANY if name in on_demand else pltpu.SMEM if name in scalars else VM
            )
            for name in arrays
        ],
        out_specs=[pl.BlockSpec(memory_space=VM) for _ in outs],
        scratch_shapes=shapes,
        compiler_params=pltpu.CompilerParams(
            collective_id=1, has_side_effects=True, vmem_limit_bytes=64 * MIB - 65536
        ),
    )(*arrays.values())
    named = Refs()
    for name, result in zip(outs, results, strict=True):
        setattr(named, name, result)
    return named


def local(
    tokens,
    w_qkv,
    b_qkv,
    freqs,
    w_out,
    b_out,
    norm1_gain,
    norm1_bias,
    norm2_gain,
    norm2_bias,
    w_up,
    b_up,
    w_down,
    b_down,
    cotangent,
    keep_mask,
    coords,
    block_group,
):
    row_count, width_loc = tokens.shape
    heads_loc = freqs.shape[1]
    row = lax.broadcasted_iota(jnp.int32, (8, D), 0)
    pack = jnp.zeros((8, D), F32)
    vectors = (b_up, norm1_gain, norm1_bias, norm2_gain, norm2_bias, b_out, b_down)
    for n, vector in enumerate(vectors):
        wide = jnp.pad(vector.astype(F32), (0, D - vector.shape[0]))
        pack = jnp.where(row == n, wide[None, :], pack)

    a = run(
        lax.axis_size("dp").bit_length() - 1,
        tok=tokens.T,
        cot=cotangent.T,
        pack=pack,
        bqkv=b_qkv,
        freqs=freqs.transpose(1, 0, 2),
        keep=keep_mask.reshape(1, row_count),
        coords=coords,
        group=block_group,
        in_wqkv=w_qkv.transpose(1, 2, 0).reshape(3 * width_loc, D),
        in_wup=w_up,
        in_wdn=w_down,
        in_wout=w_out,
    )
    sums = a.sums
    grad_qkv = a.resqkv.astype(F32)
    half = (2, heads_loc, HEAD_DIM // 2)
    return (
        a.out.T,
        a.igrad[:, :row_count].T,
        grad_qkv.reshape(3, width_loc, D).transpose(2, 0, 1),
        sums[1, : 3 * width_loc].reshape(3, width_loc),
        sums[1, 3 * width_loc :].reshape(half),
        a.reswo.astype(F32),
        sums[2, 0:192],
        sums[2, 192:384],
        sums[2, 384:576],
        sums[2, 576:768],
        sums[3, 0:192],
        a.resup.astype(F32),
        sums[0],
        a.resdn.astype(F32),
        sums[3, 192:384],
    )


def solution(mesh):
    return jax.shard_map(
        local,
        mesh=mesh,
        in_specs=(
            P("dp", "mp"),
            P(None, None, "mp"),
            P(None, "mp"),
            P(None, "mp", None),
            P("mp", None),
            P("mp"),
            P("mp"),
            P("mp"),
            P("mp"),
            P("mp"),
            P(None, "mp"),
            P("mp"),
            P("mp", None),
            P("mp"),
            P("dp", "mp"),
            P("dp"),
            P(None, "dp"),
            P("dp"),
        ),
        out_specs=(
            P("dp", "mp"),
            P("dp", "mp"),
            P(None, None, "mp"),
            P(None, "mp"),
            P(None, "mp", None),
            P("mp", None),
            P("mp"),
            P("mp"),
            P("mp"),
            P("mp"),
            P("mp"),
            P(None, "mp"),
            P("mp"),
            P("mp", None),
            P("mp"),
        ),
        check_vma=False,
    )
```

```python
import jax
import jax.numpy as jnp
from jax import lax
from jax.experimental import pallas as pl
from jax.experimental.pallas import tpu as pltpu
from jax.sharding import PartitionSpec as P

HEAD_DIM = 64
GRID_LO = 14
SLOTS = 576

MESH = pl.DeviceIdType.MESH
MIB = 1024 * 1024
VM = pltpu.VMEM
F32 = jnp.float32
BF16 = jnp.bfloat16
NT = (((1,), (1,)), ((), ()))
NN = (((1,), (0,)), ((), ()))

D = 768
OWN = 192
ROWS = 1728
LANES = 1792
CHUNK = 256
CHUNKS = LANES // CHUNK
TILE = 128
TILES = LANES // TILE
NARROW = 608

norm_eps = 1e-06
root_half = 0.7071067811865476
inv_root_two_pi = 0.3989422804014327


EARLY = 2
IN_BACKWARD = {6: (0,)}
BEFORE_TILES = {0: (0,), 1: (1,)}
AFTER_TILES = {1: (2, 0), 2: (3, 1, 2, 0), 3: (3,), 4: (1, 2, 0, 3), 5: (1,), 6: (2, 0, 3)}
AT_END = {1: (1, 2), 2: (3,), 4: (4, 6, 5, 7), 5: (1,)}
IN_SUMS = ((), (4, 2, 6, 5, 7, 3), (6, 7, 4, 5))


class Refs:
    pass


def dot(left, right, dims=NN):
    return lax.dot_general(left, right, dims, preferred_element_type=F32)


def remote(src, dst, send, recv, device):
    return pltpu.make_async_remote_copy(
        src_ref=src, dst_ref=dst, send_sem=send, recv_sem=recv, device_id=device, device_id_type=MESH
    )


def place():
    spot = Refs()
    spot.dp = lax.axis_index("dp")
    spot.mp = lax.axis_index("mp")
    spot.y = spot.mp // 2
    spot.c = spot.mp % 2
    spot.sib_mp = 2 * spot.y + 1 - spot.c
    spot.yp_mp = 2 * (1 - spot.y) + spot.c
    spot.sib = (spot.dp, spot.sib_mp)
    spot.yp = (spot.dp, spot.yp_mp)
    return spot


def greet(devices):
    barrier = pltpu.get_barrier_semaphore()
    for device in devices:
        pl.semaphore_signal(barrier, inc=1, device_id=device, device_id_type=MESH)


def meet(devices):
    pl.semaphore_wait(pltpu.get_barrier_semaphore(), len(devices))


def dp_partner(spot, bit):
    mine = (spot.dp // (1 << bit)) % 2
    return (spot.dp + (1 - 2 * mine) * (1 << bit), spot.mp)


def feat(j):
    return pl.ds(pl.multiple_of(OWN * j, 16), OWN)


def lanes(c):
    return pl.ds(pl.multiple_of(c * CHUNK, CHUNK), CHUNK)


def tile_lanes(t):
    return pl.ds(pl.multiple_of(t * TILE, TILE), TILE)


def flipped(spot, bits, number):
    dp = spot.dp
    for n, bit in enumerate(bits):
        if (number >> n) & 1:
            dp = dp + (1 - 2 * ((spot.dp // (1 << bit)) % 2)) * (1 << bit)
    return (dp, spot.mp)


def cut(shape):
    rows, cols = shape
    if (rows // 2) % 16 == 0:
        return (rows // 2, cols)
    if (cols // 2) % 128 == 0:
        return (rows, cols // 2)
    return shape


def plan(shape, groups):
    steps = []
    for bits in groups:
        after = shape
        for _ in bits:
            after = cut(after)
        whole = cut(cut(shape)) if len(bits) == 2 else cut(shape)
        if len(bits) == 2 and cut(shape) == cut(cut(shape)):
            for bit in bits:
                now = cut(shape)
                steps.append(((bit,), now, now != shape))
                shape = now
            continue
        steps.append((bits, whole, whole != shape))
        shape = after
    return steps


class Reduce:
    def __init__(self, spot, acc, arrive, res, groups, sems):
        self.spot, self.res, self.sems = spot, res, sems
        self.at = 0
        self.phases = []
        gathers = []
        source, row, col = acc, 0, 0
        steps = plan(acc.shape, groups)
        shape = acc.shape
        for (bits, after, differ), target in zip(steps, arrive, strict=True):
            corners = []
            for number in range(1 << len(bits)):
                at, part = (0, 0), shape
                for n, bit in enumerate(bits):
                    smaller = cut(part)
                    mine = (spot.dp // (1 << bit)) % 2
                    side = 1 - mine if (number >> n) & 1 else mine
                    if smaller[0] < part[0]:
                        at = (at[0] + side * smaller[0], at[1])
                    elif smaller[1] < part[1]:
                        at = (at[0], at[1] + side * smaller[1])
                    part = smaller
                corners.append(at)
            row, col = row + corners[0][0], col + corners[0][1]
            self.phases.append((bits, source, corners, after, target))
            if differ:
                gathers.append((bits, res, (row, col), after, None))
            source, shape = target.at[0], after
        self.own = (row, col)
        self.sums = len(self.phases)
        self.phases += gathers[::-1]

    def piece(self, ref, corner, shape):
        def span(start, size, unit, whole):
            if size == whole:
                return pl.ds(0, size)
            return pl.ds(pl.multiple_of(start, unit), size)

        return ref.at[
            span(corner[0], shape[0], 16, ref.shape[0]), span(corner[1], shape[1], 128, ref.shape[1])
        ]

    def copies(self):
        bits, source, corners, shape, target = self.phases[self.at]
        out = []
        for number in range(1, 1 << len(bits)):
            if target is None:
                piece = self.piece(source, corners, shape)
                goal = piece
            else:
                piece = self.piece(source, corners[number], shape)
                goal = target.at[number - 1]
            sems = (self.sems.at[0, self.at, number - 1], self.sems.at[1, self.at, number - 1])
            out.append(remote(piece, goal, *sems, flipped(self.spot, bits, number)))
        return out

    def start(self):
        for copy in self.copies():
            copy.start()

    def add(self):
        bits, source, corners, shape, target = self.phases[self.at]
        held = self.piece(source, corners[0], shape)
        last = self.at == self.sums - 1
        goal = self.piece(self.res, self.own, shape) if last else target.at[0]
        step = 48 if shape[0] % 48 == 0 else 16

        def block(i, carry):
            rows = pl.ds(pl.multiple_of(i * step, 16), step)
            total = held[rows, :].astype(F32)
            for n in range((1 << len(bits)) - 1):
                total = total + target[n, rows, :].astype(F32)
            goal[rows, :] = total.astype(BF16)
            return carry

        lax.fori_loop(0, shape[0] // step, block, 0)

    def advance(self):
        if self.at >= len(self.phases):
            return
        for copy in self.copies():
            copy.wait()
        if self.at < self.sums:
            self.add()
        self.at += 1
        if self.at < len(self.phases):
            self.start()


class Exchange:
    def __init__(self, r, spot, part, arrive, out, come, sems, stats=None):
        self.r, self.spot = r, spot
        self.part, self.arrive, self.out, self.come = part, arrive, out, come
        self.sems, self.stats = sems, stats

    def core(self, c):
        at = lanes(c)
        copies = [
            remote(
                self.part.at[:, 1 - self.spot.c, :, at],
                self.arrive.at[:, :, at],
                self.sems.at[0, c],
                self.sems.at[1, c],
                self.spot.sib,
            )
        ]
        if self.stats is not None:
            copies.append(
                remote(
                    self.stats.at[0, :, at],
                    self.stats.at[1, :, at],
                    self.sems.at[2, c],
                    self.sems.at[3, c],
                    self.spot.sib,
                )
            )
        return copies

    def over(self, c):
        at = lanes(c)
        copies = [
            remote(
                self.out.at[:, at],
                self.come.at[:, at],
                self.sems.at[4, c],
                self.sems.at[5, c],
                self.spot.yp,
            )
        ]
        if self.stats is not None:
            copies.append(
                remote(
                    self.stats.at[2, :, at],
                    self.stats.at[3, :, at],
                    self.sems.at[6, c],
                    self.sems.at[7, c],
                    self.spot.yp,
                )
            )
        return copies

    def give(self, c, values):
        at = lanes(c)
        for j in range(4):
            self.part[j // 2, j % 2, :, at] = values[OWN * j : OWN * j + OWN].astype(BF16)
        for copy in self.core(c):
            copy.start()

    def pass_on(self, c):
        at = lanes(c)
        for copy in self.core(c):
            copy.wait()
        away = 1 - self.spot.y
        self.out[:, at] = (
            self.part[away, self.spot.c, :, at].astype(F32) + self.arrive[away, :, at].astype(F32)
        ).astype(BF16)
        if self.stats is not None:
            self.stats[2, :, at] = self.stats[0, :, at] + self.stats[1, :, at]
        for copy in self.over(c):
            copy.start()

    def take(self, c):
        at = lanes(c)
        for copy in self.over(c):
            copy.wait()
        home = self.spot.y
        return (
            self.part[home, self.spot.c, :, at].astype(F32)
            + self.arrive[home, :, at].astype(F32)
            + self.come[:, at].astype(F32)
        )

    def take_stats(self, c):
        at = lanes(c)
        return (self.stats[2, :, at] + self.stats[3, :, at]) * (1.0 / D)


class Spread:
    def __init__(self, spot, full, sems):
        self.spot, self.full, self.sems = spot, full, sems

    def piece(self, j, c, kind, device):
        part = self.full.at[feat(j), lanes(c)]
        return remote(part, part, self.sems.at[2 * kind, c], self.sems.at[2 * kind + 1, c], device)

    def to_y(self, c):
        return self.piece(self.spot.mp, c, 0, self.spot.yp)

    def to_sib(self, c):
        return self.piece(self.spot.mp, c, 1, self.spot.sib)

    def onward(self, c):
        return self.piece(self.spot.yp_mp, c, 2, self.spot.sib)

    def send(self, c):
        self.to_y(c).start()
        self.to_sib(c).start()

    def relay(self, c):
        self.to_y(c).wait()
        self.onward(c).start()

    def arrived(self, c):
        self.to_sib(c).wait()
        self.onward(c).wait()


def sin_cos(angle):
    turns = jnp.floor(angle * 0.6366197723675814 + 0.5)
    rest = angle - turns * 1.5703125
    rest = rest - turns * 4.837512969970703e-4
    rest = rest - turns * 7.549789948768648e-8
    square = rest * rest
    sine = rest + rest * square * (
        -1.6666654611e-1 + square * (8.3321608736e-3 + square * -1.9515295891e-4)
    )
    cosine = (
        1.0
        - 0.5 * square
        + square
        * square
        * (4.166664568298827e-2 + square * (-1.388731625493765e-3 + square * 2.443315711809948e-5))
    )
    quarter = turns - 4.0 * jnp.floor(turns * 0.25)
    odd = (quarter == 1.0) | (quarter == 3.0)
    sine_sign = jnp.where(quarter >= 2.0, -1.0, 1.0)
    cosine_sign = jnp.where((quarter == 1.0) | (quarter == 2.0), -1.0, 1.0)
    return (
        jnp.where(odd, cosine, sine) * sine_sign,
        jnp.where(odd, sine, cosine) * cosine_sign,
    )


def phi_parts(value):
    bell = jnp.exp(-0.5 * value * value)
    inner = 1.0 / (1.0 + (0.3275911 * root_half) * jnp.abs(value))
    series = 0.5 * 1.061405429
    for factor in (-1.453152027, 1.421413741, -0.284496736, 0.254829592):
        series = series * inner + 0.5 * factor
    beyond = series * inner * bell
    return (jnp.where(value >= 0.0, 1.0 - beyond, beyond), inv_root_two_pi * bell)


def normalize(values):
    mean = jnp.mean(values, axis=0, keepdims=True)
    square = jnp.mean(values * values, axis=0, keepdims=True)
    inverse = lax.rsqrt(square - mean * mean + norm_eps)
    return ((values - mean) * inverse, mean, inverse)


def turn_by(values, cosine, sine):
    out = []
    for h in range(3):
        front, rear = values[64 * h : 64 * h + 32], values[64 * h + 32 : 64 * h + 64]
        co, si = cosine[32 * h : 32 * h + 32], sine[32 * h : 32 * h + 32]
        out += [front * co - rear * si, front * si + rear * co]
    return jnp.concatenate(out, axis=0)


def block_diagonal(tile):
    zero = jnp.zeros((64, TILE), tile.dtype)
    parts = []
    for h in range(3):
        column = [zero, zero, zero]
        column[h] = tile[64 * h : 64 * h + 64]
        parts.append(jnp.concatenate(column, axis=0))
    return jnp.concatenate(parts, axis=1)


def from_diagonal(values, heads):
    return jnp.concatenate(
        [values[64 * h : 64 * h + 64, TILE * n : TILE * n + TILE] for n, h in enumerate(heads)], axis=0
    )


def fold(values):
    return values[:, :128] + values[:, 128:]


def row_tables(r):
    pad = jnp.zeros((1, D - 3 * OWN), F32)
    qkv = jnp.concatenate([r.bqkv[n : n + 1, :].astype(F32) for n in range(3)] + [pad], axis=1)
    pad = jnp.zeros((2, D - 96), F32)
    freqs = jnp.concatenate([r.freqs[h] for h in range(3)] + [pad], axis=1)
    table = jnp.concatenate(
        [r.pack[0:1, :], qkv, freqs, r.pack[1:8, :], jnp.zeros((117, D), F32)], axis=0
    )
    for i in range(D // 128):
        r.cols[128 * i : 128 * i + 128, :] = jnp.transpose(table[:, 128 * i : 128 * i + 128])
    low = 1.0 - r.group[0].astype(F32)
    keep = r.keep[...].astype(F32)
    middle = lax.broadcasted_iota(jnp.int32, (1, ROWS), 1).astype(F32) + 0.5
    segment = low * jnp.floor(middle * (1.0 / (GRID_LO * GRID_LO))) + (1.0 - low) * jnp.floor(
        middle * (1.0 / SLOTS)
    )
    r.info[...] = jnp.zeros_like(r.info)
    r.info[0:2, 0:ROWS] = r.coords[...].astype(F32)
    r.info[2:3, 0:ROWS] = keep
    r.info[3:4, 0:ROWS] = keep * (segment + 1.0) - 1.0
    r.info[4:5, 0:ROWS] = segment
    kept = jnp.sum(keep, axis=1, keepdims=True)
    lane = lax.broadcasted_iota(jnp.int32, (8, 128), 1)
    r.cnt[...] = kept * jnp.where(lane == 0, low, jnp.where(lane == 1, 1.0 - low, 0.0))


def angle_tables(r):
    def block(c, carry):
        at = lanes(c)
        angle = r.cols[0:96, 2:3] * r.info[0:1, at] + r.cols[0:96, 3:4] * r.info[1:2, at]
        sine, cosine = sin_cos(angle)
        r.cos[:, at] = cosine
        r.sin[:, at] = sine
        return carry

    lax.fori_loop(0, CHUNKS, block, 0)

    def column(t, carry):
        row = r.info[3:4, tile_lanes(t)]
        r.kcol[pl.ds(pl.multiple_of(t * TILE, TILE), TILE), :] = jnp.transpose(
            jnp.broadcast_to(row, (TILE, TILE))
        )
        return carry

    lax.fori_loop(0, TILES, column, 0)


def flip(source, goal):
    for i in range(source.shape[1] // 128):
        part = source[:, 128 * i : 128 * i + 128].astype(F32)
        goal[128 * i : 128 * i + 128, 0 : source.shape[0]] = jnp.transpose(part).astype(BF16)


def project(r, c):
    at = lanes(c)
    normed, mean, inverse = normalize(r.x[:, at].astype(F32))
    r.rows1[0:1, at] = mean
    r.rows1[1:2, at] = inverse
    h1 = (normed * r.small[:, 4:5] + r.small[:, 5:6]).astype(BF16)
    r.h1[:, at] = h1
    projected = dot(r.wqkv[...], h1) + r.cols[0:576, 1:2]
    cosine, sine = r.cos[:, at], r.sin[:, at]
    query = turn_by(projected[0:192], cosine, sine)
    key = turn_by(projected[192:384], cosine, sine)
    value = projected[384:576]
    r.qk[0:192, at] = query.astype(BF16)
    r.qk[192:384, at] = key.astype(BF16)
    r.v[:, at] = value.astype(BF16)
    r.kn[at, :] = jnp.transpose(key).astype(BF16)
    r.vn[at, :] = jnp.transpose(value).astype(BF16)


def tile_mask(r, tile, start, width):
    window = pl.ds(pl.multiple_of(start, 16), width)
    allowed = r.kcol[window, :] == r.info[4:5, tile_lanes(tile)]
    return jnp.where(allowed, 0.0, -1e30)


def repeat(mask, values):
    return jnp.concatenate([mask] * (values.shape[1] // TILE), axis=1)


def head_groups(width):
    return [(0, 1, 2)] if width <= NARROW else [(0,), (1,), (2,)]


def attend_tile(r, spot, tile, start, width, values):
    window = pl.ds(pl.multiple_of(start, 16), width)
    at = tile_lanes(tile)
    queries = block_diagonal(r.qk[0:192, at] * BF16(0.125))
    mask = tile_mask(r, tile, start, width)
    for heads in head_groups(width):
        span = slice(TILE * heads[0], TILE * heads[-1] + TILE)
        scores = dot(r.kn[window, :], queries[:, span])
        scores = scores + repeat(mask, scores)
        top = jnp.max(scores, axis=0, keepdims=True)
        exponent = jnp.exp(scores - top)
        total = jnp.sum(exponent, axis=0, keepdims=True)
        probs = (exponent * (1.0 / total)).astype(BF16)
        out = from_diagonal(dot(values, probs), heads).astype(BF16)
        r.att[head_rows(spot, heads), at] = out
        r.lse[tile, :, span] = jnp.broadcast_to(top + jnp.log(total), (8, span.stop - span.start))


def head_rows(spot, heads):
    return pl.ds(pl.multiple_of(OWN * spot.mp + 64 * heads[0], 16), 64 * len(heads))


def key_blocks(width):
    count = -(-width // 384)
    size = -(-width // (16 * count)) * 16
    return [(at, min(size, width - at)) for at in range(0, width, size)]


def back_tile(r, spot, tile, start, width, keys):
    at = tile_lanes(tile)
    queries = block_diagonal(r.qk[0:192, at] * BF16(0.125))
    grad_rows = dot(r.wout[...], r.gatt[:, at]).astype(BF16)
    grads = block_diagonal(grad_rows)
    product = grad_rows.astype(F32) * r.atto[:, at].astype(F32)
    centers = [jnp.sum(product[64 * h : 64 * h + 64], axis=0, keepdims=True) for h in range(3)]
    for heads in head_groups(width):
        span = slice(TILE * heads[0], TILE * heads[-1] + TILE)
        query, grad = queries[:, span], grads[:, span]
        center = jnp.concatenate([centers[h] for h in heads], axis=1)
        log = r.lse[tile, 0:1, span]
        parts = []
        for offset, size in key_blocks(width):
            window = pl.ds(pl.multiple_of(start + offset, 16), size)
            mask = tile_mask(r, tile, start + offset, size)
            scores = dot(r.kn[window, :], query)
            probs = jnp.exp(scores + repeat(mask, scores) - log)
            g_probs = dot(r.vn[window, :], grad)
            g_scores = (probs * (g_probs - center)).astype(BF16)
            r.dv[window, :] += dot(probs.astype(BF16), grad, NT)
            r.dk[window, :] += dot(g_scores, query, NT)
            parts.append(g_scores)
        g_scores = jnp.concatenate(parts, axis=0)
        rows = slice(64 * heads[0], 64 * heads[-1] + 64)
        r.dq[rows, at] = (from_diagonal(dot(keys, g_scores), heads) * 0.125).astype(BF16)


def mlp_forward(r, spot, c, outward):
    at = lanes(c)
    mid = r.x[:, at].astype(F32) + (dot(r.wot[...], r.att[:, at]) + r.small[:, 8:9])
    normed, mean, inverse = normalize(mid)
    r.work[...] = mid
    r.mido[:, at] = r.work[feat(spot.mp), :]
    r.rows2[0:1, at] = mean
    r.rows2[1:2, at] = inverse
    h2 = (normed * r.small[:, 6:7] + r.small[:, 7:8]).astype(BF16)
    r.h2[:, at] = h2
    hidden = dot(r.wupt[...], h2) + r.cols[:, 0:1]
    lower, density = phi_parts(hidden)
    active = (hidden * lower).astype(BF16)
    r.act[:, at] = active
    r.gpre[:, at] = (lower + hidden * density).astype(BF16)
    outward.give(c, dot(r.wdnt[...], active))


def give_gradient(r, c, sums, grad, gain, bias, low):
    at = lanes(c)
    r.stats[0, 0:1, at] = jnp.sum(grad * gain, axis=0, keepdims=True)
    r.stats[0, 1:2, at] = jnp.sum(grad * (low[:, at].astype(F32) - bias), axis=0, keepdims=True)
    sums.give(c, grad)


def mlp_backward(r, c, sums):
    at = lanes(c)
    g_act = dot(r.wdn[...], r.gout[:, at])
    g_pre = (g_act * r.gpre[:, at].astype(F32)).astype(BF16)
    r.gpre[:, at] = g_pre
    give_gradient(r, c, sums, dot(r.wup[...], g_pre), r.small[:, 6:7], r.small[:, 7:8], r.h2)


def second_norm_back(r, spot, c, sums):
    at = lanes(c)
    grad = sums.take(c)
    means = sums.take_stats(c)
    normed = (r.mido[:, at] - r.rows2[0:1, at]) * r.rows2[1:2, at]
    r.sg2[...] += fold(grad * normed)
    r.sb2[...] += fold(grad)
    back = r.rows2[1:2, at] * (
        grad * r.cols[0:192, 6:7] - means[0:1, :] - normed * means[1:2, :]
    )
    g_att = (r.gout[feat(spot.mp), at].astype(F32) + back).astype(BF16)
    r.gatt[feat(spot.mp), at] = g_att
    r.sbo[...] += fold(g_att.astype(F32))


def unrotate(r, c):
    at = lanes(c)
    cosine, sine = r.cos[:, at], r.sin[:, at]
    g_query = r.dq[0:192, at].astype(F32)
    g_key = jnp.transpose(r.dk[at, :]).astype(BF16).astype(F32)
    g_value = jnp.transpose(r.dv[at, :]).astype(BF16)
    plain = [turn_by(g, cosine, -sine).astype(BF16) for g in (g_query, g_key)]
    r.gproj[0:576, at] = jnp.concatenate(plain + [g_value], axis=0)
    angle = []
    for h in range(3):
        total = 0.0
        for part, g in enumerate((g_query, g_key)):
            rotated = r.qk[192 * part : 192 * part + 192, at].astype(F32)
            a, b = slice(64 * h, 64 * h + 32), slice(64 * h + 32, 64 * h + 64)
            total = total + (g[b] * rotated[a] - g[a] * rotated[b])
        angle.append(total)
    angle = jnp.concatenate(angle, axis=0)
    r.sf0[...] += fold(angle * r.info[0:1, at])
    r.sf1[...] += fold(angle * r.info[1:2, at])


def first_part(r, c, sums):
    grad = dot(r.wqkvn[:, 0:576], r.gproj[0:576, lanes(c)])
    give_gradient(r, c, sums, grad, r.small[:, 4:5], r.small[:, 5:6], r.h1)


def first_norm_back(r, spot, c, sums):
    at = lanes(c)
    grad = sums.take(c)
    means = sums.take_stats(c)
    own = feat(spot.mp)
    normed = (r.x[own, at].astype(F32) - r.rows1[0:1, at]) * r.rows1[1:2, at]
    r.sg1[...] += fold(grad * normed)
    r.sb1[...] += fold(grad)
    back = r.rows1[1:2, at] * (
        grad * r.cols[0:192, 4:5] - means[0:1, :] - normed * means[1:2, :]
    )
    r.igrad[:, at] = r.gatt[own, at].astype(F32) + back


def kernel(r, spot):
    peers = [dp_partner(spot, bit) for bit in range(r.dp_bits)]
    both = [flipped(spot, bits, 3) for bits in r.groups if len(bits) == 2]
    greeted = [spot.sib, spot.yp] + peers + both
    greet(greeted)
    token_load = pltpu.make_async_copy(r.tok, r.out, r.load_sem.at[4])
    token_load.start()
    cot_load = pltpu.make_async_copy(r.cot, r.out, r.load_sem.at[5])
    loads = Refs()
    for n, (name, source) in enumerate(
        dict(wqkv=r.in_wqkv, wup=r.in_wup, wdn=r.in_wdn, wout=r.in_wout).items()
    ):
        setattr(loads, name, pltpu.make_async_copy(source, getattr(r, name), r.load_sem.at[n]))
        getattr(loads, name).start()
    own = feat(spot.mp)
    here, there = r.small.at[own], r.small.at[feat(spot.yp_mp)]
    small_y = remote(r.cols.at[0:192], here, r.sm_sem.at[0], r.sm_sem.at[1], spot.yp)
    small_c = remote(r.cols.at[0:192], here, r.sm_sem.at[2], r.sm_sem.at[3], spot.sib)
    small_f = remote(there, there, r.sm_sem.at[4], r.sm_sem.at[5], spot.sib)

    def count_copy(bit):
        return remote(
            r.cnts.at[bit], r.cntr.at[bit], r.cn_sem.at[0, bit], r.cn_sem.at[1, bit], peers[bit]
        )

    def count_step(bit):
        count_copy(bit).wait()
        if bit + 1 < r.dp_bits:
            r.cnts[bit + 1] = r.cnts[bit] + r.cntr[bit]
            count_copy(bit + 1).start()

    tokens = Spread(spot, r.x, r.tk_sem)
    attended = Spread(spot, r.att, r.at_sem)
    cotangents = Spread(spot, r.gout, r.ct_sem)
    r.x[own, ROWS - 64 : LANES] = jnp.zeros((OWN, 128), BF16)
    r.gout[own, ROWS - 64 : LANES] = jnp.zeros((OWN, 128), BF16)
    token_load.wait()
    r.x[own, 0:ROWS] = r.out[...]
    cot_load.start()
    meet(greeted)
    tokens.to_y(0).start()
    row_tables(r)
    r.small[own, :] = r.cols[0:192, :]
    r.cnts[0] = r.cnt[...]
    small_y.start()
    count_copy(0).start()
    for c in range(1, CHUNKS):
        tokens.to_y(c).start()
    small_c.start()
    for c in range(CHUNKS):
        tokens.to_sib(c).start()
    loads.wout.wait()
    wo_here = r.wof.at[own]
    wo_there = r.wof.at[feat(spot.yp_mp)]
    wo_y = remote(r.wout, wo_here, r.wo_sem.at[0], r.wo_sem.at[1], spot.yp)
    wo_c = remote(r.wout, wo_here, r.wo_sem.at[2], r.wo_sem.at[3], spot.sib)
    wo_f = remote(wo_there, wo_there, r.wo_sem.at[4], r.wo_sem.at[5], spot.sib)
    wo_y.start()
    wo_c.start()
    r.wof[own, :] = r.wout[...]
    angle_tables(r)
    small_y.wait()
    small_f.start()
    cot_load.wait()
    r.gout[own, 0:ROWS] = (r.out[...].astype(F32) * r.info[2:3, 0:ROWS]).astype(BF16)
    for c in range(2):
        cotangents.send(c)
    count_step(0)
    loads.wup.wait()
    flip(r.wup, r.wupt)
    count_step(1)
    for ref in (r.sg1, r.sb1, r.sg2, r.sb2, r.sbo, r.sf0, r.sf1, r.dk, r.dv):
        ref[...] = jnp.zeros_like(ref)
    loads.wdn.wait()
    flip(r.wdn, r.wdnt)
    loads.wqkv.wait()
    small_c.wait()
    small_f.wait()
    tokens.relay(0)

    def window(source, j):
        start = 576 * j - 32 * (j // 2)
        r.win[j, :, 0:NARROW] = source[:, start : start + NARROW]

    def both_tiles(c, tile, source):
        def narrow(t):
            j = t // 5
            tile(r, spot, t, 576 * j - 32 * (j // 2), NARROW, r.win[j, :, 0:NARROW])

        @pl.when((c != 2) & (c != 4))
        def _():
            narrow(2 * c)
            narrow(2 * c + 1)

        @pl.when(c == 2)
        def _():
            tile(r, spot, 4, 0, 1152, source[:, 0:1152])
            narrow(5)

        @pl.when(c == 4)
        def _():
            narrow(8)
            tile(r, spot, 9, 976, 752, source[:, 976:1728])

    def attention(n, carry):
        @pl.when(n < CHUNKS)
        def _():
            @pl.when(n + 1 < CHUNKS)
            def _():
                tokens.relay(n + 1)

            tokens.arrived(n)
            project(r, n)

        for j in range(3):

            @pl.when(n == 2 * j + 2)
            def _():
                window(r.v, j)

        @pl.when(n >= 2)
        def _():
            both_tiles(n - 2, attend_tile, r.v)
            attended.send(n - 2)

        @pl.when(n == CHUNKS)
        def _():
            wo_y.wait()
            wo_f.start()

        return carry

    lax.fori_loop(0, CHUNKS + 2, attention, 0)
    for c in range(2, CHUNKS):
        cotangents.send(c)
    for bit in range(2, r.dp_bits):
        count_step(bit)
    last = r.dp_bits - 1
    total = r.cnts[last] + r.cntr[last]
    low, high = total[:, 0:1], total[:, 1:2]
    own_low = 1.0 - r.group[0].astype(F32)
    share = (own_low * low + (1.0 - own_low) * high) / (low + high)
    r.share[...] = jnp.broadcast_to(share, (8, 128))

    r.atto[...] = r.att[own, :]
    attended.relay(0)
    wo_c.wait()
    wo_f.wait()
    flip(r.wof, r.wot)

    outward = Exchange(r, spot, r.mp, r.mr, r.ms, r.mc, r.mo_sem)
    second = Exchange(r, spot, r.gp, r.gr, r.gs, r.gc, r.g2_sem, r.stats)
    g_att = Spread(spot, r.gatt, r.ga_sem)

    def halves(acc, arrive, res, sems):
        rows = acc.shape[0] // 2
        return [
            Reduce(
                spot,
                acc.at[rows * n : rows * n + rows],
                arrive[n],
                res.at[rows * n : rows * n + rows],
                r.groups,
                sems.at[n],
            )
            for n in range(2)
        ]

    down = halves(r.accdn, r.ardn, r.resdn, r.dn_sem)
    up = halves(r.accup, r.arup, r.resup, r.up_sem)

    pieces = down + up

    def advance(numbers):
        for number in numbers:
            if number < len(pieces):
                pieces[number].advance()

    def slots(table, n):
        for at in sorted(table):

            @pl.when(n == at)
            def _():
                advance(table[at])

    def norm_step(c):
        second_norm_back(r, spot, c, second)
        g_att.send(c)

    def forward(n, carry):
        @pl.when(n + 1 < CHUNKS)
        def _():
            attended.relay(n + 1)

        attended.arrived(n)
        mlp_forward(r, spot, n, outward)
        return carry

    lax.fori_loop(0, CHUNKS, forward, 0)
    cotangents.relay(0)

    def backward(n, carry):
        @pl.when(n < EARLY)
        def _():
            cotangents.relay(n + 1)
            cotangents.arrived(n)

        mlp_backward(r, n, second)

        @pl.when(n >= 1)
        def _():
            second.pass_on(n - 1)

        @pl.when(n >= 4)
        def _():
            norm_step(n - 4)

        return carry

    def late_backward(n, carry):
        backward(n, carry)
        slots(IN_BACKWARD, n)
        return carry

    lax.fori_loop(0, EARLY, backward, 0)
    for c in range(EARLY + 1, CHUNKS):
        cotangents.relay(c)
    for c in range(EARLY, CHUNKS):
        cotangents.arrived(c)
    r.accdn[...] = (dot(r.act[...], r.gout[...], NT) * r.share[0:1, 0:1]).astype(BF16)
    down[0].start()
    down[1].start()
    lax.fori_loop(EARLY, CHUNKS, late_backward, 0)
    second.pass_on(CHUNKS - 1)
    r.accup[...] = (dot(r.h2[...], r.gpre[...], NT) * r.share[0:1, 0:1]).astype(BF16)
    up[0].start()
    up[1].start()
    norm_step(3)
    advance(AT_END.get(5, ()))
    flip(r.wqkv, r.wqkvn)
    for j in range(3):
        window(r.qk.at[192:384], j)
    first = Exchange(r, spot, r.gp, r.gr, r.gs, r.gc, r.g1_sem, r.stats)
    g_att.relay(0)

    def first_chunks(chunks):
        def one(c, carry):
            unrotate(r, c)
            first_part(r, c, first)
            return carry

        lax.fori_loop(chunks[0], chunks[-1] + 1, one, 0)

    def back(c, carry):
        @pl.when(c + 4 < CHUNKS)
        def _():
            norm_step(c + 4)

        @pl.when(c + 1 < CHUNKS)
        def _():
            g_att.relay(c + 1)

        g_att.arrived(c)

        slots(BEFORE_TILES, c)
        both_tiles(c, back_tile, r.qk.at[192:384])
        slots(AFTER_TILES, c)

        @pl.when((c >= 1) & (c <= 5))
        def _():
            outward.pass_on(c - 1)

        @pl.when(c == 2)
        def _():
            first_chunks((0, 1))

        @pl.when(c == 3)
        def _():
            first.pass_on(0)
            first.pass_on(1)

        @pl.when(c == 4)
        def _():
            first_chunks((2, 3))

        @pl.when(c == 5)
        def _():
            first.pass_on(2)
            first.pass_on(3)

        return carry

    lax.fori_loop(0, CHUNKS, back, 0)
    first_chunks((4, 5, 6))
    r.accqkv[...] = (dot(r.gproj[0:576, :], r.h1[...], NT) * r.share[0:1, 0:1]).astype(BF16)
    qkv = [
        Reduce(
            spot,
            r.accqkv.at[OWN * n : OWN * n + OWN],
            r.arqkv[n],
            r.resqkv.at[OWN * n : OWN * n + OWN],
            r.groups if n < 2 else r.turned,
            r.qr_sem.at[n],
        )
        for n in range(3)
    ]
    for reduce in qkv:
        reduce.start()
    pieces += qkv
    advance(AT_END.get(0, ()))
    for c in range(4, CHUNKS):
        first.pass_on(c)
    r.accwo[...] = (dot(r.atto[...], r.gatt[...], NT) * r.share[0:1, 0:1]).astype(BF16)
    out = Reduce(spot, r.accwo, r.arwo, r.reswo, r.turned, r.wr_sem)
    out.start()
    pieces.append(out)
    outward.pass_on(5)
    outward.pass_on(6)
    advance(AT_END.get(1, ()))

    def norm_one(c, carry):
        first_norm_back(r, spot, c, first)
        return carry

    lax.fori_loop(0, 2, norm_one, 0)
    advance(AT_END.get(2, ()))
    lax.fori_loop(2, 5, norm_one, 0)
    advance(AT_END.get(3, ()))
    lax.fori_loop(5, CHUNKS, norm_one, 0)
    advance(AT_END.get(4, ()))

    def lane_sum(ref):
        return jnp.sum(ref[...], axis=1, keepdims=True)

    b_down = jnp.sum(r.gout[own, :].astype(F32), axis=1, keepdims=True)
    b_qkv = jnp.sum(r.gproj[0:576, :].astype(F32), axis=1, keepdims=True)
    columns = [
        jnp.sum(r.gpre[...].astype(F32), axis=1, keepdims=True),
        jnp.concatenate([b_qkv, lane_sum(r.sf0), lane_sum(r.sf1)], axis=0),
        jnp.concatenate([lane_sum(r.sbo), lane_sum(r.sg1), lane_sum(r.sb1), lane_sum(r.sg2)], axis=0),
        jnp.concatenate([lane_sum(r.sb2), b_down, jnp.zeros((384, 1), F32)], axis=0),
    ]
    lane = lax.broadcasted_iota(jnp.int32, (D, 128), 1)
    table = jnp.zeros((D, 128), F32)
    for n, column in enumerate(columns):
        table = jnp.where(lane == n, column, table)
    table = jnp.transpose(table * r.share[0:1, 0:1])[0:8, :]
    for step, bits in enumerate(r.groups):
        r.sumx[step] = table
        copies = [
            remote(
                r.sumx.at[step],
                r.sumr.at[step, number - 1],
                r.su_sem.at[0, step, number - 1],
                r.su_sem.at[1, step, number - 1],
                flipped(spot, bits, number),
            )
            for number in range(1, 1 << len(bits))
        ]
        for copy in copies:
            copy.start()
        if step < len(IN_SUMS):
            advance(IN_SUMS[step])
        for number, copy in enumerate(copies):
            copy.wait()
            table = table + r.sumr[step, number]
    r.sums[...] = table
    finish_out(r, spot, outward)
    while any(piece.at < len(piece.phases) for piece in pieces):
        advance(range(len(pieces)))


def finish_out(r, spot, outward):
    for c in range(CHUNKS):
        at = lanes(c)
        total = outward.take(c)
        whole = r.mido[:, at] + (total + r.cols[0:192, 9:10])
        r.gs[:, at] = (r.info[2:3, at] * whole).astype(BF16)
    r.out[...] = r.gs[:, 0:ROWS]


def dma(*shape):
    return pltpu.SemaphoreType.DMA(shape)


def run(dp_bits, **arrays):
    scalars = ("group",)
    on_demand = ("tok", "cot", "in_wqkv", "in_wup", "in_wdn", "in_wout")
    outs = dict(
        out=((OWN, ROWS), BF16),
        igrad=((OWN, LANES), F32),
        resdn=((D, D), BF16),
        resup=((D, D), BF16),
        reswo=((OWN, D), BF16),
        resqkv=((576, D), BF16),
        sums=((8, D), F32),
    )

    groups = [(bit,) for bit in range(dp_bits)]
    turned = groups[1:] + groups[:1]

    def levels(rows):
        steps = plan((rows, D), groups)
        return [VM(((1 << len(bits)) - 1, *shape), BF16) for bits, shape, _ in steps]

    full = VM((D, LANES), BF16)
    own = VM((OWN, LANES), BF16)
    square = VM((D, D), BF16)
    spread = dma(6, CHUNKS)
    scratch = dict(
        x=full,
        h1=full,
        qk=VM((384, LANES), BF16),
        v=own,
        kn=VM((LANES, OWN), BF16),
        vn=VM((LANES, OWN), BF16),
        cos=VM((96, LANES), F32),
        sin=VM((96, LANES), F32),
        kcol=VM((LANES, TILE), F32),
        win=VM((3, OWN, 640), BF16),
        lse=VM((TILES, 8, 384), F32),
        small=VM((D, 128), F32),
        share=VM((8, 128), F32),
        att=full,
        gout=full,
        wqkv=VM((576, D), BF16),
        wup=square,
        wupt=square,
        wdn=square,
        wdnt=square,
        wout=VM((OWN, D), BF16),
        wof=square,
        wot=square,
        h2=full,
        act=full,
        gpre=full,
        work=VM((D, CHUNK), F32),
        mido=VM((OWN, LANES), F32),
        rows1=VM((8, LANES), F32),
        rows2=VM((8, LANES), F32),
        info=VM((8, LANES), F32),
        cols=VM((D, 128), F32),
        cnt=VM((8, 128), F32),
        stats=VM((4, 8, LANES), F32),
        mp=VM((2, 2, OWN, LANES), BF16),
        mr=VM((2, OWN, LANES), BF16),
        ms=own,
        mc=own,
        gp=VM((2, 2, OWN, LANES), BF16),
        gr=VM((2, OWN, LANES), BF16),
        gs=own,
        gc=own,
        dk=VM((LANES, OWN), F32),
        dv=VM((LANES, OWN), F32),
        ardn=[levels(384), levels(384)],
        arup=[levels(384), levels(384)],
        arwo=levels(OWN),
        arqkv=[levels(OWN), levels(OWN), levels(OWN)],
        sg1=VM((OWN, 128), F32),
        sb1=VM((OWN, 128), F32),
        sg2=VM((OWN, 128), F32),
        sb2=VM((OWN, 128), F32),
        sbo=VM((OWN, 128), F32),
        sf0=VM((96, 128), F32),
        sf1=VM((96, 128), F32),
        cnts=VM((dp_bits, 8, 128), F32),
        cntr=VM((dp_bits, 8, 128), F32),
        sumx=VM((len(groups), 8, D), F32),
        sumr=VM((len(groups), 3, 8, D), F32),
        load_sem=dma(6),
        tk_sem=spread,
        at_sem=spread,
        ct_sem=spread,
        ga_sem=spread,
        sm_sem=dma(6),
        wo_sem=dma(6),
        cn_sem=dma(2, dp_bits),
        su_sem=dma(2, len(groups), 3),
        mo_sem=dma(8, CHUNKS),
        g2_sem=dma(8, CHUNKS),
        g1_sem=dma(8, CHUNKS),
        dn_sem=dma(2, 2, 2 * dp_bits, 3),
        up_sem=dma(2, 2, 2 * dp_bits, 3),
        wr_sem=dma(2, 2 * dp_bits, 3),
        qr_sem=dma(3, 2, 2 * dp_bits, 3),
    )
    shapes, structure = jax.tree.flatten(scratch, is_leaf=lambda leaf: not isinstance(leaf, (dict, list)))

    def body(*refs):
        r = Refs()
        for name, ref in zip(list(arrays) + list(outs), refs):
            setattr(r, name, ref)
        named = jax.tree.unflatten(structure, refs[len(arrays) + len(outs) :])
        for name, ref in named.items():
            setattr(r, name, ref)
        r.gatt, r.atto = r.att, r.v
        r.dq, r.gproj = r.act, r.h2
        r.accdn, r.accup, r.accwo = r.wof, r.wupt, r.wdn.at[0:OWN]
        r.wqkvn = r.wot
        r.accqkv = r.wdnt.at[0:576]
        r.dp_bits, r.groups, r.turned = dp_bits, groups, turned
        kernel(r, place())

    results = pl.pallas_call(
        body,
        out_shape=[jax.ShapeDtypeStruct(shape, dtype) for shape, dtype in outs.values()],
        in_specs=[
            pl.BlockSpec(
                memory_space=pl.ANY if name in on_demand else pltpu.SMEM if name in scalars else VM
            )
            for name in arrays
        ],
        out_specs=[pl.BlockSpec(memory_space=VM) for _ in outs],
        scratch_shapes=shapes,
        compiler_params=pltpu.CompilerParams(
            collective_id=1, has_side_effects=True, vmem_limit_bytes=64 * MIB - 65536
        ),
    )(*arrays.values())
    named = Refs()
    for name, result in zip(outs, results, strict=True):
        setattr(named, name, result)
    return named


def local(
    tokens,
    w_qkv,
    b_qkv,
    freqs,
    w_out,
    b_out,
    norm1_gain,
    norm1_bias,
    norm2_gain,
    norm2_bias,
    w_up,
    b_up,
    w_down,
    b_down,
    cotangent,
    keep_mask,
    coords,
    block_group,
):
    row_count, width_loc = tokens.shape
    heads_loc = freqs.shape[1]
    row = lax.broadcasted_iota(jnp.int32, (8, D), 0)
    pack = jnp.zeros((8, D), F32)
    vectors = (b_up, norm1_gain, norm1_bias, norm2_gain, norm2_bias, b_out, b_down)
    for n, vector in enumerate(vectors):
        wide = jnp.pad(vector.astype(F32), (0, D - vector.shape[0]))
        pack = jnp.where(row == n, wide[None, :], pack)

    a = run(
        lax.axis_size("dp").bit_length() - 1,
        tok=tokens.T,
        cot=cotangent.T,
        pack=pack,
        bqkv=b_qkv,
        freqs=freqs.transpose(1, 0, 2),
        keep=keep_mask.reshape(1, row_count),
        coords=coords,
        group=block_group,
        in_wqkv=w_qkv.transpose(1, 2, 0).reshape(3 * width_loc, D),
        in_wup=w_up,
        in_wdn=w_down,
        in_wout=w_out,
    )
    sums = a.sums
    grad_qkv = a.resqkv.astype(F32)
    half = (2, heads_loc, HEAD_DIM // 2)
    return (
        a.out.T,
        a.igrad[:, :row_count].T,
        grad_qkv.reshape(3, width_loc, D).transpose(2, 0, 1),
        sums[1, : 3 * width_loc].reshape(3, width_loc),
        sums[1, 3 * width_loc :].reshape(half),
        a.reswo.astype(F32),
        sums[2, 0:192],
        sums[2, 192:384],
        sums[2, 384:576],
        sums[2, 576:768],
        sums[3, 0:192],
        a.resup.astype(F32),
        sums[0],
        a.resdn.astype(F32),
        sums[3, 192:384],
    )


def solution(mesh):
    return jax.shard_map(
        local,
        mesh=mesh,
        in_specs=(
            P("dp", "mp"),
            P(None, None, "mp"),
            P(None, "mp"),
            P(None, "mp", None),
            P("mp", None),
            P("mp"),
            P("mp"),
            P("mp"),
            P("mp"),
            P("mp"),
            P(None, "mp"),
            P("mp"),
            P("mp", None),
            P("mp"),
            P("dp", "mp"),
            P("dp"),
            P(None, "dp"),
            P("dp"),
        ),
        out_specs=(
            P("dp", "mp"),
            P("dp", "mp"),
            P(None, None, "mp"),
            P(None, "mp"),
            P(None, "mp", None),
            P("mp", None),
            P("mp"),
            P("mp"),
            P("mp"),
            P("mp"),
            P("mp"),
            P(None, "mp"),
            P("mp"),
            P("mp", None),
            P("mp"),
        ),
        check_vma=False,
    )
```

```python
import jax
import jax.numpy as jnp
from jax import lax
from jax.experimental import pallas as pl
from jax.experimental.pallas import tpu as pltpu
from jax.sharding import PartitionSpec as P

HEAD_DIM = 64
GRID_LO = 14
SLOTS = 576

MESH = pl.DeviceIdType.MESH
MIB = 1024 * 1024
VM = pltpu.VMEM
F32 = jnp.float32
BF16 = jnp.bfloat16
NT = (((1,), (1,)), ((), ()))
NN = (((1,), (0,)), ((), ()))

D = 768
OWN = 192
ROWS = 1728
LANES = 1792
CHUNK = 256
CHUNKS = LANES // CHUNK
TILE = 128
TILES = LANES // TILE
NARROW = 608

norm_eps = 1e-06
root_half = 0.7071067811865476
inv_root_two_pi = 0.3989422804014327


EARLY = 2
IN_BACKWARD, BEFORE_TILES, AFTER_TILES, IN_LAST, TAIL = range(5)
MOVES = (
    {6: (0,)},
    {0: (1, 0), 2: (1,), 3: (3, 2), 5: (2,)},
    {1: (2,), 2: (0,), 3: (1,), 4: (0, 3), 5: (1,), 6: (0,)},
    {0: (3, 2, 1), 1: (0,), 4: (6, 4), 5: (7, 5), 6: (3,)},
)
IN_TAIL = (9, 2, 9, 9, 9, 9, 9, 9, 6, 1, 4, 8, 7, 5, 3, 2, 6, 8, 4, 7, 5, 8, 4, 3, 5, 6, 7, 4, 5, 6, 4, 7, 5, 6, 7)


def numbered_moves():
    points = [(IN_BACKWARD, n) for n in range(CHUNKS)]
    for c in range(CHUNKS):
        points += [(BEFORE_TILES, c), (AFTER_TILES, c)]
    points += [(IN_LAST, n) for n in range(CHUNKS)]
    taken = [0] * 9
    moves = {}
    for kind, n in points:
        for piece in MOVES[kind].get(n, ()):
            moves.setdefault((kind, n), []).append((piece, taken[piece]))
            taken[piece] += 1
    tail = []
    for piece in IN_TAIL:
        if piece < 9:
            tail.append((piece, taken[piece]))
            taken[piece] += 1
        else:
            tail.append((piece, 0))
    return moves, tail, taken


class Refs:
    pass


def dot(left, right, dims=NN):
    return lax.dot_general(left, right, dims, preferred_element_type=F32)


def remote(src, dst, send, recv, device):
    return pltpu.make_async_remote_copy(
        src_ref=src, dst_ref=dst, send_sem=send, recv_sem=recv, device_id=device, device_id_type=MESH
    )


def place():
    spot = Refs()
    spot.dp = lax.axis_index("dp")
    spot.mp = lax.axis_index("mp")
    spot.y = spot.mp // 2
    spot.c = spot.mp % 2
    spot.sib_mp = 2 * spot.y + 1 - spot.c
    spot.yp_mp = 2 * (1 - spot.y) + spot.c
    spot.sib = (spot.dp, spot.sib_mp)
    spot.yp = (spot.dp, spot.yp_mp)
    return spot


def greet(devices):
    barrier = pltpu.get_barrier_semaphore()
    for device in devices:
        pl.semaphore_signal(barrier, inc=1, device_id=device, device_id_type=MESH)


def meet(devices):
    pl.semaphore_wait(pltpu.get_barrier_semaphore(), len(devices))


def dp_partner(spot, bit):
    mine = (spot.dp // (1 << bit)) % 2
    return (spot.dp + (1 - 2 * mine) * (1 << bit), spot.mp)


def feat(j):
    return pl.ds(pl.multiple_of(OWN * j, 16), OWN)


def lanes(c):
    return pl.ds(pl.multiple_of(c * CHUNK, CHUNK), CHUNK)


def tile_lanes(t):
    return pl.ds(pl.multiple_of(t * TILE, TILE), TILE)


def flipped(spot, bits, number):
    dp = spot.dp
    for n, bit in enumerate(bits):
        if (number >> n) & 1:
            dp = dp + (1 - 2 * ((spot.dp // (1 << bit)) % 2)) * (1 << bit)
    return (dp, spot.mp)


def cut(shape):
    rows, cols = shape
    if (rows // 2) % 16 == 0:
        return (rows // 2, cols)
    if (cols // 2) % 128 == 0:
        return (rows, cols // 2)
    return shape


def plan(shape, groups):
    steps = []
    for bits in groups:
        after = shape
        for _ in bits:
            after = cut(after)
        whole = cut(cut(shape)) if len(bits) == 2 else cut(shape)
        if len(bits) == 2 and cut(shape) == cut(cut(shape)):
            for bit in bits:
                now = cut(shape)
                steps.append(((bit,), now, now != shape))
                shape = now
            continue
        steps.append((bits, whole, whole != shape))
        shape = after
    return steps


class Reduce:
    def __init__(self, spot, acc, arrive, res, groups, sems):
        self.spot, self.res, self.sems = spot, res, sems
        self.phases = []
        gathers = []
        source, row, col = acc, 0, 0
        steps = plan(acc.shape, groups)
        shape = acc.shape
        for (bits, after, differ), target in zip(steps, arrive, strict=True):
            corners = []
            for number in range(1 << len(bits)):
                at, part = (0, 0), shape
                for n, bit in enumerate(bits):
                    smaller = cut(part)
                    mine = (spot.dp // (1 << bit)) % 2
                    side = 1 - mine if (number >> n) & 1 else mine
                    if smaller[0] < part[0]:
                        at = (at[0] + side * smaller[0], at[1])
                    elif smaller[1] < part[1]:
                        at = (at[0], at[1] + side * smaller[1])
                    part = smaller
                corners.append(at)
            row, col = row + corners[0][0], col + corners[0][1]
            self.phases.append((bits, source, corners, after, target))
            if differ:
                gathers.append((bits, res, (row, col), after, None))
            source, shape = target.at[0], after
        self.own = (row, col)
        self.sums = len(self.phases)
        self.phases += gathers[::-1]

    def piece(self, ref, corner, shape):
        def span(start, size, unit, whole):
            if size == whole:
                return pl.ds(0, size)
            return pl.ds(pl.multiple_of(start, unit), size)

        return ref.at[
            span(corner[0], shape[0], 16, ref.shape[0]), span(corner[1], shape[1], 128, ref.shape[1])
        ]

    def copies(self, at):
        bits, source, corners, shape, target = self.phases[at]
        out = []
        for number in range(1, 1 << len(bits)):
            if target is None:
                piece = self.piece(source, corners, shape)
                goal = piece
            else:
                piece = self.piece(source, corners[number], shape)
                goal = target.at[number - 1]
            sems = (self.sems.at[0, at, number - 1], self.sems.at[1, at, number - 1])
            out.append(remote(piece, goal, *sems, flipped(self.spot, bits, number)))
        return out

    def start(self, at=0):
        for copy in self.copies(at):
            copy.start()

    def add(self, at):
        bits, source, corners, shape, target = self.phases[at]
        held = self.piece(source, corners[0], shape)
        last = at == self.sums - 1
        goal = self.piece(self.res, self.own, shape) if last else target.at[0]
        step = 48 if shape[0] % 48 == 0 else 16

        def block(i, carry):
            rows = pl.ds(pl.multiple_of(i * step, 16), step)
            total = held[rows, :].astype(F32)
            for n in range((1 << len(bits)) - 1):
                total = total + target[n, rows, :].astype(F32)
            goal[rows, :] = total.astype(BF16)
            return carry

        lax.fori_loop(0, shape[0] // step, block, 0)

    def advance(self, at):
        if at >= len(self.phases):
            return
        for copy in self.copies(at):
            copy.wait()
        if at < self.sums:
            self.add(at)
        if at + 1 < len(self.phases):
            self.start(at + 1)


class Exchange:
    def __init__(self, r, spot, part, arrive, out, come, sems, stats=None):
        self.r, self.spot = r, spot
        self.part, self.arrive, self.out, self.come = part, arrive, out, come
        self.sems, self.stats = sems, stats

    def core(self, c):
        at = lanes(c)
        copies = [
            remote(
                self.part.at[:, 1 - self.spot.c, :, at],
                self.arrive.at[:, :, at],
                self.sems.at[0, c],
                self.sems.at[1, c],
                self.spot.sib,
            )
        ]
        if self.stats is not None:
            copies.append(
                remote(
                    self.stats.at[0, :, at],
                    self.stats.at[1, :, at],
                    self.sems.at[2, c],
                    self.sems.at[3, c],
                    self.spot.sib,
                )
            )
        return copies

    def over(self, c):
        at = lanes(c)
        copies = [
            remote(
                self.out.at[:, at],
                self.come.at[:, at],
                self.sems.at[4, c],
                self.sems.at[5, c],
                self.spot.yp,
            )
        ]
        if self.stats is not None:
            copies.append(
                remote(
                    self.stats.at[2, :, at],
                    self.stats.at[3, :, at],
                    self.sems.at[6, c],
                    self.sems.at[7, c],
                    self.spot.yp,
                )
            )
        return copies

    def give(self, c, values):
        at = lanes(c)
        for j in range(4):
            self.part[j // 2, j % 2, :, at] = values[OWN * j : OWN * j + OWN].astype(BF16)
        for copy in self.core(c):
            copy.start()

    def pass_on(self, c):
        at = lanes(c)
        for copy in self.core(c):
            copy.wait()
        away = 1 - self.spot.y
        self.out[:, at] = (
            self.part[away, self.spot.c, :, at].astype(F32) + self.arrive[away, :, at].astype(F32)
        ).astype(BF16)
        if self.stats is not None:
            self.stats[2, :, at] = self.stats[0, :, at] + self.stats[1, :, at]
        for copy in self.over(c):
            copy.start()

    def take(self, c):
        at = lanes(c)
        for copy in self.over(c):
            copy.wait()
        home = self.spot.y
        return (
            self.part[home, self.spot.c, :, at].astype(F32)
            + self.arrive[home, :, at].astype(F32)
            + self.come[:, at].astype(F32)
        )

    def take_stats(self, c):
        at = lanes(c)
        return (self.stats[2, :, at] + self.stats[3, :, at]) * (1.0 / D)


class Spread:
    def __init__(self, spot, full, sems):
        self.spot, self.full, self.sems = spot, full, sems

    def piece(self, j, c, kind, device):
        part = self.full.at[feat(j), lanes(c)]
        return remote(part, part, self.sems.at[2 * kind, c], self.sems.at[2 * kind + 1, c], device)

    def to_y(self, c):
        return self.piece(self.spot.mp, c, 0, self.spot.yp)

    def to_sib(self, c):
        return self.piece(self.spot.mp, c, 1, self.spot.sib)

    def onward(self, c):
        return self.piece(self.spot.yp_mp, c, 2, self.spot.sib)

    def send(self, c):
        self.to_y(c).start()
        self.to_sib(c).start()

    def relay(self, c):
        self.to_y(c).wait()
        self.onward(c).start()

    def arrived(self, c):
        self.to_sib(c).wait()
        self.onward(c).wait()


def sin_cos(angle):
    turns = jnp.floor(angle * 0.6366197723675814 + 0.5)
    rest = angle - turns * 1.5703125
    rest = rest - turns * 4.837512969970703e-4
    rest = rest - turns * 7.549789948768648e-8
    square = rest * rest
    sine = rest + rest * square * (
        -1.6666654611e-1 + square * (8.3321608736e-3 + square * -1.9515295891e-4)
    )
    cosine = (
        1.0
        - 0.5 * square
        + square
        * square
        * (4.166664568298827e-2 + square * (-1.388731625493765e-3 + square * 2.443315711809948e-5))
    )
    quarter = turns - 4.0 * jnp.floor(turns * 0.25)
    odd = (quarter == 1.0) | (quarter == 3.0)
    sine_sign = jnp.where(quarter >= 2.0, -1.0, 1.0)
    cosine_sign = jnp.where((quarter == 1.0) | (quarter == 2.0), -1.0, 1.0)
    return (
        jnp.where(odd, cosine, sine) * sine_sign,
        jnp.where(odd, sine, cosine) * cosine_sign,
    )


def phi_parts(value):
    bell = jnp.exp(-0.5 * value * value)
    inner = 1.0 / (1.0 + (0.3275911 * root_half) * jnp.abs(value))
    series = 0.5 * 1.061405429
    for factor in (-1.453152027, 1.421413741, -0.284496736, 0.254829592):
        series = series * inner + 0.5 * factor
    beyond = series * inner * bell
    return (jnp.where(value >= 0.0, 1.0 - beyond, beyond), inv_root_two_pi * bell)


def normalize(values):
    mean = jnp.mean(values, axis=0, keepdims=True)
    square = jnp.mean(values * values, axis=0, keepdims=True)
    inverse = lax.rsqrt(square - mean * mean + norm_eps)
    return ((values - mean) * inverse, mean, inverse)


def turn_by(values, cosine, sine):
    out = []
    for h in range(3):
        front, rear = values[64 * h : 64 * h + 32], values[64 * h + 32 : 64 * h + 64]
        co, si = cosine[32 * h : 32 * h + 32], sine[32 * h : 32 * h + 32]
        out += [front * co - rear * si, front * si + rear * co]
    return jnp.concatenate(out, axis=0)


def block_diagonal(tile):
    zero = jnp.zeros((64, TILE), tile.dtype)
    parts = []
    for h in range(3):
        column = [zero, zero, zero]
        column[h] = tile[64 * h : 64 * h + 64]
        parts.append(jnp.concatenate(column, axis=0))
    return jnp.concatenate(parts, axis=1)


def from_diagonal(values, heads):
    return jnp.concatenate(
        [values[64 * h : 64 * h + 64, TILE * n : TILE * n + TILE] for n, h in enumerate(heads)], axis=0
    )


def fold(values):
    return values[:, :128] + values[:, 128:]


def row_tables(r):
    pad = jnp.zeros((1, D - 3 * OWN), F32)
    qkv = jnp.concatenate([r.bqkv[n : n + 1, :].astype(F32) for n in range(3)] + [pad], axis=1)
    pad = jnp.zeros((2, D - 96), F32)
    freqs = jnp.concatenate([r.freqs[h] for h in range(3)] + [pad], axis=1)
    table = jnp.concatenate(
        [r.pack[0:1, :], qkv, freqs, r.pack[1:8, :], jnp.zeros((117, D), F32)], axis=0
    )
    for i in range(D // 128):
        r.cols[128 * i : 128 * i + 128, :] = jnp.transpose(table[:, 128 * i : 128 * i + 128])
    low = 1.0 - r.group[0].astype(F32)
    keep = r.keep[...].astype(F32)
    middle = lax.broadcasted_iota(jnp.int32, (1, ROWS), 1).astype(F32) + 0.5
    segment = low * jnp.floor(middle * (1.0 / (GRID_LO * GRID_LO))) + (1.0 - low) * jnp.floor(
        middle * (1.0 / SLOTS)
    )
    r.info[...] = jnp.zeros_like(r.info)
    r.info[0:2, 0:ROWS] = r.coords[...].astype(F32)
    r.info[2:3, 0:ROWS] = keep
    r.info[3:4, 0:ROWS] = keep * (segment + 1.0) - 1.0
    r.info[4:5, 0:ROWS] = segment
    kept = jnp.sum(keep, axis=1, keepdims=True)
    lane = lax.broadcasted_iota(jnp.int32, (8, 128), 1)
    r.cnt[...] = kept * jnp.where(lane == 0, low, jnp.where(lane == 1, 1.0 - low, 0.0))


def angle_tables(r):
    def block(c, carry):
        at = lanes(c)
        angle = r.cols[0:96, 2:3] * r.info[0:1, at] + r.cols[0:96, 3:4] * r.info[1:2, at]
        sine, cosine = sin_cos(angle)
        r.cos[:, at] = cosine
        r.sin[:, at] = sine
        return carry

    lax.fori_loop(0, CHUNKS, block, 0)

    def column(t, carry):
        row = r.info[3:4, tile_lanes(t)]
        r.kcol[pl.ds(pl.multiple_of(t * TILE, TILE), TILE), :] = jnp.transpose(
            jnp.broadcast_to(row, (TILE, TILE))
        )
        return carry

    lax.fori_loop(0, TILES, column, 0)


def flip(source, goal):
    for i in range(source.shape[1] // 128):
        part = source[:, 128 * i : 128 * i + 128].astype(F32)
        goal[128 * i : 128 * i + 128, 0 : source.shape[0]] = jnp.transpose(part).astype(BF16)


def project(r, c):
    at = lanes(c)
    normed, mean, inverse = normalize(r.x[:, at].astype(F32))
    r.rows1[0:1, at] = mean
    r.rows1[1:2, at] = inverse
    h1 = (normed * r.small[:, 4:5] + r.small[:, 5:6]).astype(BF16)
    r.h1[:, at] = h1
    projected = dot(r.wqkv[...], h1) + r.cols[0:576, 1:2]
    cosine, sine = r.cos[:, at], r.sin[:, at]
    query = turn_by(projected[0:192], cosine, sine)
    key = turn_by(projected[192:384], cosine, sine)
    value = projected[384:576]
    r.qk[0:192, at] = query.astype(BF16)
    r.qk[192:384, at] = key.astype(BF16)
    r.v[:, at] = value.astype(BF16)
    r.kn[at, :] = jnp.transpose(key).astype(BF16)
    r.vn[at, :] = jnp.transpose(value).astype(BF16)


def tile_mask(r, tile, start, width):
    window = pl.ds(pl.multiple_of(start, 16), width)
    allowed = r.kcol[window, :] == r.info[4:5, tile_lanes(tile)]
    return jnp.where(allowed, 0.0, -1e30)


def repeat(mask, values):
    return jnp.concatenate([mask] * (values.shape[1] // TILE), axis=1)


def head_groups(width):
    return [(0, 1, 2)] if width <= NARROW else [(0,), (1,), (2,)]


def attend_tile(r, spot, tile, start, width, values):
    window = pl.ds(pl.multiple_of(start, 16), width)
    at = tile_lanes(tile)
    queries = block_diagonal(r.qk[0:192, at] * BF16(0.125))
    mask = tile_mask(r, tile, start, width)
    for heads in head_groups(width):
        span = slice(TILE * heads[0], TILE * heads[-1] + TILE)
        scores = dot(r.kn[window, :], queries[:, span])
        scores = scores + repeat(mask, scores)
        top = jnp.max(scores, axis=0, keepdims=True)
        exponent = jnp.exp(scores - top)
        total = jnp.sum(exponent, axis=0, keepdims=True)
        probs = (exponent * (1.0 / total)).astype(BF16)
        out = from_diagonal(dot(values, probs), heads).astype(BF16)
        r.att[head_rows(spot, heads), at] = out
        r.lse[tile, :, span] = jnp.broadcast_to(top + jnp.log(total), (8, span.stop - span.start))


def head_rows(spot, heads):
    return pl.ds(pl.multiple_of(OWN * spot.mp + 64 * heads[0], 16), 64 * len(heads))


def key_blocks(width):
    count = -(-width // 384)
    size = -(-width // (16 * count)) * 16
    return [(at, min(size, width - at)) for at in range(0, width, size)]


def back_tile(r, spot, tile, start, width, keys):
    at = tile_lanes(tile)
    queries = block_diagonal(r.qk[0:192, at] * BF16(0.125))
    grad_rows = dot(r.wout[...], r.gatt[:, at]).astype(BF16)
    grads = block_diagonal(grad_rows)
    product = grad_rows.astype(F32) * r.atto[:, at].astype(F32)
    centers = [jnp.sum(product[64 * h : 64 * h + 64], axis=0, keepdims=True) for h in range(3)]
    for heads in head_groups(width):
        span = slice(TILE * heads[0], TILE * heads[-1] + TILE)
        query, grad = queries[:, span], grads[:, span]
        center = jnp.concatenate([centers[h] for h in heads], axis=1)
        log = r.lse[tile, 0:1, span]
        parts = []
        for offset, size in key_blocks(width):
            window = pl.ds(pl.multiple_of(start + offset, 16), size)
            mask = tile_mask(r, tile, start + offset, size)
            scores = dot(r.kn[window, :], query)
            probs = jnp.exp(scores + repeat(mask, scores) - log)
            g_probs = dot(r.vn[window, :], grad)
            g_scores = (probs * (g_probs - center)).astype(BF16)
            r.dv[window, :] += dot(probs.astype(BF16), grad, NT)
            r.dk[window, :] += dot(g_scores, query, NT)
            parts.append(g_scores)
        g_scores = jnp.concatenate(parts, axis=0)
        rows = slice(64 * heads[0], 64 * heads[-1] + 64)
        r.dq[rows, at] = (from_diagonal(dot(keys, g_scores), heads) * 0.125).astype(BF16)


def mlp_forward(r, spot, c, outward):
    at = lanes(c)
    mid = r.x[:, at].astype(F32) + (dot(r.wot[...], r.att[:, at]) + r.small[:, 8:9])
    normed, mean, inverse = normalize(mid)
    r.work[...] = mid
    r.mido[:, at] = r.work[feat(spot.mp), :]
    r.rows2[0:1, at] = mean
    r.rows2[1:2, at] = inverse
    h2 = (normed * r.small[:, 6:7] + r.small[:, 7:8]).astype(BF16)
    r.h2[:, at] = h2
    hidden = dot(r.wupt[...], h2) + r.cols[:, 0:1]
    lower, density = phi_parts(hidden)
    active = (hidden * lower).astype(BF16)
    r.act[:, at] = active
    r.gpre[:, at] = (lower + hidden * density).astype(BF16)
    outward.give(c, dot(r.wdnt[...], active))


def give_gradient(r, c, sums, grad, gain, bias, low):
    at = lanes(c)
    r.stats[0, 0:1, at] = jnp.sum(grad * gain, axis=0, keepdims=True)
    r.stats[0, 1:2, at] = jnp.sum(grad * (low[:, at].astype(F32) - bias), axis=0, keepdims=True)
    sums.give(c, grad)


def mlp_backward(r, c, sums):
    at = lanes(c)
    g_act = dot(r.wdn[...], r.gout[:, at])
    g_pre = (g_act * r.gpre[:, at].astype(F32)).astype(BF16)
    r.gpre[:, at] = g_pre
    give_gradient(r, c, sums, dot(r.wup[...], g_pre), r.small[:, 6:7], r.small[:, 7:8], r.h2)


def second_norm_back(r, spot, c, sums):
    at = lanes(c)
    grad = sums.take(c)
    means = sums.take_stats(c)
    normed = (r.mido[:, at] - r.rows2[0:1, at]) * r.rows2[1:2, at]
    r.sg2[...] += fold(grad * normed)
    r.sb2[...] += fold(grad)
    back = r.rows2[1:2, at] * (
        grad * r.cols[0:192, 6:7] - means[0:1, :] - normed * means[1:2, :]
    )
    g_att = (r.gout[feat(spot.mp), at].astype(F32) + back).astype(BF16)
    r.gatt[feat(spot.mp), at] = g_att
    r.sbo[...] += fold(g_att.astype(F32))


def unrotate(r, c):
    at = lanes(c)
    cosine, sine = r.cos[:, at], r.sin[:, at]
    g_query = r.dq[0:192, at].astype(F32)
    g_key = jnp.transpose(r.dk[at, :]).astype(BF16).astype(F32)
    g_value = jnp.transpose(r.dv[at, :]).astype(BF16)
    plain = [turn_by(g, cosine, -sine).astype(BF16) for g in (g_query, g_key)]
    r.gproj[0:576, at] = jnp.concatenate(plain + [g_value], axis=0)
    angle = []
    for h in range(3):
        total = 0.0
        for part, g in enumerate((g_query, g_key)):
            rotated = r.qk[192 * part : 192 * part + 192, at].astype(F32)
            a, b = slice(64 * h, 64 * h + 32), slice(64 * h + 32, 64 * h + 64)
            total = total + (g[b] * rotated[a] - g[a] * rotated[b])
        angle.append(total)
    angle = jnp.concatenate(angle, axis=0)
    r.sf0[...] += fold(angle * r.info[0:1, at])
    r.sf1[...] += fold(angle * r.info[1:2, at])


def first_part(r, c, sums):
    grad = dot(r.wqkvn[:, 0:576], r.gproj[0:576, lanes(c)])
    give_gradient(r, c, sums, grad, r.small[:, 4:5], r.small[:, 5:6], r.h1)


def first_norm_back(r, spot, c, sums):
    at = lanes(c)
    grad = sums.take(c)
    means = sums.take_stats(c)
    own = feat(spot.mp)
    normed = (r.x[own, at].astype(F32) - r.rows1[0:1, at]) * r.rows1[1:2, at]
    r.sg1[...] += fold(grad * normed)
    r.sb1[...] += fold(grad)
    back = r.rows1[1:2, at] * (
        grad * r.cols[0:192, 4:5] - means[0:1, :] - normed * means[1:2, :]
    )
    r.igrad[:, at] = r.gatt[own, at].astype(F32) + back


def kernel(r, spot):
    peers = [dp_partner(spot, bit) for bit in range(r.dp_bits)]
    both = [flipped(spot, bits, 3) for bits in r.groups if len(bits) == 2]
    greeted = [spot.sib, spot.yp] + peers + both
    greet(greeted)
    token_load = pltpu.make_async_copy(r.tok, r.out, r.load_sem.at[4])
    token_load.start()
    cot_load = pltpu.make_async_copy(r.cot, r.out, r.load_sem.at[5])
    loads = Refs()
    for n, (name, source) in enumerate(
        dict(wqkv=r.in_wqkv, wup=r.in_wup, wdn=r.in_wdn, wout=r.in_wout).items()
    ):
        setattr(loads, name, pltpu.make_async_copy(source, getattr(r, name), r.load_sem.at[n]))
        getattr(loads, name).start()
    own = feat(spot.mp)
    here, there = r.small.at[own], r.small.at[feat(spot.yp_mp)]
    small_y = remote(r.cols.at[0:192], here, r.sm_sem.at[0], r.sm_sem.at[1], spot.yp)
    small_c = remote(r.cols.at[0:192], here, r.sm_sem.at[2], r.sm_sem.at[3], spot.sib)
    small_f = remote(there, there, r.sm_sem.at[4], r.sm_sem.at[5], spot.sib)

    def count_copy(bit):
        return remote(
            r.cnts.at[bit], r.cntr.at[bit], r.cn_sem.at[0, bit], r.cn_sem.at[1, bit], peers[bit]
        )

    def count_step(bit):
        count_copy(bit).wait()
        if bit + 1 < r.dp_bits:
            r.cnts[bit + 1] = r.cnts[bit] + r.cntr[bit]
            count_copy(bit + 1).start()

    tokens = Spread(spot, r.x, r.tk_sem)
    attended = Spread(spot, r.att, r.at_sem)
    cotangents = Spread(spot, r.gout, r.ct_sem)
    r.x[own, ROWS - 64 : LANES] = jnp.zeros((OWN, 128), BF16)
    r.gout[own, ROWS - 64 : LANES] = jnp.zeros((OWN, 128), BF16)
    token_load.wait()
    r.x[own, 0:ROWS] = r.out[...]
    cot_load.start()
    meet(greeted)
    tokens.to_y(0).start()
    row_tables(r)
    r.small[own, :] = r.cols[0:192, :]
    r.cnts[0] = r.cnt[...]
    small_y.start()
    count_copy(0).start()
    for c in range(1, CHUNKS):
        tokens.to_y(c).start()
    small_c.start()
    for c in range(CHUNKS):
        tokens.to_sib(c).start()
    loads.wout.wait()
    wo_here = r.wof.at[own]
    wo_there = r.wof.at[feat(spot.yp_mp)]
    wo_y = remote(r.wout, wo_here, r.wo_sem.at[0], r.wo_sem.at[1], spot.yp)
    wo_c = remote(r.wout, wo_here, r.wo_sem.at[2], r.wo_sem.at[3], spot.sib)
    wo_f = remote(wo_there, wo_there, r.wo_sem.at[4], r.wo_sem.at[5], spot.sib)
    wo_y.start()
    wo_c.start()
    r.wof[own, :] = r.wout[...]
    angle_tables(r)
    small_y.wait()
    small_f.start()
    cot_load.wait()
    r.gout[own, 0:ROWS] = (r.out[...].astype(F32) * r.info[2:3, 0:ROWS]).astype(BF16)
    for c in range(2):
        cotangents.send(c)
    count_step(0)
    loads.wup.wait()
    flip(r.wup, r.wupt)
    count_step(1)
    for ref in (r.sg1, r.sb1, r.sg2, r.sb2, r.sbo, r.sf0, r.sf1, r.dk, r.dv):
        ref[...] = jnp.zeros_like(ref)
    loads.wdn.wait()
    flip(r.wdn, r.wdnt)
    loads.wqkv.wait()
    small_c.wait()
    small_f.wait()
    tokens.relay(0)

    def window(source, j):
        start = 576 * j - 32 * (j // 2)
        r.win[j, :, 0:NARROW] = source[:, start : start + NARROW]

    def both_tiles(c, tile, source):
        def narrow(t):
            j = t // 5
            tile(r, spot, t, 576 * j - 32 * (j // 2), NARROW, r.win[j, :, 0:NARROW])

        @pl.when((c != 2) & (c != 4))
        def _():
            narrow(2 * c)
            narrow(2 * c + 1)

        @pl.when(c == 2)
        def _():
            tile(r, spot, 4, 0, 1152, source[:, 0:1152])
            narrow(5)

        @pl.when(c == 4)
        def _():
            narrow(8)
            tile(r, spot, 9, 976, 752, source[:, 976:1728])

    def attention(n, carry):
        @pl.when(n < CHUNKS)
        def _():
            @pl.when(n + 1 < CHUNKS)
            def _():
                tokens.relay(n + 1)

            tokens.arrived(n)
            project(r, n)

        for j in range(3):

            @pl.when(n == 2 * j + 2)
            def _():
                window(r.v, j)

        @pl.when(n >= 2)
        def _():
            both_tiles(n - 2, attend_tile, r.v)
            attended.send(n - 2)

        @pl.when(n == CHUNKS)
        def _():
            wo_y.wait()
            wo_f.start()

        return carry

    lax.fori_loop(0, CHUNKS + 2, attention, 0)
    for c in range(2, CHUNKS):
        cotangents.send(c)
    for bit in range(2, r.dp_bits):
        count_step(bit)
    last = r.dp_bits - 1
    total = r.cnts[last] + r.cntr[last]
    low, high = total[:, 0:1], total[:, 1:2]
    own_low = 1.0 - r.group[0].astype(F32)
    share = (own_low * low + (1.0 - own_low) * high) / (low + high)
    r.share[...] = jnp.broadcast_to(share, (8, 128))

    r.atto[...] = r.att[own, :]
    attended.relay(0)
    wo_c.wait()
    wo_f.wait()
    flip(r.wof, r.wot)

    outward = Exchange(r, spot, r.mp, r.mr, r.ms, r.mc, r.mo_sem)
    second = Exchange(r, spot, r.gp, r.gr, r.gs, r.gc, r.g2_sem, r.stats)
    g_att = Spread(spot, r.gatt, r.ga_sem)

    def halves(acc, arrive, res, sems):
        rows = acc.shape[0] // 2
        return [
            Reduce(
                spot,
                acc.at[rows * n : rows * n + rows],
                arrive[n],
                res.at[rows * n : rows * n + rows],
                r.groups,
                sems.at[n],
            )
            for n in range(2)
        ]

    down = halves(r.accdn, r.ardn, r.resdn, r.dn_sem)
    up = halves(r.accup, r.arup, r.resup, r.up_sem)

    pieces = down + up

    moves, tail, taken = numbered_moves()

    def move(kind, n):
        for piece, step in moves.get((kind, n), ()):
            pieces[piece].advance(step)

    def slots(kind, n):
        for point, at in sorted(moves):
            if point == kind:

                @pl.when(n == at)
                def _():
                    move(kind, at)

    def norm_step(c):
        second_norm_back(r, spot, c, second)
        g_att.send(c)

    def forward(n, carry):
        @pl.when(n + 1 < CHUNKS)
        def _():
            attended.relay(n + 1)

        attended.arrived(n)
        mlp_forward(r, spot, n, outward)
        return carry

    lax.fori_loop(0, CHUNKS, forward, 0)
    cotangents.relay(0)

    def backward(n, carry):
        @pl.when(n < EARLY)
        def _():
            cotangents.relay(n + 1)
            cotangents.arrived(n)

        mlp_backward(r, n, second)

        @pl.when(n >= 1)
        def _():
            second.pass_on(n - 1)

        @pl.when(n >= 4)
        def _():
            norm_step(n - 4)

        return carry

    def late_backward(n, carry):
        backward(n, carry)
        slots(IN_BACKWARD, n)
        return carry

    lax.fori_loop(0, EARLY, backward, 0)
    for c in range(EARLY + 1, CHUNKS):
        cotangents.relay(c)
    for c in range(EARLY, CHUNKS):
        cotangents.arrived(c)
    r.accdn[...] = (dot(r.act[...], r.gout[...], NT) * r.share[0:1, 0:1]).astype(BF16)
    down[0].start()
    down[1].start()
    lax.fori_loop(EARLY, CHUNKS, late_backward, 0)
    second.pass_on(CHUNKS - 1)
    r.accup[...] = (dot(r.h2[...], r.gpre[...], NT) * r.share[0:1, 0:1]).astype(BF16)
    up[0].start()
    up[1].start()
    norm_step(3)
    flip(r.wqkv, r.wqkvn)
    for j in range(3):
        window(r.qk.at[192:384], j)
    first = Exchange(r, spot, r.gp, r.gr, r.gs, r.gc, r.g1_sem, r.stats)
    g_att.relay(0)

    def back(c, carry):
        @pl.when(c + 4 < CHUNKS)
        def _():
            norm_step(c + 4)

        @pl.when(c + 1 < CHUNKS)
        def _():
            g_att.relay(c + 1)

        g_att.arrived(c)

        slots(BEFORE_TILES, c)
        both_tiles(c, back_tile, r.qk.at[192:384])
        slots(AFTER_TILES, c)

        def ready(chunks, give):
            def one(n, carry):
                unrotate(r, n)
                if give:
                    first_part(r, n, first)
                return carry

            lax.fori_loop(chunks[0], chunks[-1] + 1, one, 0)

        @pl.when(c == 2)
        def _():
            ready((0, 1), True)

        @pl.when(c == 3)
        def _():
            first.pass_on(0)
            first.pass_on(1)

        @pl.when(c == 4)
        def _():
            ready((2, 3), True)

        @pl.when(c == 5)
        def _():
            first.pass_on(2)
            first.pass_on(3)

        @pl.when(c == 6)
        def _():
            outward.pass_on(0)
            outward.pass_on(1)
            ready((4, 5, 6), False)

        return carry

    lax.fori_loop(0, CHUNKS, back, 0)
    r.accqkv[...] = (dot(r.gproj[0:576, :], r.h1[...], NT) * r.share[0:1, 0:1]).astype(BF16)
    qkv = [
        Reduce(
            spot,
            r.accqkv.at[OWN * n : OWN * n + OWN],
            r.arqkv[n],
            r.resqkv.at[OWN * n : OWN * n + OWN],
            r.groups if n < 2 else r.turned,
            r.qr_sem.at[n],
        )
        for n in range(3)
    ]
    for reduce in qkv:
        reduce.start()
    pieces += qkv
    lax.fori_loop(4, CHUNKS, lambda n, carry: (first_part(r, n, first), carry)[1], 0)
    r.accwo[...] = (dot(r.atto[...], r.gatt[...], NT) * r.share[0:1, 0:1]).astype(BF16)
    out = Reduce(spot, r.accwo, r.arwo, r.reswo, r.turned, r.wr_sem)
    out.start()
    pieces.append(out)

    def last(n, carry):
        @pl.when(n < 3)
        def _():
            first.pass_on(n + 4)

        @pl.when(n >= 2)
        def _():
            outward.pass_on(n)

        first_norm_back(r, spot, n, first)
        slots(IN_LAST, n)
        return carry

    lax.fori_loop(0, CHUNKS, last, 0)

    def lane_sum(ref):
        return jnp.sum(ref[...], axis=1, keepdims=True)

    b_down = jnp.sum(r.gout[own, :].astype(F32), axis=1, keepdims=True)
    b_qkv = jnp.sum(r.gproj[0:576, :].astype(F32), axis=1, keepdims=True)
    columns = [
        jnp.sum(r.gpre[...].astype(F32), axis=1, keepdims=True),
        jnp.concatenate([b_qkv, lane_sum(r.sf0), lane_sum(r.sf1)], axis=0),
        jnp.concatenate([lane_sum(r.sbo), lane_sum(r.sg1), lane_sum(r.sb1), lane_sum(r.sg2)], axis=0),
        jnp.concatenate([lane_sum(r.sb2), b_down, jnp.zeros((384, 1), F32)], axis=0),
    ]
    lane = lax.broadcasted_iota(jnp.int32, (D, 128), 1)
    table = jnp.zeros((D, 128), F32)
    for n, column in enumerate(columns):
        table = jnp.where(lane == n, column, table)
    table = jnp.transpose(table * r.share[0:1, 0:1])[0:8, :]
    vectors = Vectors(r, spot, table)
    vectors.start()
    pieces.append(vectors)
    finished = 0
    for piece, step in tail:
        if piece < 9:
            pieces[piece].advance(step)
        else:
            finish_out(r, outward, finished)
            finished += 1
    r.out[...] = r.gs[:, 0:ROWS]
    for step in range(2 * r.dp_bits):
        for piece, first_step in zip(pieces, taken, strict=True):
            piece.advance(first_step + step)
    r.sums[...] = vectors.table


class Vectors:
    def __init__(self, r, spot, table):
        self.r, self.spot, self.table = r, spot, table

    def copy(self, at):
        r = self.r
        return remote(
            r.sumx.at[at], r.sumr.at[at], r.su_sem.at[0, at], r.su_sem.at[1, at], dp_partner(self.spot, at)
        )

    def start(self, at=0):
        self.r.sumx[at] = self.table
        self.copy(at).start()

    def advance(self, at):
        if at >= self.r.dp_bits:
            return
        self.copy(at).wait()
        self.table = self.table + self.r.sumr[at]
        if at + 1 < self.r.dp_bits:
            self.start(at + 1)


def finish_out(r, outward, c):
    at = lanes(c)
    whole = r.mido[:, at] + (outward.take(c) + r.cols[0:192, 9:10])
    r.gs[:, at] = (r.info[2:3, at] * whole).astype(BF16)


def dma(*shape):
    return pltpu.SemaphoreType.DMA(shape)


def run(dp_bits, **arrays):
    scalars = ("group",)
    on_demand = ("tok", "cot", "in_wqkv", "in_wup", "in_wdn", "in_wout")
    outs = dict(
        out=((OWN, ROWS), BF16),
        igrad=((OWN, LANES), F32),
        resdn=((D, D), BF16),
        resup=((D, D), BF16),
        reswo=((OWN, D), BF16),
        resqkv=((576, D), BF16),
        sums=((8, D), F32),
    )

    groups = [(bit,) for bit in range(dp_bits)]
    turned = groups[1:] + groups[:1]

    def levels(rows):
        steps = plan((rows, D), groups)
        return [VM(((1 << len(bits)) - 1, *shape), BF16) for bits, shape, _ in steps]

    full = VM((D, LANES), BF16)
    own = VM((OWN, LANES), BF16)
    square = VM((D, D), BF16)
    spread = dma(6, CHUNKS)
    scratch = dict(
        x=full,
        h1=full,
        qk=VM((384, LANES), BF16),
        v=own,
        kn=VM((LANES, OWN), BF16),
        vn=VM((LANES, OWN), BF16),
        cos=VM((96, LANES), F32),
        sin=VM((96, LANES), F32),
        kcol=VM((LANES, TILE), F32),
        win=VM((3, OWN, 640), BF16),
        lse=VM((TILES, 8, 384), F32),
        small=VM((D, 128), F32),
        share=VM((8, 128), F32),
        att=full,
        gout=full,
        wqkv=VM((576, D), BF16),
        wup=square,
        wupt=square,
        wdn=square,
        wdnt=square,
        wout=VM((OWN, D), BF16),
        wof=square,
        wot=square,
        h2=full,
        act=full,
        gpre=full,
        work=VM((D, CHUNK), F32),
        mido=VM((OWN, LANES), F32),
        rows1=VM((8, LANES), F32),
        rows2=VM((8, LANES), F32),
        info=VM((8, LANES), F32),
        cols=VM((D, 128), F32),
        cnt=VM((8, 128), F32),
        stats=VM((4, 8, LANES), F32),
        mp=VM((2, 2, OWN, LANES), BF16),
        mr=VM((2, OWN, LANES), BF16),
        ms=own,
        mc=own,
        gp=VM((2, 2, OWN, LANES), BF16),
        gr=VM((2, OWN, LANES), BF16),
        gs=own,
        gc=own,
        dk=VM((LANES, OWN), F32),
        dv=VM((LANES, OWN), F32),
        ardn=[levels(384), levels(384)],
        arup=[levels(384), levels(384)],
        arwo=levels(OWN),
        arqkv=[levels(OWN), levels(OWN), levels(OWN)],
        sg1=VM((OWN, 128), F32),
        sb1=VM((OWN, 128), F32),
        sg2=VM((OWN, 128), F32),
        sb2=VM((OWN, 128), F32),
        sbo=VM((OWN, 128), F32),
        sf0=VM((96, 128), F32),
        sf1=VM((96, 128), F32),
        cnts=VM((dp_bits, 8, 128), F32),
        cntr=VM((dp_bits, 8, 128), F32),
        sumx=VM((dp_bits, 8, D), F32),
        sumr=VM((dp_bits, 8, D), F32),
        load_sem=dma(6),
        tk_sem=spread,
        at_sem=spread,
        ct_sem=spread,
        ga_sem=spread,
        sm_sem=dma(6),
        wo_sem=dma(6),
        cn_sem=dma(2, dp_bits),
        su_sem=dma(2, dp_bits),
        mo_sem=dma(8, CHUNKS),
        g2_sem=dma(8, CHUNKS),
        g1_sem=dma(8, CHUNKS),
        dn_sem=dma(2, 2, 2 * dp_bits, 3),
        up_sem=dma(2, 2, 2 * dp_bits, 3),
        wr_sem=dma(2, 2 * dp_bits, 3),
        qr_sem=dma(3, 2, 2 * dp_bits, 3),
    )
    shapes, structure = jax.tree.flatten(scratch, is_leaf=lambda leaf: not isinstance(leaf, (dict, list)))

    def body(*refs):
        r = Refs()
        for name, ref in zip(list(arrays) + list(outs), refs):
            setattr(r, name, ref)
        named = jax.tree.unflatten(structure, refs[len(arrays) + len(outs) :])
        for name, ref in named.items():
            setattr(r, name, ref)
        r.gatt, r.atto = r.att, r.v
        r.dq, r.gproj = r.act, r.h2
        r.accdn, r.accup, r.accwo = r.wof, r.wupt, r.wdn.at[0:OWN]
        r.wqkvn = r.wot
        r.accqkv = r.wdnt.at[0:576]
        r.dp_bits, r.groups, r.turned = dp_bits, groups, turned
        kernel(r, place())

    results = pl.pallas_call(
        body,
        out_shape=[jax.ShapeDtypeStruct(shape, dtype) for shape, dtype in outs.values()],
        in_specs=[
            pl.BlockSpec(
                memory_space=pl.ANY if name in on_demand else pltpu.SMEM if name in scalars else VM
            )
            for name in arrays
        ],
        out_specs=[pl.BlockSpec(memory_space=VM) for _ in outs],
        scratch_shapes=shapes,
        compiler_params=pltpu.CompilerParams(
            collective_id=1, has_side_effects=True, vmem_limit_bytes=64 * MIB - 65536
        ),
    )(*arrays.values())
    named = Refs()
    for name, result in zip(outs, results, strict=True):
        setattr(named, name, result)
    return named


def local(
    tokens,
    w_qkv,
    b_qkv,
    freqs,
    w_out,
    b_out,
    norm1_gain,
    norm1_bias,
    norm2_gain,
    norm2_bias,
    w_up,
    b_up,
    w_down,
    b_down,
    cotangent,
    keep_mask,
    coords,
    block_group,
):
    row_count, width_loc = tokens.shape
    heads_loc = freqs.shape[1]
    row = lax.broadcasted_iota(jnp.int32, (8, D), 0)
    pack = jnp.zeros((8, D), F32)
    vectors = (b_up, norm1_gain, norm1_bias, norm2_gain, norm2_bias, b_out, b_down)
    for n, vector in enumerate(vectors):
        wide = jnp.pad(vector.astype(F32), (0, D - vector.shape[0]))
        pack = jnp.where(row == n, wide[None, :], pack)

    a = run(
        lax.axis_size("dp").bit_length() - 1,
        tok=tokens.T,
        cot=cotangent.T,
        pack=pack,
        bqkv=b_qkv,
        freqs=freqs.transpose(1, 0, 2),
        keep=keep_mask.reshape(1, row_count),
        coords=coords,
        group=block_group,
        in_wqkv=w_qkv.transpose(1, 2, 0).reshape(3 * width_loc, D),
        in_wup=w_up,
        in_wdn=w_down,
        in_wout=w_out,
    )
    sums = a.sums
    grad_qkv = a.resqkv.astype(F32)
    half = (2, heads_loc, HEAD_DIM // 2)
    return (
        a.out.T,
        a.igrad[:, :row_count].T,
        grad_qkv.reshape(3, width_loc, D).transpose(2, 0, 1),
        sums[1, : 3 * width_loc].reshape(3, width_loc),
        sums[1, 3 * width_loc :].reshape(half),
        a.reswo.astype(F32),
        sums[2, 0:192],
        sums[2, 192:384],
        sums[2, 384:576],
        sums[2, 576:768],
        sums[3, 0:192],
        a.resup.astype(F32),
        sums[0],
        a.resdn.astype(F32),
        sums[3, 192:384],
    )


def solution(mesh):
    return jax.shard_map(
        local,
        mesh=mesh,
        in_specs=(
            P("dp", "mp"),
            P(None, None, "mp"),
            P(None, "mp"),
            P(None, "mp", None),
            P("mp", None),
            P("mp"),
            P("mp"),
            P("mp"),
            P("mp"),
            P("mp"),
            P(None, "mp"),
            P("mp"),
            P("mp", None),
            P("mp"),
            P("dp", "mp"),
            P("dp"),
            P(None, "dp"),
            P("dp"),
        ),
        out_specs=(
            P("dp", "mp"),
            P("dp", "mp"),
            P(None, None, "mp"),
            P(None, "mp"),
            P(None, "mp", None),
            P("mp", None),
            P("mp"),
            P("mp"),
            P("mp"),
            P("mp"),
            P("mp"),
            P(None, "mp"),
            P("mp"),
            P("mp", None),
            P("mp"),
        ),
        check_vma=False,
    )
```

```python
import jax
import jax.numpy as jnp
from jax import lax
from jax.experimental import pallas as pl
from jax.experimental.pallas import tpu as pltpu
from jax.sharding import PartitionSpec as P

HEAD_DIM = 64
GRID_LO = 14
SLOTS = 576

MESH = pl.DeviceIdType.MESH
MIB = 1024 * 1024
VM = pltpu.VMEM
F32 = jnp.float32
BF16 = jnp.bfloat16
NT = (((1,), (1,)), ((), ()))
NN = (((1,), (0,)), ((), ()))

D = 768
OWN = 192
ROWS = 1728
LANES = 1792
CHUNK = 256
CHUNKS = LANES // CHUNK
TILE = 128
TILES = LANES // TILE
NARROW = 608

norm_eps = 1e-06
root_half = 0.7071067811865476
inv_root_two_pi = 0.3989422804014327


EARLY = 2
IN_BACKWARD, BEFORE_TILES, AFTER_TILES, IN_LAST, TAIL = range(5)
MOVES = (
    {6: (0, 1,)},
    {0: (0, 1,), 2: (0,), 3: (2,), 5: (2, 0,), 6: (1,)},
    {1: (2,), 2: (1, 3,), 3: (0,), 4: (1, 3,)},
    {0: (3, 2, 0, 1,), 3: (4, 6,), 5: (5, 3,), 6: (2, 7, 4,)},
)
IN_TAIL = (6, 9, 5, 9, 9, 9, 9, 9, 9, 3, 7, 4, 2, 6, 8, 5, 7, 8, 4, 6, 3, 5, 7, 4, 8, 6, 5, 7, 4, 6, 5, 7)


def numbered_moves():
    points = [(IN_BACKWARD, n) for n in range(CHUNKS)]
    for c in range(CHUNKS):
        points += [(BEFORE_TILES, c), (AFTER_TILES, c)]
    points += [(IN_LAST, n) for n in range(CHUNKS)]
    taken = [0] * 9
    moves = {}
    for kind, n in points:
        for piece in MOVES[kind].get(n, ()):
            moves.setdefault((kind, n), []).append((piece, taken[piece]))
            taken[piece] += 1
    tail = []
    for piece in IN_TAIL:
        if piece < 9:
            tail.append((piece, taken[piece]))
            taken[piece] += 1
        else:
            tail.append((piece, 0))
    return moves, tail, taken


class Refs:
    pass


def dot(left, right, dims=NN):
    return lax.dot_general(left, right, dims, preferred_element_type=F32)


def remote(src, dst, send, recv, device):
    return pltpu.make_async_remote_copy(
        src_ref=src, dst_ref=dst, send_sem=send, recv_sem=recv, device_id=device, device_id_type=MESH
    )


def place():
    spot = Refs()
    spot.dp = lax.axis_index("dp")
    spot.mp = lax.axis_index("mp")
    spot.y = spot.mp // 2
    spot.c = spot.mp % 2
    spot.sib_mp = 2 * spot.y + 1 - spot.c
    spot.yp_mp = 2 * (1 - spot.y) + spot.c
    spot.sib = (spot.dp, spot.sib_mp)
    spot.yp = (spot.dp, spot.yp_mp)
    return spot


def greet(devices):
    barrier = pltpu.get_barrier_semaphore()
    for device in devices:
        pl.semaphore_signal(barrier, inc=1, device_id=device, device_id_type=MESH)


def meet(devices):
    pl.semaphore_wait(pltpu.get_barrier_semaphore(), len(devices))


def dp_partner(spot, bit):
    mine = (spot.dp // (1 << bit)) % 2
    return (spot.dp + (1 - 2 * mine) * (1 << bit), spot.mp)


def feat(j):
    return pl.ds(pl.multiple_of(OWN * j, 16), OWN)


def lanes(c):
    return pl.ds(pl.multiple_of(c * CHUNK, CHUNK), CHUNK)


def tile_lanes(t):
    return pl.ds(pl.multiple_of(t * TILE, TILE), TILE)


def flipped(spot, bits, number):
    dp = spot.dp
    for n, bit in enumerate(bits):
        if (number >> n) & 1:
            dp = dp + (1 - 2 * ((spot.dp // (1 << bit)) % 2)) * (1 << bit)
    return (dp, spot.mp)


def cut(shape):
    rows, cols = shape
    if (rows // 2) % 16 == 0:
        return (rows // 2, cols)
    if (cols // 2) % 128 == 0:
        return (rows, cols // 2)
    return shape


def plan(shape, groups):
    steps = []
    for bits in groups:
        after = shape
        for _ in bits:
            after = cut(after)
        whole = cut(cut(shape)) if len(bits) == 2 else cut(shape)
        if len(bits) == 2 and cut(shape) == cut(cut(shape)):
            for bit in bits:
                now = cut(shape)
                steps.append(((bit,), now, now != shape))
                shape = now
            continue
        steps.append((bits, whole, whole != shape))
        shape = after
    return steps


class Reduce:
    def __init__(self, spot, acc, arrive, res, groups, sems):
        self.spot, self.res, self.sems = spot, res, sems
        self.phases = []
        gathers = []
        source, row, col = acc, 0, 0
        steps = plan(acc.shape, groups)
        shape = acc.shape
        for (bits, after, differ), target in zip(steps, arrive, strict=True):
            corners = []
            for number in range(1 << len(bits)):
                at, part = (0, 0), shape
                for n, bit in enumerate(bits):
                    smaller = cut(part)
                    mine = (spot.dp // (1 << bit)) % 2
                    side = 1 - mine if (number >> n) & 1 else mine
                    if smaller[0] < part[0]:
                        at = (at[0] + side * smaller[0], at[1])
                    elif smaller[1] < part[1]:
                        at = (at[0], at[1] + side * smaller[1])
                    part = smaller
                corners.append(at)
            row, col = row + corners[0][0], col + corners[0][1]
            self.phases.append((bits, source, corners, after, target))
            if differ:
                gathers.append((bits, res, (row, col), after, None))
            source, shape = target.at[0], after
        self.own = (row, col)
        self.sums = len(self.phases)
        self.phases += gathers[::-1]

    def piece(self, ref, corner, shape):
        def span(start, size, unit, whole):
            if size == whole:
                return pl.ds(0, size)
            return pl.ds(pl.multiple_of(start, unit), size)

        return ref.at[
            span(corner[0], shape[0], 16, ref.shape[0]), span(corner[1], shape[1], 128, ref.shape[1])
        ]

    def copies(self, at):
        bits, source, corners, shape, target = self.phases[at]
        out = []
        for number in range(1, 1 << len(bits)):
            if target is None:
                piece = self.piece(source, corners, shape)
                goal = piece
            else:
                piece = self.piece(source, corners[number], shape)
                goal = target.at[number - 1]
            sems = (self.sems.at[0, at, number - 1], self.sems.at[1, at, number - 1])
            out.append(remote(piece, goal, *sems, flipped(self.spot, bits, number)))
        return out

    def start(self, at=0):
        for copy in self.copies(at):
            copy.start()

    def add(self, at):
        bits, source, corners, shape, target = self.phases[at]
        held = self.piece(source, corners[0], shape)
        last = at == self.sums - 1
        goal = self.piece(self.res, self.own, shape) if last else target.at[0]
        step = 48 if shape[0] % 48 == 0 else 16

        def block(i, carry):
            rows = pl.ds(pl.multiple_of(i * step, 16), step)
            total = held[rows, :].astype(F32)
            for n in range((1 << len(bits)) - 1):
                total = total + target[n, rows, :].astype(F32)
            goal[rows, :] = total.astype(BF16)
            return carry

        lax.fori_loop(0, shape[0] // step, block, 0)

    def advance(self, at):
        if at >= len(self.phases):
            return
        for copy in self.copies(at):
            copy.wait()
        if at < self.sums:
            self.add(at)
        if at + 1 < len(self.phases):
            self.start(at + 1)


class Exchange:
    def __init__(self, r, spot, part, arrive, out, come, sems, stats=None):
        self.r, self.spot = r, spot
        self.part, self.arrive, self.out, self.come = part, arrive, out, come
        self.sems, self.stats = sems, stats

    def core(self, c):
        at = lanes(c)
        copies = [
            remote(
                self.part.at[:, 1 - self.spot.c, :, at],
                self.arrive.at[:, :, at],
                self.sems.at[0, c],
                self.sems.at[1, c],
                self.spot.sib,
            )
        ]
        if self.stats is not None:
            copies.append(
                remote(
                    self.stats.at[0, :, at],
                    self.stats.at[1, :, at],
                    self.sems.at[2, c],
                    self.sems.at[3, c],
                    self.spot.sib,
                )
            )
        return copies

    def over(self, c):
        at = lanes(c)
        copies = [
            remote(
                self.out.at[:, at],
                self.come.at[:, at],
                self.sems.at[4, c],
                self.sems.at[5, c],
                self.spot.yp,
            )
        ]
        if self.stats is not None:
            copies.append(
                remote(
                    self.stats.at[2, :, at],
                    self.stats.at[3, :, at],
                    self.sems.at[6, c],
                    self.sems.at[7, c],
                    self.spot.yp,
                )
            )
        return copies

    def give(self, c, values):
        at = lanes(c)
        for j in range(4):
            self.part[j // 2, j % 2, :, at] = values[OWN * j : OWN * j + OWN].astype(BF16)
        for copy in self.core(c):
            copy.start()

    def pass_on(self, c):
        at = lanes(c)
        for copy in self.core(c):
            copy.wait()
        away = 1 - self.spot.y
        self.out[:, at] = (
            self.part[away, self.spot.c, :, at].astype(F32) + self.arrive[away, :, at].astype(F32)
        ).astype(BF16)
        if self.stats is not None:
            self.stats[2, :, at] = self.stats[0, :, at] + self.stats[1, :, at]
        for copy in self.over(c):
            copy.start()

    def take(self, c):
        at = lanes(c)
        for copy in self.over(c):
            copy.wait()
        home = self.spot.y
        return (
            self.part[home, self.spot.c, :, at].astype(F32)
            + self.arrive[home, :, at].astype(F32)
            + self.come[:, at].astype(F32)
        )

    def take_stats(self, c):
        at = lanes(c)
        return (self.stats[2, :, at] + self.stats[3, :, at]) * (1.0 / D)


class Spread:
    def __init__(self, spot, full, sems):
        self.spot, self.full, self.sems = spot, full, sems

    def piece(self, j, c, kind, device):
        part = self.full.at[feat(j), lanes(c)]
        return remote(part, part, self.sems.at[2 * kind, c], self.sems.at[2 * kind + 1, c], device)

    def to_y(self, c):
        return self.piece(self.spot.mp, c, 0, self.spot.yp)

    def to_sib(self, c):
        return self.piece(self.spot.mp, c, 1, self.spot.sib)

    def onward(self, c):
        return self.piece(self.spot.yp_mp, c, 2, self.spot.sib)

    def send(self, c):
        self.to_y(c).start()
        self.to_sib(c).start()

    def relay(self, c):
        self.to_y(c).wait()
        self.onward(c).start()

    def arrived(self, c):
        self.to_sib(c).wait()
        self.onward(c).wait()


def sin_cos(angle):
    turns = jnp.floor(angle * 0.6366197723675814 + 0.5)
    rest = angle - turns * 1.5703125
    rest = rest - turns * 4.837512969970703e-4
    rest = rest - turns * 7.549789948768648e-8
    square = rest * rest
    sine = rest + rest * square * (
        -1.6666654611e-1 + square * (8.3321608736e-3 + square * -1.9515295891e-4)
    )
    cosine = (
        1.0
        - 0.5 * square
        + square
        * square
        * (4.166664568298827e-2 + square * (-1.388731625493765e-3 + square * 2.443315711809948e-5))
    )
    quarter = turns - 4.0 * jnp.floor(turns * 0.25)
    odd = (quarter == 1.0) | (quarter == 3.0)
    sine_sign = jnp.where(quarter >= 2.0, -1.0, 1.0)
    cosine_sign = jnp.where((quarter == 1.0) | (quarter == 2.0), -1.0, 1.0)
    return (
        jnp.where(odd, cosine, sine) * sine_sign,
        jnp.where(odd, sine, cosine) * cosine_sign,
    )


def phi_parts(value):
    bell = jnp.exp(-0.5 * value * value)
    inner = 1.0 / (1.0 + (0.3275911 * root_half) * jnp.abs(value))
    series = 0.5 * 1.061405429
    for factor in (-1.453152027, 1.421413741, -0.284496736, 0.254829592):
        series = series * inner + 0.5 * factor
    beyond = series * inner * bell
    return (jnp.where(value >= 0.0, 1.0 - beyond, beyond), inv_root_two_pi * bell)


def normalize(values):
    mean = jnp.mean(values, axis=0, keepdims=True)
    square = jnp.mean(values * values, axis=0, keepdims=True)
    inverse = lax.rsqrt(square - mean * mean + norm_eps)
    return ((values - mean) * inverse, mean, inverse)


def turn_by(values, cosine, sine):
    out = []
    for h in range(3):
        front, rear = values[64 * h : 64 * h + 32], values[64 * h + 32 : 64 * h + 64]
        co, si = cosine[32 * h : 32 * h + 32], sine[32 * h : 32 * h + 32]
        out += [front * co - rear * si, front * si + rear * co]
    return jnp.concatenate(out, axis=0)


def block_diagonal(tile):
    zero = jnp.zeros((64, TILE), tile.dtype)
    parts = []
    for h in range(3):
        column = [zero, zero, zero]
        column[h] = tile[64 * h : 64 * h + 64]
        parts.append(jnp.concatenate(column, axis=0))
    return jnp.concatenate(parts, axis=1)


def from_diagonal(values, heads):
    return jnp.concatenate(
        [values[64 * h : 64 * h + 64, TILE * n : TILE * n + TILE] for n, h in enumerate(heads)], axis=0
    )


def fold(values):
    return values[:, :128] + values[:, 128:]


def row_tables(r):
    pad = jnp.zeros((1, D - 3 * OWN), F32)
    rest = jnp.zeros((1, D - OWN), F32)
    qkv = jnp.concatenate([r.bqkv[n : n + 1, :].astype(F32) for n in range(3)] + [pad], axis=1)
    pad = jnp.zeros((2, D - 96), F32)
    freqs = jnp.concatenate([r.freqs[h] for h in range(3)] + [pad], axis=1)
    table = jnp.concatenate(
        [r.b_up[...].astype(F32).reshape(1, D), qkv, freqs]
        + [
            jnp.concatenate([ref[...].astype(F32).reshape(1, OWN), rest], axis=1)
            for ref in (r.gain1, r.bias1, r.gain2, r.bias2, r.b_out, r.b_down)
        ]
        + [jnp.zeros((118, D), F32)],
        axis=0,
    )
    for i in range(D // 128):
        r.cols[128 * i : 128 * i + 128, :] = jnp.transpose(table[:, 128 * i : 128 * i + 128])
    low = 1.0 - r.group[0].astype(F32)
    keep = r.keep[...].astype(F32).reshape(1, ROWS)
    middle = lax.broadcasted_iota(jnp.int32, (1, ROWS), 1).astype(F32) + 0.5
    segment = low * jnp.floor(middle * (1.0 / (GRID_LO * GRID_LO))) + (1.0 - low) * jnp.floor(
        middle * (1.0 / SLOTS)
    )
    r.info[...] = jnp.zeros_like(r.info)
    r.info[0:2, 0:ROWS] = r.coords[...].astype(F32)
    r.info[2:3, 0:ROWS] = keep
    r.info[3:4, 0:ROWS] = keep * (segment + 1.0) - 1.0
    r.info[4:5, 0:ROWS] = segment
    kept = jnp.sum(keep, axis=1, keepdims=True)
    lane = lax.broadcasted_iota(jnp.int32, (8, 128), 1)
    r.cnt[...] = kept * jnp.where(lane == 0, low, jnp.where(lane == 1, 1.0 - low, 0.0))


def angle_tables(r):
    def block(c, carry):
        at = lanes(c)
        angle = r.cols[0:96, 2:3] * r.info[0:1, at] + r.cols[0:96, 3:4] * r.info[1:2, at]
        sine, cosine = sin_cos(angle)
        r.cos[:, at] = cosine
        r.sin[:, at] = sine
        return carry

    lax.fori_loop(0, CHUNKS, block, 0)

    def column(t, carry):
        row = r.info[3:4, tile_lanes(t)]
        r.kcol[pl.ds(pl.multiple_of(t * TILE, TILE), TILE), :] = jnp.transpose(
            jnp.broadcast_to(row, (TILE, TILE))
        )
        return carry

    lax.fori_loop(0, TILES, column, 0)


def flip(source, goal):
    for i in range(source.shape[1] // 128):
        part = source[:, 128 * i : 128 * i + 128].astype(F32)
        goal[128 * i : 128 * i + 128, 0 : source.shape[0]] = jnp.transpose(part).astype(BF16)


def project(r, c):
    at = lanes(c)
    normed, mean, inverse = normalize(r.x[:, at].astype(F32))
    r.rows1[0:1, at] = mean
    r.rows1[1:2, at] = inverse
    h1 = (normed * r.small[:, 4:5] + r.small[:, 5:6]).astype(BF16)
    r.h1[:, at] = h1
    projected = dot(r.wqkv[...], h1) + r.cols[0:576, 1:2]
    cosine, sine = r.cos[:, at], r.sin[:, at]
    query = turn_by(projected[0:192], cosine, sine)
    key = turn_by(projected[192:384], cosine, sine)
    value = projected[384:576]
    r.qk[0:192, at] = query.astype(BF16)
    r.qk[192:384, at] = key.astype(BF16)
    r.v[:, at] = value.astype(BF16)
    r.kn[at, :] = jnp.transpose(key).astype(BF16)
    r.vn[at, :] = jnp.transpose(value).astype(BF16)


def tile_mask(r, tile, start, width):
    window = pl.ds(pl.multiple_of(start, 16), width)
    allowed = r.kcol[window, :] == r.info[4:5, tile_lanes(tile)]
    return jnp.where(allowed, 0.0, -1e30)


def repeat(mask, values):
    return jnp.concatenate([mask] * (values.shape[1] // TILE), axis=1)


def head_groups(width):
    return [(0, 1, 2)] if width <= NARROW else [(0,), (1,), (2,)]


def attend_tile(r, spot, tile, start, width, values):
    window = pl.ds(pl.multiple_of(start, 16), width)
    at = tile_lanes(tile)
    queries = block_diagonal(r.qk[0:192, at] * BF16(0.125))
    mask = tile_mask(r, tile, start, width)
    for heads in head_groups(width):
        span = slice(TILE * heads[0], TILE * heads[-1] + TILE)
        scores = dot(r.kn[window, :], queries[:, span])
        scores = scores + repeat(mask, scores)
        top = jnp.max(scores, axis=0, keepdims=True)
        exponent = jnp.exp(scores - top)
        total = jnp.sum(exponent, axis=0, keepdims=True)
        probs = (exponent * (1.0 / total)).astype(BF16)
        out = from_diagonal(dot(values, probs), heads).astype(BF16)
        r.att[head_rows(spot, heads), at] = out
        r.lse[tile, :, span] = jnp.broadcast_to(top + jnp.log(total), (8, span.stop - span.start))


def head_rows(spot, heads):
    return pl.ds(pl.multiple_of(OWN * spot.mp + 64 * heads[0], 16), 64 * len(heads))


def key_blocks(width):
    count = -(-width // 384)
    size = -(-width // (16 * count)) * 16
    return [(at, min(size, width - at)) for at in range(0, width, size)]


def back_tile(r, spot, tile, start, width, keys):
    at = tile_lanes(tile)
    queries = block_diagonal(r.qk[0:192, at] * BF16(0.125))
    grad_rows = dot(r.wout[...], r.gatt[:, at]).astype(BF16)
    grads = block_diagonal(grad_rows)
    product = grad_rows.astype(F32) * r.atto[:, at].astype(F32)
    centers = [jnp.sum(product[64 * h : 64 * h + 64], axis=0, keepdims=True) for h in range(3)]
    for heads in head_groups(width):
        span = slice(TILE * heads[0], TILE * heads[-1] + TILE)
        query, grad = queries[:, span], grads[:, span]
        center = jnp.concatenate([centers[h] for h in heads], axis=1)
        log = r.lse[tile, 0:1, span]
        parts = []
        for offset, size in key_blocks(width):
            window = pl.ds(pl.multiple_of(start + offset, 16), size)
            mask = tile_mask(r, tile, start + offset, size)
            scores = dot(r.kn[window, :], query)
            probs = jnp.exp(scores + repeat(mask, scores) - log)
            g_probs = dot(r.vn[window, :], grad)
            g_scores = (probs * (g_probs - center)).astype(BF16)
            r.dv[window, :] += dot(probs.astype(BF16), grad, NT)
            r.dk[window, :] += dot(g_scores, query, NT)
            parts.append(g_scores)
        g_scores = jnp.concatenate(parts, axis=0)
        rows = slice(64 * heads[0], 64 * heads[-1] + 64)
        r.dq[rows, at] = (from_diagonal(dot(keys, g_scores), heads) * 0.125).astype(BF16)


def mlp_forward(r, spot, c, outward):
    at = lanes(c)
    mid = r.x[:, at].astype(F32) + (dot(r.wot[...], r.att[:, at]) + r.small[:, 8:9])
    normed, mean, inverse = normalize(mid)
    r.work[...] = mid
    r.mido[:, at] = r.work[feat(spot.mp), :]
    r.rows2[0:1, at] = mean
    r.rows2[1:2, at] = inverse
    h2 = (normed * r.small[:, 6:7] + r.small[:, 7:8]).astype(BF16)
    r.h2[:, at] = h2
    hidden = dot(r.wupt[...], h2) + r.cols[:, 0:1]
    lower, density = phi_parts(hidden)
    active = (hidden * lower).astype(BF16)
    r.act[:, at] = active
    r.gpre[:, at] = (lower + hidden * density).astype(BF16)
    outward.give(c, dot(r.wdnt[...], active))


def give_gradient(r, c, sums, grad, gain, bias, low):
    at = lanes(c)
    r.stats[0, 0:1, at] = jnp.sum(grad * gain, axis=0, keepdims=True)
    r.stats[0, 1:2, at] = jnp.sum(grad * (low[:, at].astype(F32) - bias), axis=0, keepdims=True)
    sums.give(c, grad)


def mlp_backward(r, c, sums):
    at = lanes(c)
    g_act = dot(r.wdn[...], r.gout[:, at])
    g_pre = (g_act * r.gpre[:, at].astype(F32)).astype(BF16)
    r.gpre[:, at] = g_pre
    give_gradient(r, c, sums, dot(r.wup[...], g_pre), r.small[:, 6:7], r.small[:, 7:8], r.h2)


def second_norm_back(r, spot, c, sums):
    at = lanes(c)
    grad = sums.take(c)
    means = sums.take_stats(c)
    normed = (r.mido[:, at] - r.rows2[0:1, at]) * r.rows2[1:2, at]
    r.sg2[...] += fold(grad * normed)
    r.sb2[...] += fold(grad)
    back = r.rows2[1:2, at] * (
        grad * r.cols[0:192, 6:7] - means[0:1, :] - normed * means[1:2, :]
    )
    g_att = (r.gout[feat(spot.mp), at].astype(F32) + back).astype(BF16)
    r.gatt[feat(spot.mp), at] = g_att
    r.sbo[...] += fold(g_att.astype(F32))


def unrotate(r, c):
    at = lanes(c)
    cosine, sine = r.cos[:, at], r.sin[:, at]
    g_query = r.dq[0:192, at].astype(F32)
    g_key = jnp.transpose(r.dk[at, :]).astype(BF16).astype(F32)
    g_value = jnp.transpose(r.dv[at, :]).astype(BF16)
    plain = [turn_by(g, cosine, -sine).astype(BF16) for g in (g_query, g_key)]
    r.gproj[0:576, at] = jnp.concatenate(plain + [g_value], axis=0)
    angle = []
    for h in range(3):
        total = 0.0
        for part, g in enumerate((g_query, g_key)):
            rotated = r.qk[192 * part : 192 * part + 192, at].astype(F32)
            a, b = slice(64 * h, 64 * h + 32), slice(64 * h + 32, 64 * h + 64)
            total = total + (g[b] * rotated[a] - g[a] * rotated[b])
        angle.append(total)
    angle = jnp.concatenate(angle, axis=0)
    r.sf0[...] += fold(angle * r.info[0:1, at])
    r.sf1[...] += fold(angle * r.info[1:2, at])


def first_part(r, c, sums):
    grad = dot(r.wqkvn[:, 0:576], r.gproj[0:576, lanes(c)])
    give_gradient(r, c, sums, grad, r.small[:, 4:5], r.small[:, 5:6], r.h1)


def first_norm_back(r, spot, c, sums):
    at = lanes(c)
    grad = sums.take(c)
    means = sums.take_stats(c)
    own = feat(spot.mp)
    normed = (r.x[own, at].astype(F32) - r.rows1[0:1, at]) * r.rows1[1:2, at]
    r.sg1[...] += fold(grad * normed)
    r.sb1[...] += fold(grad)
    back = r.rows1[1:2, at] * (
        grad * r.cols[0:192, 4:5] - means[0:1, :] - normed * means[1:2, :]
    )
    r.igrad[:, at] = r.gatt[own, at].astype(F32) + back


def kernel(r, spot):
    peers = [dp_partner(spot, bit) for bit in range(r.dp_bits)]
    both = [flipped(spot, bits, 3) for bits in r.groups if len(bits) == 2]
    greeted = [spot.sib, spot.yp] + peers + both
    greet(greeted)
    token_load = pltpu.make_async_copy(r.tok, r.out, r.load_sem.at[4])
    token_load.start()
    cot_load = pltpu.make_async_copy(r.cot, r.out, r.load_sem.at[5])
    loads = Refs()
    for n, (name, source) in enumerate(
        dict(wqkv=r.in_wqkv, wup=r.in_wup, wdn=r.in_wdn, wout=r.in_wout).items()
    ):
        setattr(loads, name, pltpu.make_async_copy(source, getattr(r, name), r.load_sem.at[n]))
        getattr(loads, name).start()
    own = feat(spot.mp)
    here, there = r.small.at[own], r.small.at[feat(spot.yp_mp)]
    small_y = remote(r.cols.at[0:192], here, r.sm_sem.at[0], r.sm_sem.at[1], spot.yp)
    small_c = remote(r.cols.at[0:192], here, r.sm_sem.at[2], r.sm_sem.at[3], spot.sib)
    small_f = remote(there, there, r.sm_sem.at[4], r.sm_sem.at[5], spot.sib)

    def count_copy(bit):
        return remote(
            r.cnts.at[bit], r.cntr.at[bit], r.cn_sem.at[0, bit], r.cn_sem.at[1, bit], peers[bit]
        )

    def count_step(bit):
        count_copy(bit).wait()
        if bit + 1 < r.dp_bits:
            r.cnts[bit + 1] = r.cnts[bit] + r.cntr[bit]
            count_copy(bit + 1).start()

    tokens = Spread(spot, r.x, r.tk_sem)
    attended = Spread(spot, r.att, r.at_sem)
    cotangents = Spread(spot, r.gout, r.ct_sem)
    r.x[own, ROWS - 64 : LANES] = jnp.zeros((OWN, 128), BF16)
    r.gout[own, ROWS - 64 : LANES] = jnp.zeros((OWN, 128), BF16)
    token_load.wait()
    r.x[own, 0:ROWS] = r.out[...]
    cot_load.start()
    meet(greeted)
    tokens.to_y(0).start()
    row_tables(r)
    r.small[own, :] = r.cols[0:192, :]
    r.cnts[0] = r.cnt[...]
    small_y.start()
    count_copy(0).start()
    for c in range(1, CHUNKS):
        tokens.to_y(c).start()
    small_c.start()
    for c in range(CHUNKS):
        tokens.to_sib(c).start()
    loads.wout.wait()
    wo_here = r.wof.at[own]
    wo_there = r.wof.at[feat(spot.yp_mp)]
    wo_y = remote(r.wout, wo_here, r.wo_sem.at[0], r.wo_sem.at[1], spot.yp)
    wo_c = remote(r.wout, wo_here, r.wo_sem.at[2], r.wo_sem.at[3], spot.sib)
    wo_f = remote(wo_there, wo_there, r.wo_sem.at[4], r.wo_sem.at[5], spot.sib)
    wo_y.start()
    wo_c.start()
    r.wof[own, :] = r.wout[...]
    angle_tables(r)
    small_y.wait()
    small_f.start()
    cot_load.wait()
    r.gout[own, 0:ROWS] = (r.out[...].astype(F32) * r.info[2:3, 0:ROWS]).astype(BF16)
    for c in range(2):
        cotangents.send(c)
    count_step(0)
    loads.wup.wait()
    flip(r.wup, r.wupt)
    count_step(1)
    for ref in (r.sg1, r.sb1, r.sg2, r.sb2, r.sbo, r.sf0, r.sf1, r.dk, r.dv):
        ref[...] = jnp.zeros_like(ref)
    loads.wdn.wait()
    flip(r.wdn, r.wdnt)
    loads.wqkv.wait()
    small_c.wait()
    small_f.wait()
    tokens.relay(0)

    def window(source, j):
        start = 576 * j - 32 * (j // 2)
        r.win[j, :, 0:NARROW] = source[:, start : start + NARROW]

    def both_tiles(c, tile, source):
        def narrow(t):
            j = t // 5
            tile(r, spot, t, 576 * j - 32 * (j // 2), NARROW, r.win[j, :, 0:NARROW])

        @pl.when((c != 2) & (c != 4))
        def _():
            narrow(2 * c)
            narrow(2 * c + 1)

        @pl.when(c == 2)
        def _():
            tile(r, spot, 4, 0, 1152, source[:, 0:1152])
            narrow(5)

        @pl.when(c == 4)
        def _():
            narrow(8)
            tile(r, spot, 9, 976, 752, source[:, 976:1728])

    def attention(n, carry):
        @pl.when(n < CHUNKS)
        def _():
            @pl.when(n + 1 < CHUNKS)
            def _():
                tokens.relay(n + 1)

            tokens.arrived(n)
            project(r, n)

        for j in range(3):

            @pl.when(n == 2 * j + 2)
            def _():
                window(r.v, j)

        @pl.when(n >= 2)
        def _():
            both_tiles(n - 2, attend_tile, r.v)
            attended.send(n - 2)

        @pl.when(n == CHUNKS)
        def _():
            wo_y.wait()
            wo_f.start()

        return carry

    lax.fori_loop(0, CHUNKS + 2, attention, 0)
    for c in range(2, CHUNKS):
        cotangents.send(c)
    for bit in range(2, r.dp_bits):
        count_step(bit)
    last = r.dp_bits - 1
    total = r.cnts[last] + r.cntr[last]
    low, high = total[:, 0:1], total[:, 1:2]
    own_low = 1.0 - r.group[0].astype(F32)
    share = (own_low * low + (1.0 - own_low) * high) / (low + high)
    r.share[...] = jnp.broadcast_to(share, (8, 128))

    r.atto[...] = r.att[own, :]
    attended.relay(0)
    wo_c.wait()
    wo_f.wait()
    flip(r.wof, r.wot)

    outward = Exchange(r, spot, r.mp, r.mr, r.ms, r.mc, r.mo_sem)
    second = Exchange(r, spot, r.gp, r.gr, r.gs, r.gc, r.g2_sem, r.stats)
    g_att = Spread(spot, r.gatt, r.ga_sem)

    def halves(acc, arrive, res, sems, orders):
        rows = acc.shape[0] // 2
        return [
            Reduce(
                spot,
                acc.at[rows * n : rows * n + rows],
                arrive[n],
                res.at[rows * n : rows * n + rows],
                orders[n],
                sems.at[n],
            )
            for n in range(2)
        ]

    down = halves(r.accdn, r.ardn, r.resdn, r.dn_sem, (r.swapped, r.groups))
    up = halves(r.accup, r.arup, r.resup, r.up_sem, (r.groups, r.groups))

    pieces = down + up

    moves, tail, taken = numbered_moves()

    def move(kind, n):
        for piece, step in moves.get((kind, n), ()):
            pieces[piece].advance(step)

    def slots(kind, n):
        for point, at in sorted(moves):
            if point == kind:

                @pl.when(n == at)
                def _():
                    move(kind, at)

    def norm_step(c):
        second_norm_back(r, spot, c, second)
        g_att.send(c)

    def forward(n, carry):
        @pl.when(n + 1 < CHUNKS)
        def _():
            attended.relay(n + 1)

        attended.arrived(n)
        mlp_forward(r, spot, n, outward)
        return carry

    lax.fori_loop(0, CHUNKS, forward, 0)
    cotangents.relay(0)

    def backward(n, carry):
        @pl.when(n < EARLY)
        def _():
            cotangents.relay(n + 1)
            cotangents.arrived(n)

        mlp_backward(r, n, second)

        @pl.when(n >= 1)
        def _():
            second.pass_on(n - 1)

        @pl.when(n >= 4)
        def _():
            norm_step(n - 4)

        return carry

    def late_backward(n, carry):
        backward(n, carry)
        slots(IN_BACKWARD, n)
        return carry

    lax.fori_loop(0, EARLY, backward, 0)
    for c in range(EARLY + 1, CHUNKS):
        cotangents.relay(c)
    for c in range(EARLY, CHUNKS):
        cotangents.arrived(c)
    r.accdn[...] = (dot(r.act[...], r.gout[...], NT) * r.share[0:1, 0:1]).astype(BF16)
    down[0].start()
    down[1].start()
    lax.fori_loop(EARLY, CHUNKS, late_backward, 0)
    second.pass_on(CHUNKS - 1)
    r.accup[...] = (dot(r.h2[...], r.gpre[...], NT) * r.share[0:1, 0:1]).astype(BF16)
    up[0].start()
    up[1].start()
    norm_step(3)
    flip(r.wqkv, r.wqkvn)
    for j in range(3):
        window(r.qk.at[192:384], j)
    first = Exchange(r, spot, r.gp, r.gr, r.gs, r.gc, r.g1_sem, r.stats)
    g_att.relay(0)

    def back(c, carry):
        @pl.when(c + 4 < CHUNKS)
        def _():
            norm_step(c + 4)

        @pl.when(c + 1 < CHUNKS)
        def _():
            g_att.relay(c + 1)

        g_att.arrived(c)

        slots(BEFORE_TILES, c)
        both_tiles(c, back_tile, r.qk.at[192:384])
        slots(AFTER_TILES, c)

        def ready(chunks, give):
            def one(n, carry):
                unrotate(r, n)
                if give:
                    first_part(r, n, first)
                return carry

            lax.fori_loop(chunks[0], chunks[-1] + 1, one, 0)

        @pl.when(c == 2)
        def _():
            ready((0, 1), True)

        @pl.when(c == 3)
        def _():
            first.pass_on(0)
            first.pass_on(1)

        @pl.when(c == 4)
        def _():
            ready((2, 3), True)

        @pl.when(c == 5)
        def _():
            first.pass_on(2)
            first.pass_on(3)

        @pl.when(c == 6)
        def _():
            outward.pass_on(0)
            outward.pass_on(1)
            ready((4, 5, 6), False)

        return carry

    lax.fori_loop(0, CHUNKS, back, 0)
    r.accqkv[...] = (dot(r.gproj[0:576, :], r.h1[...], NT) * r.share[0:1, 0:1]).astype(BF16)
    qkv = [
        Reduce(
            spot,
            r.accqkv.at[OWN * n : OWN * n + OWN],
            r.arqkv[n],
            r.resqkv.at[OWN * n : OWN * n + OWN],
            r.groups if n < 2 else r.swapped,
            r.qr_sem.at[n],
        )
        for n in range(3)
    ]
    for reduce in qkv:
        reduce.start()
    pieces += qkv
    lax.fori_loop(4, CHUNKS, lambda n, carry: (first_part(r, n, first), carry)[1], 0)
    r.accwo[...] = (dot(r.atto[...], r.gatt[...], NT) * r.share[0:1, 0:1]).astype(BF16)
    out = Reduce(spot, r.accwo, r.arwo, r.reswo, r.groups, r.wr_sem)
    out.start()
    pieces.append(out)

    def last(n, carry):
        @pl.when(n < 3)
        def _():
            first.pass_on(n + 4)

        @pl.when(n >= 2)
        def _():
            outward.pass_on(n)

        first_norm_back(r, spot, n, first)
        slots(IN_LAST, n)
        return carry

    lax.fori_loop(0, CHUNKS, last, 0)

    def lane_sum(ref):
        return jnp.sum(ref[...], axis=1, keepdims=True)

    b_down = jnp.sum(r.gout[own, :].astype(F32), axis=1, keepdims=True)
    b_qkv = jnp.sum(r.gproj[0:576, :].astype(F32), axis=1, keepdims=True)
    turn = (lane_sum(r.sf0), lane_sum(r.sf1))
    turns = [turn[n][32 * h : 32 * h + 32] for h in range(3) for n in range(2)]
    columns = [
        jnp.sum(r.gpre[...].astype(F32), axis=1, keepdims=True),
        jnp.concatenate([lane_sum(r.sbo), lane_sum(r.sg1), lane_sum(r.sb1), lane_sum(r.sg2)], axis=0),
        jnp.concatenate([lane_sum(r.sb2), b_down] + turns + [jnp.zeros((OWN, 1), F32)], axis=0),
    ]
    rest = jnp.zeros((D - OWN, 1), F32)
    columns += [jnp.concatenate([b_qkv[OWN * n : OWN * n + OWN], rest], axis=0) for n in range(3)]
    lane = lax.broadcasted_iota(jnp.int32, (D, 128), 1)
    table = jnp.zeros((D, 128), F32)
    for n, column in enumerate(columns):
        table = jnp.where(lane == n, column, table)
    table = jnp.transpose(table * r.share[0:1, 0:1])[0:8, :]
    vectors = Vectors(r, spot, table)
    vectors.start()
    pieces.append(vectors)
    finished = 0
    for piece, step in tail:
        if piece < 9:
            pieces[piece].advance(step)
        else:
            finish_out(r, outward, finished)
            finished += 1
    r.out[...] = r.gs[:, 0:ROWS]
    for step in range(2 * r.dp_bits):
        for piece, first_step in zip(pieces, taken, strict=True):
            piece.advance(first_step + step)
    r.sums[...] = vectors.table


class Vectors:
    def __init__(self, r, spot, table):
        self.r, self.spot, self.table = r, spot, table

    def copy(self, at):
        r = self.r
        return remote(
            r.sumx.at[at], r.sumr.at[at], r.su_sem.at[0, at], r.su_sem.at[1, at], dp_partner(self.spot, at)
        )

    def start(self, at=0):
        self.r.sumx[at] = self.table
        self.copy(at).start()

    def advance(self, at):
        if at >= self.r.dp_bits:
            return
        self.copy(at).wait()
        self.table = self.table + self.r.sumr[at]
        if at + 1 < self.r.dp_bits:
            self.start(at + 1)


def finish_out(r, outward, c):
    at = lanes(c)
    whole = r.mido[:, at] + (outward.take(c) + r.cols[0:192, 9:10])
    r.gs[:, at] = (r.info[2:3, at] * whole).astype(BF16)


def dma(*shape):
    return pltpu.SemaphoreType.DMA(shape)


def run(dp_bits, **arrays):
    scalars = ("group",)
    on_demand = ("tok", "cot", "in_wqkv", "in_wup", "in_wdn", "in_wout")
    outs = dict(
        out=((OWN, ROWS), BF16),
        igrad=((OWN, LANES), F32),
        resdn=((D, D), BF16),
        resup=((D, D), BF16),
        reswo=((OWN, D), BF16),
        resqkv=((576, D), BF16),
        sums=((8, D), F32),
    )

    groups = [(bit,) for bit in range(dp_bits)]
    swapped = groups[1::-1] + groups[2:]

    def levels(rows):
        steps = plan((rows, D), groups)
        return [VM(((1 << len(bits)) - 1, *shape), BF16) for bits, shape, _ in steps]

    full = VM((D, LANES), BF16)
    own = VM((OWN, LANES), BF16)
    square = VM((D, D), BF16)
    spread = dma(6, CHUNKS)
    scratch = dict(
        x=full,
        h1=full,
        qk=VM((384, LANES), BF16),
        v=own,
        kn=VM((LANES, OWN), BF16),
        vn=VM((LANES, OWN), BF16),
        cos=VM((96, LANES), F32),
        sin=VM((96, LANES), F32),
        kcol=VM((LANES, TILE), F32),
        win=VM((3, OWN, 640), BF16),
        lse=VM((TILES, 8, 384), F32),
        small=VM((D, 128), F32),
        share=VM((8, 128), F32),
        att=full,
        gout=full,
        wqkv=VM((576, D), BF16),
        wup=square,
        wupt=square,
        wdn=square,
        wdnt=square,
        wout=VM((OWN, D), BF16),
        wof=square,
        wot=square,
        h2=full,
        act=full,
        gpre=full,
        work=VM((D, CHUNK), F32),
        mido=VM((OWN, LANES), F32),
        rows1=VM((8, LANES), F32),
        rows2=VM((8, LANES), F32),
        info=VM((8, LANES), F32),
        cols=VM((D, 128), F32),
        cnt=VM((8, 128), F32),
        stats=VM((4, 8, LANES), F32),
        mp=VM((2, 2, OWN, LANES), BF16),
        mr=VM((2, OWN, LANES), BF16),
        ms=own,
        mc=own,
        gp=VM((2, 2, OWN, LANES), BF16),
        gr=VM((2, OWN, LANES), BF16),
        gs=own,
        gc=own,
        dk=VM((LANES, OWN), F32),
        dv=VM((LANES, OWN), F32),
        ardn=[levels(384), levels(384)],
        arup=[levels(384), levels(384)],
        arwo=levels(OWN),
        arqkv=[levels(OWN), levels(OWN), levels(OWN)],
        sg1=VM((OWN, 128), F32),
        sb1=VM((OWN, 128), F32),
        sg2=VM((OWN, 128), F32),
        sb2=VM((OWN, 128), F32),
        sbo=VM((OWN, 128), F32),
        sf0=VM((96, 128), F32),
        sf1=VM((96, 128), F32),
        cnts=VM((dp_bits, 8, 128), F32),
        cntr=VM((dp_bits, 8, 128), F32),
        sumx=VM((dp_bits, 8, D), F32),
        sumr=VM((dp_bits, 8, D), F32),
        load_sem=dma(6),
        tk_sem=spread,
        at_sem=spread,
        ct_sem=spread,
        ga_sem=spread,
        sm_sem=dma(6),
        wo_sem=dma(6),
        cn_sem=dma(2, dp_bits),
        su_sem=dma(2, dp_bits),
        mo_sem=dma(8, CHUNKS),
        g2_sem=dma(8, CHUNKS),
        g1_sem=dma(8, CHUNKS),
        dn_sem=dma(2, 2, 2 * dp_bits, 3),
        up_sem=dma(2, 2, 2 * dp_bits, 3),
        wr_sem=dma(2, 2 * dp_bits, 3),
        qr_sem=dma(3, 2, 2 * dp_bits, 3),
    )
    shapes, structure = jax.tree.flatten(scratch, is_leaf=lambda leaf: not isinstance(leaf, (dict, list)))

    def body(*refs):
        r = Refs()
        for name, ref in zip(list(arrays) + list(outs), refs):
            setattr(r, name, ref)
        named = jax.tree.unflatten(structure, refs[len(arrays) + len(outs) :])
        for name, ref in named.items():
            setattr(r, name, ref)
        r.gatt, r.atto = r.att, r.v
        r.dq, r.gproj = r.act, r.h2
        r.accdn, r.accup, r.accwo = r.wof, r.wupt, r.wdn.at[0:OWN]
        r.wqkvn = r.wot
        r.accqkv = r.wdnt.at[0:576]
        r.dp_bits, r.groups, r.swapped = dp_bits, groups, swapped
        kernel(r, place())

    results = pl.pallas_call(
        body,
        out_shape=[jax.ShapeDtypeStruct(shape, dtype) for shape, dtype in outs.values()],
        in_specs=[
            pl.BlockSpec(
                memory_space=pl.ANY if name in on_demand else pltpu.SMEM if name in scalars else VM
            )
            for name in arrays
        ],
        out_specs=[pl.BlockSpec(memory_space=VM) for _ in outs],
        scratch_shapes=shapes,
        compiler_params=pltpu.CompilerParams(
            collective_id=1, has_side_effects=True, vmem_limit_bytes=64 * MIB - 65536
        ),
    )(*arrays.values())
    named = Refs()
    for name, result in zip(outs, results, strict=True):
        setattr(named, name, result)
    return named


def local(
    tokens,
    w_qkv,
    b_qkv,
    freqs,
    w_out,
    b_out,
    norm1_gain,
    norm1_bias,
    norm2_gain,
    norm2_bias,
    w_up,
    b_up,
    w_down,
    b_down,
    cotangent,
    keep_mask,
    coords,
    block_group,
):
    row_count, width_loc = tokens.shape
    heads_loc = freqs.shape[1]
    a = run(
        lax.axis_size("dp").bit_length() - 1,
        tok=tokens.T,
        cot=cotangent.T,
        b_up=b_up,
        gain1=norm1_gain,
        bias1=norm1_bias,
        gain2=norm2_gain,
        bias2=norm2_bias,
        b_out=b_out,
        b_down=b_down,
        bqkv=b_qkv,
        freqs=freqs.transpose(1, 0, 2),
        keep=keep_mask,
        coords=coords,
        group=block_group,
        in_wqkv=w_qkv.transpose(1, 2, 0).reshape(3 * width_loc, D),
        in_wup=w_up,
        in_wdn=w_down,
        in_wout=w_out,
    )
    sums = a.sums
    grad_qkv = a.resqkv.astype(F32)
    turns = sums[2, 2 * width_loc : 3 * width_loc].reshape(heads_loc, 2, HEAD_DIM // 2)
    return (
        a.out.T,
        a.igrad[:, :row_count].T,
        grad_qkv.reshape(3, width_loc, D).transpose(2, 0, 1),
        sums[3:6, :width_loc],
        turns.transpose(1, 0, 2),
        a.reswo.astype(F32),
        sums[1, 0:192],
        sums[1, 192:384],
        sums[1, 384:576],
        sums[1, 576:768],
        sums[2, 0:192],
        a.resup.astype(F32),
        sums[0],
        a.resdn.astype(F32),
        sums[2, 192:384],
    )


def solution(mesh):
    return jax.shard_map(
        local,
        mesh=mesh,
        in_specs=(
            P("dp", "mp"),
            P(None, None, "mp"),
            P(None, "mp"),
            P(None, "mp", None),
            P("mp", None),
            P("mp"),
            P("mp"),
            P("mp"),
            P("mp"),
            P("mp"),
            P(None, "mp"),
            P("mp"),
            P("mp", None),
            P("mp"),
            P("dp", "mp"),
            P("dp"),
            P(None, "dp"),
            P("dp"),
        ),
        out_specs=(
            P("dp", "mp"),
            P("dp", "mp"),
            P(None, None, "mp"),
            P(None, "mp"),
            P(None, "mp", None),
            P("mp", None),
            P("mp"),
            P("mp"),
            P("mp"),
            P("mp"),
            P("mp"),
            P(None, "mp"),
            P("mp"),
            P("mp", None),
            P("mp"),
        ),
        check_vma=False,
    )
```

```python
import jax
import jax.numpy as jnp
from jax import lax
from jax.experimental import pallas as pl
from jax.experimental.pallas import tpu as pltpu
from jax.sharding import PartitionSpec as P

HEAD_DIM = 64
GRID_LO = 14
SLOTS = 576

MESH = pl.DeviceIdType.MESH
MIB = 1024 * 1024
VM = pltpu.VMEM
F32 = jnp.float32
BF16 = jnp.bfloat16
NT = (((1,), (1,)), ((), ()))
NN = (((1,), (0,)), ((), ()))

D = 768
OWN = 192
ROWS = 1728
LANES = 1792
CHUNK = 256
CHUNKS = LANES // CHUNK
TILE = 128
TILES = LANES // TILE
NARROW = 608

norm_eps = 1e-06
root_half = 0.7071067811865476
inv_root_two_pi = 0.3989422804014327


EARLY = 1
IN_BACKWARD, BEFORE_TILES, AFTER_TILES, IN_LAST, TAIL = range(5)
MOVES = (
    {5: (0, 1,)},
    {0: (0, 1,), 2: (1,), 3: (3, 0, 2,), 5: (2,)},
    {1: (0, 2,), 3: (1,), 4: (3, 0,), 5: (1,), 6: (3,)},
    {0: (0, 2, 1, 3,), 3: (4, 5,), 5: (6, 7, 4,), 6: (2,)},
)
IN_TAIL = (9, 9, 9, 9, 6, 3, 9, 9, 9, 5, 7, 4, 6, 2, 5, 8, 7, 4, 8, 6, 5, 3, 7, 4, 8, 6, 5, 7, 4, 5, 6, 7)


def numbered_moves():
    points = [(IN_BACKWARD, n) for n in range(CHUNKS)]
    for c in range(CHUNKS):
        points += [(BEFORE_TILES, c), (AFTER_TILES, c)]
    points += [(IN_LAST, n) for n in range(CHUNKS)]
    taken = [0] * 9
    moves = {}
    for kind, n in points:
        for piece in MOVES[kind].get(n, ()):
            moves.setdefault((kind, n), []).append((piece, taken[piece]))
            taken[piece] += 1
    tail = []
    for piece in IN_TAIL:
        if piece < 9:
            tail.append((piece, taken[piece]))
            taken[piece] += 1
        else:
            tail.append((piece, 0))
    return moves, tail, taken


class Refs:
    pass


def dot(left, right, dims=NN):
    return lax.dot_general(left, right, dims, preferred_element_type=F32)


def remote(src, dst, send, recv, device):
    return pltpu.make_async_remote_copy(
        src_ref=src, dst_ref=dst, send_sem=send, recv_sem=recv, device_id=device, device_id_type=MESH
    )


def place():
    spot = Refs()
    spot.dp = lax.axis_index("dp")
    spot.mp = lax.axis_index("mp")
    spot.y = spot.mp // 2
    spot.c = spot.mp % 2
    spot.sib_mp = 2 * spot.y + 1 - spot.c
    spot.yp_mp = 2 * (1 - spot.y) + spot.c
    spot.sib = (spot.dp, spot.sib_mp)
    spot.yp = (spot.dp, spot.yp_mp)
    return spot


def greet(devices):
    barrier = pltpu.get_barrier_semaphore()
    for device in devices:
        pl.semaphore_signal(barrier, inc=1, device_id=device, device_id_type=MESH)


def meet(devices):
    pl.semaphore_wait(pltpu.get_barrier_semaphore(), len(devices))


def dp_partner(spot, bit):
    mine = (spot.dp // (1 << bit)) % 2
    return (spot.dp + (1 - 2 * mine) * (1 << bit), spot.mp)


def feat(j):
    return pl.ds(pl.multiple_of(OWN * j, 16), OWN)


def lanes(c):
    return pl.ds(pl.multiple_of(c * CHUNK, CHUNK), CHUNK)


def tile_lanes(t):
    return pl.ds(pl.multiple_of(t * TILE, TILE), TILE)


def flipped(spot, bits, number):
    dp = spot.dp
    for n, bit in enumerate(bits):
        if (number >> n) & 1:
            dp = dp + (1 - 2 * ((spot.dp // (1 << bit)) % 2)) * (1 << bit)
    return (dp, spot.mp)


def cut(shape):
    rows, cols = shape
    if (rows // 2) % 16 == 0:
        return (rows // 2, cols)
    if (cols // 2) % 128 == 0:
        return (rows, cols // 2)
    return shape


def plan(shape, groups):
    steps = []
    for bits in groups:
        after = shape
        for _ in bits:
            after = cut(after)
        whole = cut(cut(shape)) if len(bits) == 2 else cut(shape)
        if len(bits) == 2 and cut(shape) == cut(cut(shape)):
            for bit in bits:
                now = cut(shape)
                steps.append(((bit,), now, now != shape))
                shape = now
            continue
        steps.append((bits, whole, whole != shape))
        shape = after
    return steps


class Reduce:
    def __init__(self, spot, acc, arrive, res, groups, sems):
        self.spot, self.res, self.sems = spot, res, sems
        self.phases = []
        gathers = []
        source, row, col = acc, 0, 0
        steps = plan(acc.shape, groups)
        shape = acc.shape
        for (bits, after, differ), target in zip(steps, arrive, strict=True):
            corners = []
            for number in range(1 << len(bits)):
                at, part = (0, 0), shape
                for n, bit in enumerate(bits):
                    smaller = cut(part)
                    mine = (spot.dp // (1 << bit)) % 2
                    side = 1 - mine if (number >> n) & 1 else mine
                    if smaller[0] < part[0]:
                        at = (at[0] + side * smaller[0], at[1])
                    elif smaller[1] < part[1]:
                        at = (at[0], at[1] + side * smaller[1])
                    part = smaller
                corners.append(at)
            row, col = row + corners[0][0], col + corners[0][1]
            self.phases.append((bits, source, corners, after, target))
            if differ:
                gathers.append((bits, res, (row, col), after, None))
            source, shape = target.at[0], after
        self.own = (row, col)
        self.sums = len(self.phases)
        self.phases += gathers[::-1]

    def piece(self, ref, corner, shape):
        def span(start, size, unit, whole):
            if size == whole:
                return pl.ds(0, size)
            return pl.ds(pl.multiple_of(start, unit), size)

        return ref.at[
            span(corner[0], shape[0], 16, ref.shape[0]), span(corner[1], shape[1], 128, ref.shape[1])
        ]

    def copies(self, at):
        bits, source, corners, shape, target = self.phases[at]
        out = []
        for number in range(1, 1 << len(bits)):
            if target is None:
                piece = self.piece(source, corners, shape)
                goal = piece
            else:
                piece = self.piece(source, corners[number], shape)
                goal = target.at[number - 1]
            sems = (self.sems.at[0, at, number - 1], self.sems.at[1, at, number - 1])
            out.append(remote(piece, goal, *sems, flipped(self.spot, bits, number)))
        return out

    def start(self, at=0):
        for copy in self.copies(at):
            copy.start()

    def add(self, at):
        bits, source, corners, shape, target = self.phases[at]
        held = self.piece(source, corners[0], shape)
        last = at == self.sums - 1
        goal = self.piece(self.res, self.own, shape) if last else target.at[0]
        step = 48 if shape[0] % 48 == 0 else 16

        def block(i, carry):
            rows = pl.ds(pl.multiple_of(i * step, 16), step)
            total = held[rows, :].astype(F32)
            for n in range((1 << len(bits)) - 1):
                total = total + target[n, rows, :].astype(F32)
            goal[rows, :] = total.astype(BF16)
            return carry

        lax.fori_loop(0, shape[0] // step, block, 0)

    def advance(self, at):
        if at >= len(self.phases):
            return
        for copy in self.copies(at):
            copy.wait()
        if at < self.sums:
            self.add(at)
        if at + 1 < len(self.phases):
            self.start(at + 1)


class Exchange:
    def __init__(self, r, spot, part, arrive, out, come, sems, stats=None):
        self.r, self.spot = r, spot
        self.part, self.arrive, self.out, self.come = part, arrive, out, come
        self.sems, self.stats = sems, stats

    def core(self, c):
        at = lanes(c)
        copies = [
            remote(
                self.part.at[:, 1 - self.spot.c, :, at],
                self.arrive.at[:, :, at],
                self.sems.at[0, c],
                self.sems.at[1, c],
                self.spot.sib,
            )
        ]
        if self.stats is not None:
            copies.append(
                remote(
                    self.stats.at[0, :, at],
                    self.stats.at[1, :, at],
                    self.sems.at[2, c],
                    self.sems.at[3, c],
                    self.spot.sib,
                )
            )
        return copies

    def over(self, c):
        at = lanes(c)
        copies = [
            remote(
                self.out.at[:, at],
                self.come.at[:, at],
                self.sems.at[4, c],
                self.sems.at[5, c],
                self.spot.yp,
            )
        ]
        if self.stats is not None:
            copies.append(
                remote(
                    self.stats.at[2, :, at],
                    self.stats.at[3, :, at],
                    self.sems.at[6, c],
                    self.sems.at[7, c],
                    self.spot.yp,
                )
            )
        return copies

    def give(self, c, values):
        at = lanes(c)
        for j in range(4):
            self.part[j // 2, j % 2, :, at] = values[OWN * j : OWN * j + OWN].astype(BF16)
        for copy in self.core(c):
            copy.start()

    def pass_on(self, c):
        at = lanes(c)
        for copy in self.core(c):
            copy.wait()
        away = 1 - self.spot.y
        self.out[:, at] = (
            self.part[away, self.spot.c, :, at].astype(F32) + self.arrive[away, :, at].astype(F32)
        ).astype(BF16)
        if self.stats is not None:
            self.stats[2, :, at] = self.stats[0, :, at] + self.stats[1, :, at]
        for copy in self.over(c):
            copy.start()

    def take(self, c):
        at = lanes(c)
        for copy in self.over(c):
            copy.wait()
        home = self.spot.y
        return (
            self.part[home, self.spot.c, :, at].astype(F32)
            + self.arrive[home, :, at].astype(F32)
            + self.come[:, at].astype(F32)
        )

    def take_stats(self, c):
        at = lanes(c)
        return (self.stats[2, :, at] + self.stats[3, :, at]) * (1.0 / D)


class Spread:
    def __init__(self, spot, full, sems):
        self.spot, self.full, self.sems = spot, full, sems

    def piece(self, j, c, kind, device):
        part = self.full.at[feat(j), lanes(c)]
        return remote(part, part, self.sems.at[2 * kind, c], self.sems.at[2 * kind + 1, c], device)

    def to_y(self, c):
        return self.piece(self.spot.mp, c, 0, self.spot.yp)

    def to_sib(self, c):
        return self.piece(self.spot.mp, c, 1, self.spot.sib)

    def onward(self, c):
        return self.piece(self.spot.yp_mp, c, 2, self.spot.sib)

    def send(self, c):
        self.to_y(c).start()
        self.to_sib(c).start()

    def relay(self, c):
        self.to_y(c).wait()
        self.onward(c).start()

    def arrived(self, c):
        self.to_sib(c).wait()
        self.onward(c).wait()


def sin_cos(angle):
    turns = jnp.floor(angle * 0.6366197723675814 + 0.5)
    rest = angle - turns * 1.5703125
    rest = rest - turns * 4.837512969970703e-4
    rest = rest - turns * 7.549789948768648e-8
    square = rest * rest
    sine = rest + rest * square * (
        -1.6666654611e-1 + square * (8.3321608736e-3 + square * -1.9515295891e-4)
    )
    cosine = (
        1.0
        - 0.5 * square
        + square
        * square
        * (4.166664568298827e-2 + square * (-1.388731625493765e-3 + square * 2.443315711809948e-5))
    )
    quarter = turns - 4.0 * jnp.floor(turns * 0.25)
    odd = (quarter == 1.0) | (quarter == 3.0)
    sine_sign = jnp.where(quarter >= 2.0, -1.0, 1.0)
    cosine_sign = jnp.where((quarter == 1.0) | (quarter == 2.0), -1.0, 1.0)
    return (
        jnp.where(odd, cosine, sine) * sine_sign,
        jnp.where(odd, sine, cosine) * cosine_sign,
    )


def phi_parts(value):
    bell = jnp.exp(-0.5 * value * value)
    inner = 1.0 / (1.0 + (0.3275911 * root_half) * jnp.abs(value))
    series = 0.5 * 1.061405429
    for factor in (-1.453152027, 1.421413741, -0.284496736, 0.254829592):
        series = series * inner + 0.5 * factor
    beyond = series * inner * bell
    return (jnp.where(value >= 0.0, 1.0 - beyond, beyond), inv_root_two_pi * bell)


def normalize(values):
    mean = jnp.mean(values, axis=0, keepdims=True)
    square = jnp.mean(values * values, axis=0, keepdims=True)
    inverse = lax.rsqrt(square - mean * mean + norm_eps)
    return ((values - mean) * inverse, mean, inverse)


def turn_by(values, cosine, sine):
    out = []
    for h in range(3):
        front, rear = values[64 * h : 64 * h + 32], values[64 * h + 32 : 64 * h + 64]
        co, si = cosine[32 * h : 32 * h + 32], sine[32 * h : 32 * h + 32]
        out += [front * co - rear * si, front * si + rear * co]
    return jnp.concatenate(out, axis=0)


def block_diagonal(tile):
    zero = jnp.zeros((64, TILE), tile.dtype)
    parts = []
    for h in range(3):
        column = [zero, zero, zero]
        column[h] = tile[64 * h : 64 * h + 64]
        parts.append(jnp.concatenate(column, axis=0))
    return jnp.concatenate(parts, axis=1)


def from_diagonal(values, heads):
    return jnp.concatenate(
        [values[64 * h : 64 * h + 64, TILE * n : TILE * n + TILE] for n, h in enumerate(heads)], axis=0
    )


def fold(values):
    return values[:, :128] + values[:, 128:]


def row_tables(r):
    pad = jnp.zeros((1, D - 3 * OWN), F32)
    rest = jnp.zeros((1, D - OWN), F32)
    qkv = jnp.concatenate([r.bqkv[n : n + 1, :].astype(F32) for n in range(3)] + [pad], axis=1)
    pad = jnp.zeros((2, D - 96), F32)
    freqs = jnp.concatenate([r.freqs[h] for h in range(3)] + [pad], axis=1)
    table = jnp.concatenate(
        [r.b_up[...].astype(F32).reshape(1, D), qkv, freqs]
        + [
            jnp.concatenate([ref[...].astype(F32).reshape(1, OWN), rest], axis=1)
            for ref in (r.gain1, r.bias1, r.gain2, r.bias2, r.b_out, r.b_down)
        ]
        + [jnp.zeros((118, D), F32)],
        axis=0,
    )
    for i in range(D // 128):
        r.cols[128 * i : 128 * i + 128, :] = jnp.transpose(table[:, 128 * i : 128 * i + 128])
    low = 1.0 - r.group[0].astype(F32)
    keep = r.keep[...].astype(F32).reshape(1, ROWS)
    middle = lax.broadcasted_iota(jnp.int32, (1, ROWS), 1).astype(F32) + 0.5
    segment = low * jnp.floor(middle * (1.0 / (GRID_LO * GRID_LO))) + (1.0 - low) * jnp.floor(
        middle * (1.0 / SLOTS)
    )
    r.info[...] = jnp.zeros_like(r.info)
    r.info[0:2, 0:ROWS] = r.coords[...].astype(F32)
    r.info[2:3, 0:ROWS] = keep
    r.info[3:4, 0:ROWS] = keep * (segment + 1.0) - 1.0
    r.info[4:5, 0:ROWS] = segment
    kept = jnp.sum(keep, axis=1, keepdims=True)
    lane = lax.broadcasted_iota(jnp.int32, (8, 128), 1)
    r.cnt[...] = kept * jnp.where(lane == 0, low, jnp.where(lane == 1, 1.0 - low, 0.0))


def angle_tables(r):
    def block(c, carry):
        at = lanes(c)
        angle = r.cols[0:96, 2:3] * r.info[0:1, at] + r.cols[0:96, 3:4] * r.info[1:2, at]
        sine, cosine = sin_cos(angle)
        r.cos[:, at] = cosine
        r.sin[:, at] = sine
        return carry

    lax.fori_loop(0, CHUNKS, block, 0)

    def column(t, carry):
        row = r.info[3:4, tile_lanes(t)]
        r.kcol[pl.ds(pl.multiple_of(t * TILE, TILE), TILE), :] = jnp.transpose(
            jnp.broadcast_to(row, (TILE, TILE))
        )
        return carry

    lax.fori_loop(0, TILES, column, 0)


def flip(source, goal):
    for i in range(source.shape[1] // 128):
        part = source[:, 128 * i : 128 * i + 128].astype(F32)
        goal[128 * i : 128 * i + 128, 0 : source.shape[0]] = jnp.transpose(part).astype(BF16)


def project(r, c):
    at = lanes(c)
    normed, mean, inverse = normalize(r.x[:, at].astype(F32))
    r.rows1[0:1, at] = mean
    r.rows1[1:2, at] = inverse
    h1 = (normed * r.small[:, 4:5] + r.small[:, 5:6]).astype(BF16)
    r.h1[:, at] = h1
    projected = dot(r.wqkv[...], h1) + r.cols[0:576, 1:2]
    cosine, sine = r.cos[:, at], r.sin[:, at]
    query = turn_by(projected[0:192], cosine, sine)
    key = turn_by(projected[192:384], cosine, sine)
    value = projected[384:576]
    r.qk[0:192, at] = query.astype(BF16)
    r.qk[192:384, at] = key.astype(BF16)
    r.v[:, at] = value.astype(BF16)
    r.kn[at, :] = jnp.transpose(key).astype(BF16)
    r.vn[at, :] = jnp.transpose(value).astype(BF16)


def tile_mask(r, tile, start, width):
    window = pl.ds(pl.multiple_of(start, 16), width)
    allowed = r.kcol[window, :] == r.info[4:5, tile_lanes(tile)]
    return jnp.where(allowed, 0.0, -1e30)


def repeat(mask, values):
    return jnp.concatenate([mask] * (values.shape[1] // TILE), axis=1)


def head_groups(width):
    return [(0, 1, 2)] if width <= NARROW else [(0,), (1,), (2,)]


def attend_tile(r, spot, tile, start, width, values):
    window = pl.ds(pl.multiple_of(start, 16), width)
    at = tile_lanes(tile)
    queries = block_diagonal(r.qk[0:192, at] * BF16(0.125))
    mask = tile_mask(r, tile, start, width)
    for heads in head_groups(width):
        span = slice(TILE * heads[0], TILE * heads[-1] + TILE)
        scores = dot(r.kn[window, :], queries[:, span])
        scores = scores + repeat(mask, scores)
        top = jnp.max(scores, axis=0, keepdims=True)
        exponent = jnp.exp(scores - top)
        total = jnp.sum(exponent, axis=0, keepdims=True)
        probs = (exponent * (1.0 / total)).astype(BF16)
        out = from_diagonal(dot(values, probs), heads).astype(BF16)
        r.att[head_rows(spot, heads), at] = out
        r.lse[tile, :, span] = jnp.broadcast_to(top + jnp.log(total), (8, span.stop - span.start))


def head_rows(spot, heads):
    return pl.ds(pl.multiple_of(OWN * spot.mp + 64 * heads[0], 16), 64 * len(heads))


def key_blocks(width):
    count = -(-width // 384)
    size = -(-width // (16 * count)) * 16
    return [(at, min(size, width - at)) for at in range(0, width, size)]


def back_tile(r, spot, tile, start, width, keys):
    at = tile_lanes(tile)
    queries = block_diagonal(r.qk[0:192, at] * BF16(0.125))
    grad_rows = dot(r.wout[...], r.gatt[:, at]).astype(BF16)
    grads = block_diagonal(grad_rows)
    product = grad_rows.astype(F32) * r.atto[:, at].astype(F32)
    centers = [jnp.sum(product[64 * h : 64 * h + 64], axis=0, keepdims=True) for h in range(3)]
    for heads in head_groups(width):
        span = slice(TILE * heads[0], TILE * heads[-1] + TILE)
        query, grad = queries[:, span], grads[:, span]
        center = jnp.concatenate([centers[h] for h in heads], axis=1)
        log = r.lse[tile, 0:1, span]
        parts = []
        for offset, size in key_blocks(width):
            window = pl.ds(pl.multiple_of(start + offset, 16), size)
            mask = tile_mask(r, tile, start + offset, size)
            scores = dot(r.kn[window, :], query)
            probs = jnp.exp(scores + repeat(mask, scores) - log)
            g_probs = dot(r.vn[window, :], grad)
            g_scores = (probs * (g_probs - center)).astype(BF16)
            r.dv[window, :] += dot(probs.astype(BF16), grad, NT)
            r.dk[window, :] += dot(g_scores, query, NT)
            parts.append(g_scores)
        g_scores = jnp.concatenate(parts, axis=0)
        rows = slice(64 * heads[0], 64 * heads[-1] + 64)
        r.dq[rows, at] = (from_diagonal(dot(keys, g_scores), heads) * 0.125).astype(BF16)


def mlp_forward(r, spot, c, outward):
    at = lanes(c)
    mid = r.x[:, at].astype(F32) + (dot(r.wot[...], r.att[:, at]) + r.small[:, 8:9])
    normed, mean, inverse = normalize(mid)
    r.work[...] = mid
    r.mido[:, at] = r.work[feat(spot.mp), :]
    r.rows2[0:1, at] = mean
    r.rows2[1:2, at] = inverse
    h2 = (normed * r.small[:, 6:7] + r.small[:, 7:8]).astype(BF16)
    r.h2[:, at] = h2
    hidden = dot(r.wupt[...], h2) + r.cols[:, 0:1]
    lower, density = phi_parts(hidden)
    active = (hidden * lower).astype(BF16)
    r.act[:, at] = active
    r.gpre[:, at] = (lower + hidden * density).astype(BF16)
    outward.give(c, dot(r.wdnt[...], active))


def give_gradient(r, c, sums, grad, gain, bias, low):
    at = lanes(c)
    r.stats[0, 0:1, at] = jnp.sum(grad * gain, axis=0, keepdims=True)
    r.stats[0, 1:2, at] = jnp.sum(grad * (low[:, at].astype(F32) - bias), axis=0, keepdims=True)
    sums.give(c, grad)


def mlp_backward(r, c, sums):
    at = lanes(c)
    g_act = dot(r.wdn[...], r.gout[:, at])
    g_pre = (g_act * r.gpre[:, at].astype(F32)).astype(BF16)
    r.gpre[:, at] = g_pre
    give_gradient(r, c, sums, dot(r.wup[...], g_pre), r.small[:, 6:7], r.small[:, 7:8], r.h2)


def second_norm_back(r, spot, c, sums):
    at = lanes(c)
    grad = sums.take(c)
    means = sums.take_stats(c)
    normed = (r.mido[:, at] - r.rows2[0:1, at]) * r.rows2[1:2, at]
    r.sg2[...] += fold(grad * normed)
    r.sb2[...] += fold(grad)
    back = r.rows2[1:2, at] * (
        grad * r.cols[0:192, 6:7] - means[0:1, :] - normed * means[1:2, :]
    )
    g_att = (r.gout[feat(spot.mp), at].astype(F32) + back).astype(BF16)
    r.gatt[feat(spot.mp), at] = g_att
    r.sbo[...] += fold(g_att.astype(F32))


def unrotate(r, c):
    at = lanes(c)
    cosine, sine = r.cos[:, at], r.sin[:, at]
    g_query = r.dq[0:192, at].astype(F32)
    g_key = jnp.transpose(r.dk[at, :]).astype(BF16).astype(F32)
    g_value = jnp.transpose(r.dv[at, :]).astype(BF16)
    plain = [turn_by(g, cosine, -sine).astype(BF16) for g in (g_query, g_key)]
    r.gproj[0:576, at] = jnp.concatenate(plain + [g_value], axis=0)
    angle = []
    for h in range(3):
        total = 0.0
        for part, g in enumerate((g_query, g_key)):
            rotated = r.qk[192 * part : 192 * part + 192, at].astype(F32)
            a, b = slice(64 * h, 64 * h + 32), slice(64 * h + 32, 64 * h + 64)
            total = total + (g[b] * rotated[a] - g[a] * rotated[b])
        angle.append(total)
    angle = jnp.concatenate(angle, axis=0)
    r.sf0[...] += fold(angle * r.info[0:1, at])
    r.sf1[...] += fold(angle * r.info[1:2, at])


def first_part(r, c, sums):
    grad = dot(r.wqkvn[:, 0:576], r.gproj[0:576, lanes(c)])
    give_gradient(r, c, sums, grad, r.small[:, 4:5], r.small[:, 5:6], r.h1)


def first_norm_back(r, spot, c, sums):
    at = lanes(c)
    grad = sums.take(c)
    means = sums.take_stats(c)
    own = feat(spot.mp)
    normed = (r.x[own, at].astype(F32) - r.rows1[0:1, at]) * r.rows1[1:2, at]
    r.sg1[...] += fold(grad * normed)
    r.sb1[...] += fold(grad)
    back = r.rows1[1:2, at] * (
        grad * r.cols[0:192, 4:5] - means[0:1, :] - normed * means[1:2, :]
    )
    r.igrad[:, at] = r.gatt[own, at].astype(F32) + back


def kernel(r, spot):
    peers = [dp_partner(spot, bit) for bit in range(r.dp_bits)]
    both = [flipped(spot, bits, 3) for bits in r.groups if len(bits) == 2]
    greeted = [spot.sib, spot.yp] + peers + both
    greet(greeted)
    token_load = pltpu.make_async_copy(r.tok, r.out, r.load_sem.at[4])
    token_load.start()
    cot_load = pltpu.make_async_copy(r.cot, r.out, r.load_sem.at[5])
    loads = Refs()
    for n, (name, source) in enumerate(
        dict(wqkv=r.in_wqkv, wup=r.in_wup, wdn=r.in_wdn, wout=r.in_wout).items()
    ):
        setattr(loads, name, pltpu.make_async_copy(source, getattr(r, name), r.load_sem.at[n]))
        getattr(loads, name).start()
    own = feat(spot.mp)
    here, there = r.small.at[own], r.small.at[feat(spot.yp_mp)]
    small_y = remote(r.cols.at[0:192], here, r.sm_sem.at[0], r.sm_sem.at[1], spot.yp)
    small_c = remote(r.cols.at[0:192], here, r.sm_sem.at[2], r.sm_sem.at[3], spot.sib)
    small_f = remote(there, there, r.sm_sem.at[4], r.sm_sem.at[5], spot.sib)

    def count_copy(bit):
        return remote(
            r.cnts.at[bit], r.cntr.at[bit], r.cn_sem.at[0, bit], r.cn_sem.at[1, bit], peers[bit]
        )

    def count_step(bit):
        count_copy(bit).wait()
        if bit + 1 < r.dp_bits:
            r.cnts[bit + 1] = r.cnts[bit] + r.cntr[bit]
            count_copy(bit + 1).start()

    tokens = Spread(spot, r.x, r.tk_sem)
    attended = Spread(spot, r.att, r.at_sem)
    cotangents = Spread(spot, r.gout, r.ct_sem)
    r.x[own, ROWS - 64 : LANES] = jnp.zeros((OWN, 128), BF16)
    r.gout[own, ROWS - 64 : LANES] = jnp.zeros((OWN, 128), BF16)
    token_load.wait()
    r.x[own, 0:ROWS] = r.out[...]
    cot_load.start()
    meet(greeted)
    tokens.to_y(0).start()
    row_tables(r)
    r.small[own, :] = r.cols[0:192, :]
    r.cnts[0] = r.cnt[...]
    small_y.start()
    count_copy(0).start()
    for c in range(1, CHUNKS):
        tokens.to_y(c).start()
    small_c.start()
    for c in range(CHUNKS):
        tokens.to_sib(c).start()
    loads.wout.wait()
    wo_here = r.wof.at[own]
    wo_there = r.wof.at[feat(spot.yp_mp)]
    wo_y = remote(r.wout, wo_here, r.wo_sem.at[0], r.wo_sem.at[1], spot.yp)
    wo_c = remote(r.wout, wo_here, r.wo_sem.at[2], r.wo_sem.at[3], spot.sib)
    wo_f = remote(wo_there, wo_there, r.wo_sem.at[4], r.wo_sem.at[5], spot.sib)
    wo_y.start()
    wo_c.start()
    r.wof[own, :] = r.wout[...]
    angle_tables(r)
    small_y.wait()
    small_f.start()
    cot_load.wait()
    r.gout[own, 0:ROWS] = (r.out[...].astype(F32) * r.info[2:3, 0:ROWS]).astype(BF16)
    for c in range(2):
        cotangents.send(c)
    count_step(0)
    loads.wup.wait()
    flip(r.wup, r.wupt)
    count_step(1)
    for ref in (r.sg1, r.sb1, r.sg2, r.sb2, r.sbo, r.sf0, r.sf1, r.dk, r.dv):
        ref[...] = jnp.zeros_like(ref)
    loads.wdn.wait()
    flip(r.wdn, r.wdnt)
    loads.wqkv.wait()
    small_c.wait()
    small_f.wait()
    tokens.relay(0)

    def window(source, j):
        start = 576 * j - 32 * (j // 2)
        r.win[j, :, 0:NARROW] = source[:, start : start + NARROW]

    def both_tiles(c, tile, source):
        def narrow(t):
            j = t // 5
            tile(r, spot, t, 576 * j - 32 * (j // 2), NARROW, r.win[j, :, 0:NARROW])

        @pl.when((c != 2) & (c != 4))
        def _():
            narrow(2 * c)
            narrow(2 * c + 1)

        @pl.when(c == 2)
        def _():
            tile(r, spot, 4, 0, 1152, source[:, 0:1152])
            narrow(5)

        @pl.when(c == 4)
        def _():
            narrow(8)
            tile(r, spot, 9, 976, 752, source[:, 976:1728])

    def attention(n, carry):
        @pl.when(n < CHUNKS)
        def _():
            @pl.when(n + 1 < CHUNKS)
            def _():
                tokens.relay(n + 1)

            tokens.arrived(n)
            project(r, n)

        for j in range(3):

            @pl.when(n == 2 * j + 2)
            def _():
                window(r.v, j)

        @pl.when(n >= 2)
        def _():
            both_tiles(n - 2, attend_tile, r.v)
            attended.send(n - 2)

        @pl.when(n == CHUNKS)
        def _():
            wo_y.wait()
            wo_f.start()

        return carry

    lax.fori_loop(0, CHUNKS + 2, attention, 0)
    for c in range(2, CHUNKS):
        cotangents.send(c)
    for bit in range(2, r.dp_bits):
        count_step(bit)
    last = r.dp_bits - 1
    total = r.cnts[last] + r.cntr[last]
    low, high = total[:, 0:1], total[:, 1:2]
    own_low = 1.0 - r.group[0].astype(F32)
    share = (own_low * low + (1.0 - own_low) * high) / (low + high)
    r.share[...] = jnp.broadcast_to(share, (8, 128))

    r.atto[...] = r.att[own, :]
    attended.relay(0)
    wo_c.wait()
    wo_f.wait()
    flip(r.wof, r.wot)

    outward = Exchange(r, spot, r.mp, r.mr, r.ms, r.mc, r.mo_sem)
    second = Exchange(r, spot, r.gp, r.gr, r.gs, r.gc, r.g2_sem, r.stats)
    g_att = Spread(spot, r.gatt, r.ga_sem)

    def halves(acc, arrive, res, sems, orders):
        rows = acc.shape[0] // 2
        return [
            Reduce(
                spot,
                acc.at[rows * n : rows * n + rows],
                arrive[n],
                res.at[rows * n : rows * n + rows],
                orders[n],
                sems.at[n],
            )
            for n in range(2)
        ]

    down = halves(r.accdn, r.ardn, r.resdn, r.dn_sem, (r.swapped, r.groups))
    up = halves(r.accup, r.arup, r.resup, r.up_sem, (r.groups, r.groups))

    pieces = down + up

    moves, tail, taken = numbered_moves()

    def move(kind, n):
        for piece, step in moves.get((kind, n), ()):
            pieces[piece].advance(step)

    def slots(kind, n):
        for point, at in sorted(moves):
            if point == kind:

                @pl.when(n == at)
                def _():
                    move(kind, at)

    def norm_step(c):
        second_norm_back(r, spot, c, second)
        g_att.send(c)

    def forward(n, carry):
        @pl.when(n + 1 < CHUNKS)
        def _():
            attended.relay(n + 1)

        attended.arrived(n)
        mlp_forward(r, spot, n, outward)
        return carry

    lax.fori_loop(0, CHUNKS, forward, 0)
    cotangents.relay(0)

    def backward(n, carry):
        @pl.when(n < EARLY)
        def _():
            cotangents.relay(n + 1)
            cotangents.arrived(n)

        mlp_backward(r, n, second)

        @pl.when(n >= 1)
        def _():
            second.pass_on(n - 1)

        @pl.when(n >= 4)
        def _():
            norm_step(n - 4)

        return carry

    def late_backward(n, carry):
        backward(n, carry)
        slots(IN_BACKWARD, n)
        return carry

    lax.fori_loop(0, EARLY, backward, 0)
    for c in range(EARLY + 1, CHUNKS):
        cotangents.relay(c)
    for c in range(EARLY, CHUNKS):
        cotangents.arrived(c)
    r.accdn[...] = (dot(r.act[...], r.gout[...], NT) * r.share[0:1, 0:1]).astype(BF16)
    down[0].start()
    down[1].start()
    lax.fori_loop(EARLY, CHUNKS, late_backward, 0)
    second.pass_on(CHUNKS - 1)
    r.accup[...] = (dot(r.h2[...], r.gpre[...], NT) * r.share[0:1, 0:1]).astype(BF16)
    up[0].start()
    up[1].start()
    norm_step(3)
    flip(r.wqkv, r.wqkvn)
    for j in range(3):
        window(r.qk.at[192:384], j)
    first = Exchange(r, spot, r.gp, r.gr, r.gs, r.gc, r.g1_sem, r.stats)
    g_att.relay(0)

    def back(c, carry):
        @pl.when(c + 4 < CHUNKS)
        def _():
            norm_step(c + 4)

        @pl.when(c + 1 < CHUNKS)
        def _():
            g_att.relay(c + 1)

        g_att.arrived(c)

        slots(BEFORE_TILES, c)
        both_tiles(c, back_tile, r.qk.at[192:384])
        slots(AFTER_TILES, c)

        def ready(chunks, give):
            def one(n, carry):
                unrotate(r, n)
                if give:
                    first_part(r, n, first)
                return carry

            lax.fori_loop(chunks[0], chunks[-1] + 1, one, 0)

        @pl.when(c == 2)
        def _():
            ready((0, 1), True)

        @pl.when(c == 3)
        def _():
            first.pass_on(0)
            first.pass_on(1)

        @pl.when(c == 4)
        def _():
            ready((2, 3), True)

        @pl.when(c == 5)
        def _():
            first.pass_on(2)
            first.pass_on(3)

        @pl.when(c == 6)
        def _():
            outward.pass_on(0)
            outward.pass_on(1)
            ready((4, 5, 6), False)

        return carry

    lax.fori_loop(0, CHUNKS, back, 0)
    r.accqkv[...] = (dot(r.gproj[0:576, :], r.h1[...], NT) * r.share[0:1, 0:1]).astype(BF16)
    qkv = [
        Reduce(
            spot,
            r.accqkv.at[OWN * n : OWN * n + OWN],
            r.arqkv[n],
            r.resqkv.at[OWN * n : OWN * n + OWN],
            r.swapped if n != 1 else r.groups,
            r.qr_sem.at[n],
        )
        for n in range(3)
    ]
    for reduce in qkv:
        reduce.start()
    pieces += qkv
    lax.fori_loop(4, CHUNKS, lambda n, carry: (first_part(r, n, first), carry)[1], 0)
    r.accwo[...] = (dot(r.atto[...], r.gatt[...], NT) * r.share[0:1, 0:1]).astype(BF16)
    out = Reduce(spot, r.accwo, r.arwo, r.reswo, r.groups, r.wr_sem)
    out.start()
    pieces.append(out)

    def last(n, carry):
        @pl.when(n < 3)
        def _():
            first.pass_on(n + 4)

        @pl.when(n >= 2)
        def _():
            outward.pass_on(n)

        first_norm_back(r, spot, n, first)
        slots(IN_LAST, n)
        return carry

    lax.fori_loop(0, CHUNKS, last, 0)

    def lane_sum(ref):
        return jnp.sum(ref[...], axis=1, keepdims=True)

    b_down = jnp.sum(r.gout[own, :].astype(F32), axis=1, keepdims=True)
    b_qkv = jnp.sum(r.gproj[0:576, :].astype(F32), axis=1, keepdims=True)
    turn = (lane_sum(r.sf0), lane_sum(r.sf1))
    turns = [turn[n][32 * h : 32 * h + 32] for h in range(3) for n in range(2)]
    columns = [
        jnp.sum(r.gpre[...].astype(F32), axis=1, keepdims=True),
        jnp.concatenate([lane_sum(r.sbo), lane_sum(r.sg1), lane_sum(r.sb1), lane_sum(r.sg2)], axis=0),
        jnp.concatenate([lane_sum(r.sb2), b_down] + turns + [jnp.zeros((OWN, 1), F32)], axis=0),
    ]
    rest = jnp.zeros((D - OWN, 1), F32)
    columns += [jnp.concatenate([b_qkv[OWN * n : OWN * n + OWN], rest], axis=0) for n in range(3)]
    lane = lax.broadcasted_iota(jnp.int32, (D, 128), 1)
    table = jnp.zeros((D, 128), F32)
    for n, column in enumerate(columns):
        table = jnp.where(lane == n, column, table)
    table = jnp.transpose(table * r.share[0:1, 0:1])[0:8, :]
    vectors = Vectors(r, spot, table)
    vectors.start()
    pieces.append(vectors)
    finished = 0
    for piece, step in tail:
        if piece < 9:
            pieces[piece].advance(step)
        else:
            finish_out(r, outward, finished)
            finished += 1
    r.out[...] = r.gs[:, 0:ROWS]
    for step in range(2 * r.dp_bits):
        for piece, first_step in zip(pieces, taken, strict=True):
            piece.advance(first_step + step)
    r.sums[...] = vectors.table


class Vectors:
    def __init__(self, r, spot, table):
        self.r, self.spot, self.table = r, spot, table

    def copy(self, at):
        r = self.r
        return remote(
            r.sumx.at[at], r.sumr.at[at], r.su_sem.at[0, at], r.su_sem.at[1, at], dp_partner(self.spot, at)
        )

    def start(self, at=0):
        self.r.sumx[at] = self.table
        self.copy(at).start()

    def advance(self, at):
        if at >= self.r.dp_bits:
            return
        self.copy(at).wait()
        self.table = self.table + self.r.sumr[at]
        if at + 1 < self.r.dp_bits:
            self.start(at + 1)


def finish_out(r, outward, c):
    at = lanes(c)
    whole = r.mido[:, at] + (outward.take(c) + r.cols[0:192, 9:10])
    r.gs[:, at] = (r.info[2:3, at] * whole).astype(BF16)


def dma(*shape):
    return pltpu.SemaphoreType.DMA(shape)


def run(dp_bits, **arrays):
    scalars = ("group",)
    on_demand = ("tok", "cot", "in_wqkv", "in_wup", "in_wdn", "in_wout")
    outs = dict(
        out=((OWN, ROWS), BF16),
        igrad=((OWN, LANES), F32),
        resdn=((D, D), BF16),
        resup=((D, D), BF16),
        reswo=((OWN, D), BF16),
        resqkv=((576, D), BF16),
        sums=((8, D), F32),
    )

    groups = [(bit,) for bit in range(dp_bits)]
    swapped = groups[1::-1] + groups[2:]

    def levels(rows):
        steps = plan((rows, D), groups)
        return [VM(((1 << len(bits)) - 1, *shape), BF16) for bits, shape, _ in steps]

    full = VM((D, LANES), BF16)
    own = VM((OWN, LANES), BF16)
    square = VM((D, D), BF16)
    spread = dma(6, CHUNKS)
    scratch = dict(
        x=full,
        h1=full,
        qk=VM((384, LANES), BF16),
        v=own,
        kn=VM((LANES, OWN), BF16),
        vn=VM((LANES, OWN), BF16),
        cos=VM((96, LANES), F32),
        sin=VM((96, LANES), F32),
        kcol=VM((LANES, TILE), F32),
        win=VM((3, OWN, 640), BF16),
        lse=VM((TILES, 8, 384), F32),
        small=VM((D, 128), F32),
        share=VM((8, 128), F32),
        att=full,
        gout=full,
        wqkv=VM((576, D), BF16),
        wup=square,
        wupt=square,
        wdn=square,
        wdnt=square,
        wout=VM((OWN, D), BF16),
        wof=square,
        wot=square,
        h2=full,
        act=full,
        gpre=full,
        work=VM((D, CHUNK), F32),
        mido=VM((OWN, LANES), F32),
        rows1=VM((8, LANES), F32),
        rows2=VM((8, LANES), F32),
        info=VM((8, LANES), F32),
        cols=VM((D, 128), F32),
        cnt=VM((8, 128), F32),
        stats=VM((4, 8, LANES), F32),
        mp=VM((2, 2, OWN, LANES), BF16),
        mr=VM((2, OWN, LANES), BF16),
        ms=own,
        mc=own,
        gp=VM((2, 2, OWN, LANES), BF16),
        gr=VM((2, OWN, LANES), BF16),
        gs=own,
        gc=own,
        dk=VM((LANES, OWN), F32),
        dv=VM((LANES, OWN), F32),
        ardn=[levels(384), levels(384)],
        arup=[levels(384), levels(384)],
        arwo=levels(OWN),
        arqkv=[levels(OWN), levels(OWN), levels(OWN)],
        sg1=VM((OWN, 128), F32),
        sb1=VM((OWN, 128), F32),
        sg2=VM((OWN, 128), F32),
        sb2=VM((OWN, 128), F32),
        sbo=VM((OWN, 128), F32),
        sf0=VM((96, 128), F32),
        sf1=VM((96, 128), F32),
        cnts=VM((dp_bits, 8, 128), F32),
        cntr=VM((dp_bits, 8, 128), F32),
        sumx=VM((dp_bits, 8, D), F32),
        sumr=VM((dp_bits, 8, D), F32),
        load_sem=dma(6),
        tk_sem=spread,
        at_sem=spread,
        ct_sem=spread,
        ga_sem=spread,
        sm_sem=dma(6),
        wo_sem=dma(6),
        cn_sem=dma(2, dp_bits),
        su_sem=dma(2, dp_bits),
        mo_sem=dma(8, CHUNKS),
        g2_sem=dma(8, CHUNKS),
        g1_sem=dma(8, CHUNKS),
        dn_sem=dma(2, 2, 2 * dp_bits, 3),
        up_sem=dma(2, 2, 2 * dp_bits, 3),
        wr_sem=dma(2, 2 * dp_bits, 3),
        qr_sem=dma(3, 2, 2 * dp_bits, 3),
    )
    shapes, structure = jax.tree.flatten(scratch, is_leaf=lambda leaf: not isinstance(leaf, (dict, list)))

    def body(*refs):
        r = Refs()
        for name, ref in zip(list(arrays) + list(outs), refs):
            setattr(r, name, ref)
        named = jax.tree.unflatten(structure, refs[len(arrays) + len(outs) :])
        for name, ref in named.items():
            setattr(r, name, ref)
        r.gatt, r.atto = r.att, r.v
        r.dq, r.gproj = r.act, r.h2
        r.accdn, r.accup, r.accwo = r.wof, r.wupt, r.wdn.at[0:OWN]
        r.wqkvn = r.wot
        r.accqkv = r.wdnt.at[0:576]
        r.dp_bits, r.groups, r.swapped = dp_bits, groups, swapped
        kernel(r, place())

    results = pl.pallas_call(
        body,
        out_shape=[jax.ShapeDtypeStruct(shape, dtype) for shape, dtype in outs.values()],
        in_specs=[
            pl.BlockSpec(
                memory_space=pl.ANY if name in on_demand else pltpu.SMEM if name in scalars else VM
            )
            for name in arrays
        ],
        out_specs=[pl.BlockSpec(memory_space=VM) for _ in outs],
        scratch_shapes=shapes,
        compiler_params=pltpu.CompilerParams(
            collective_id=1, has_side_effects=True, vmem_limit_bytes=64 * MIB - 65536
        ),
    )(*arrays.values())
    named = Refs()
    for name, result in zip(outs, results, strict=True):
        setattr(named, name, result)
    return named


def local(
    tokens,
    w_qkv,
    b_qkv,
    freqs,
    w_out,
    b_out,
    norm1_gain,
    norm1_bias,
    norm2_gain,
    norm2_bias,
    w_up,
    b_up,
    w_down,
    b_down,
    cotangent,
    keep_mask,
    coords,
    block_group,
):
    row_count, width_loc = tokens.shape
    heads_loc = freqs.shape[1]
    a = run(
        lax.axis_size("dp").bit_length() - 1,
        tok=tokens.T,
        cot=cotangent.T,
        b_up=b_up,
        gain1=norm1_gain,
        bias1=norm1_bias,
        gain2=norm2_gain,
        bias2=norm2_bias,
        b_out=b_out,
        b_down=b_down,
        bqkv=b_qkv,
        freqs=freqs.transpose(1, 0, 2),
        keep=keep_mask,
        coords=coords,
        group=block_group,
        in_wqkv=w_qkv.transpose(1, 2, 0).reshape(3 * width_loc, D),
        in_wup=w_up,
        in_wdn=w_down,
        in_wout=w_out,
    )
    sums = a.sums
    grad_qkv = a.resqkv.astype(F32)
    turns = sums[2, 2 * width_loc : 3 * width_loc].reshape(heads_loc, 2, HEAD_DIM // 2)
    return (
        a.out.T,
        a.igrad[:, :row_count].T,
        grad_qkv.reshape(3, width_loc, D).transpose(2, 0, 1),
        sums[3:6, :width_loc],
        turns.transpose(1, 0, 2),
        a.reswo.astype(F32),
        sums[1, 0:192],
        sums[1, 192:384],
        sums[1, 384:576],
        sums[1, 576:768],
        sums[2, 0:192],
        a.resup.astype(F32),
        sums[0],
        a.resdn.astype(F32),
        sums[2, 192:384],
    )


def solution(mesh):
    return jax.shard_map(
        local,
        mesh=mesh,
        in_specs=(
            P("dp", "mp"),
            P(None, None, "mp"),
            P(None, "mp"),
            P(None, "mp", None),
            P("mp", None),
            P("mp"),
            P("mp"),
            P("mp"),
            P("mp"),
            P("mp"),
            P(None, "mp"),
            P("mp"),
            P("mp", None),
            P("mp"),
            P("dp", "mp"),
            P("dp"),
            P(None, "dp"),
            P("dp"),
        ),
        out_specs=(
            P("dp", "mp"),
            P("dp", "mp"),
            P(None, None, "mp"),
            P(None, "mp"),
            P(None, "mp", None),
            P("mp", None),
            P("mp"),
            P("mp"),
            P("mp"),
            P("mp"),
            P("mp"),
            P(None, "mp"),
            P("mp"),
            P("mp", None),
            P("mp"),
        ),
        check_vma=False,
    )
```
